128 devices in a mesh: ctx: 32 (over x, z, core), tp: 2 (over y_lo), dp: 2 (over y_hi).
Axes of the slice: x: 4, y: 4 (y_hi: 2, y_lo: 2; y = y_hi * 2 + y_lo), z: 4, core: 2. Of those that a mesh axis runs over, the one named last changes fastest.
Arguments:
- prompt_hidden: bfloat16 [2, 2048, 5120], P('dp', 'ctx'), may hold values from -6 to 6
- key_weight: bfloat16 [5120, 1024], P(None, 'tp'), may hold values from -0.078125 to 0.078125
- value_weight: bfloat16 [5120, 1024], P(None, 'tp'), may hold values from -0.078125 to 0.078125
- key_gain: float32 [128], replicated, may hold values from 0.1 to 1.9
- queries: bfloat16 [2, 3072, 8192], P('dp', 'ctx', 'tp'), may hold values from -100 to 100
- response_kv: bfloat16 [2, 3072, 2, 1024], P('dp', 'ctx', None, 'tp'), may hold values from -6 to 6
- targets: bfloat16 [2, 3072, 8192], P('dp', 'ctx', 'tp'), may hold values from -1.5 to 1.5
- ref_scores: float32 [2, 256], P('dp'), may hold values from -16 to 16
- lengths: int32 [2, 32, 8], P('dp', 'ctx'), may hold values from 1 to 48, 96 in all within a row
- placement_map: int32 [2, 256], P('dp', 'ctx'), may hold values from 0 to 255, each once within a row
Outputs:
- dpo_loss: float32 [2], P('dp')
- query_grad: bfloat16 [2, 3072, 8192], P('dp', 'ctx', 'tp')
- response_kv_grad: bfloat16 [2, 3072, 2, 1024], P('dp', 'ctx', None, 'tp')
- prompt_grad: bfloat16 [2, 2048, 5120], P('dp', 'ctx', 'tp')
- weight_grad: float32 [5120, 2, 1024], P(('ctx', 'dp'), None, 'tp')
The draws below stay inside these ranges and needn't reach their ends.
Inputs may be any that keep to these rules, and one draw needn't show every extreme that they name: The 8 lengths of one device sum to 96. `placement_map`: each group's map names every response once; response p < 128 is the chosen one of pair p, response p + 128 its rejected one.
All inputs are finite; a program needn't handle non-finite values.
Results may differ from the reference program's by a relative error of at most 0.035.
Values may be sent and summed in bfloat16 or wider, within the bound.
A program may use at most 192 MiB of HBM per device.

```python
import math
import jax
import jax.numpy as jnp
import numpy as np
from jax import lax

D = 5120
HEADS = 64
KV_HEADS = 8
HEAD_DIM = 128
R_DEV = 96
SLOTS = 8
PROMPT = 2048
RESP = 3072
RESPONSES = 256
PAIRS = 128
GROUPS = 2
N_CTX = 32


def draw_queries(key, part):
    key = jax.random.fold_in(key, 11)
    return jax.random.truncated_normal(key, -6.0, 6.0, (GROUPS, RESP, HEADS * HEAD_DIM), jnp.float32).astype(jnp.bfloat16)


def draw_response_kv(key, part):
    key = jax.random.fold_in(key, 12)
    return jax.random.truncated_normal(key, -6.0, 6.0, (GROUPS, RESP, 2, KV_HEADS * HEAD_DIM), jnp.float32).astype(jnp.bfloat16)


def block_levels(stream_key, dims, shards, smallest, largest):
    def one(dim, shards_of):
        steps = jax.random.uniform(jax.random.fold_in(jax.random.fold_in(stream_key, 6), dim), (shards_of,), jnp.float32, smallest / len(shards), largest / len(shards))
        return jnp.repeat(jnp.exp(steps), dims[dim] // shards_of).reshape((-1,) + (1,) * (len(dims) - dim - 1))

    loudness = one(*shards[0])
    for cut in shards[1:]:
        loudness = loudness * one(*cut)
    return loudness


def split_up(amount, total, bound, skew):
    weights = [(1 << 20) // math.isqrt(grade ** skew) + 1 for grade in range(2, amount + 1)]
    spare, counts = total - bound - (amount - 1), [1] * (amount - 1)
    while spare > 0:
        free = [i for i in range(amount - 1) if counts[i] < bound]
        whole, budget = sum([weights[i] for i in free]), spare
        for i in free:
            extra = min(bound - counts[i], max(1, budget * weights[i] // whole), spare)
            counts[i] = counts[i] + extra
            spare = spare - extra
    return np.array([bound] + counts)


def ragged_sizes(rng, number_of, total, limit, slope):
    if number_of == 2:
        one = jax.random.randint(rng, (), max(1, total - limit), min(limit, total - 1) + 1)
        return jnp.stack([one, total - one])
    sizes = jnp.asarray(split_up(number_of, total, limit, slope), jnp.int32)
    twos = (number_of - 1) // 2
    source_of, taker = sizes[1:1 + 2 * twos:2], sizes[2:2 + 2 * twos:2]
    slack = jnp.minimum(source_of - 1, limit - taker)
    moved = jax.random.randint(jax.random.fold_in(rng, 1), (twos,), 0, 1 << 20) % (slack + 1)
    sizes = sizes.at[1:1 + 2 * twos:2].set(source_of - moved).at[2:2 + 2 * twos:2].set(taker + moved)
    return sizes[jax.random.permutation(jax.random.fold_in(rng, 2), number_of)]


def centred(stream_key, extent, scale, most, shards=(), kind=jnp.bfloat16):
    entries = jax.random.normal(stream_key, extent, jnp.float32) * scale
    if len(shards) > 0:
        entries = block_levels(stream_key, extent, shards, -0.22, 0.18) * entries
    return jnp.clip(entries, min=-most, max=most).astype(kind)


def setup_inputs(seed: int = 0) -> dict:
    keys = jax.random.split(jax.random.key(seed), 11)
    return {
        "prompt_hidden": centred(keys[0], (GROUPS, PROMPT, D), 1.0, 6.0, ((0, 2), (1, 32))),
        "key_weight": centred(keys[1], (D, KV_HEADS * HEAD_DIM), D ** -0.5, 0.078125, ((1, 2),)),
        "value_weight": centred(keys[2], (D, KV_HEADS * HEAD_DIM), D ** -0.5, 0.078125, ((1, 2),)),
        "key_gain": jnp.clip(1.0 + 0.18 * jax.random.normal(keys[3], (HEAD_DIM,), jnp.float32), 0.1, 1.9),
        "queries": draw_queries(jax.random.fold_in(keys[10], 71), 0),
        "response_kv": draw_response_kv(jax.random.fold_in(keys[10], 71), 0),
        "targets": centred(keys[6], (GROUPS, RESP, HEADS * HEAD_DIM), 0.25, 1.5, ((0, 2), (1, 32), (2, 2))),
        "ref_scores": centred(keys[7], (GROUPS, RESPONSES), 3.0, 16.0, ((0, 2),), jnp.float32),
        "lengths": jax.vmap(lambda own: ragged_sizes(own, SLOTS, R_DEV, R_DEV // 2, 2))(jax.random.split(keys[8], GROUPS * N_CTX)).reshape((GROUPS, N_CTX, SLOTS)).astype(jnp.int32),
        "placement_map": jax.vmap(lambda own: jax.random.permutation(own, RESPONSES))(jax.random.split(keys[9], GROUPS)).reshape((GROUPS, RESPONSES)).astype(jnp.int32),
    }


NORM_EPS = 1e-06
DPO_BETA = 0.5
MASK_FILL = -1e+30

def rounded(value):
    return lax.optimization_barrier(value.astype(jnp.bfloat16)).astype(jnp.float32)

def slot_layout(lengths_here):
    ends = jnp.cumsum(lengths_here, dtype=jnp.int32)
    row_ids = jnp.arange(R_DEV, dtype=jnp.int32)
    slot_ids = lax.optimization_barrier(jnp.sum((row_ids[:, None] >= ends[None, :]).astype(jnp.int32), axis=1, dtype=jnp.int32))
    same_slot = (slot_ids[:, None] == slot_ids[None, :]) & (row_ids[None, :] <= row_ids[:, None])
    keep_mask = jnp.concatenate([jnp.ones((R_DEV, PROMPT), dtype=bool), same_slot], axis=1)
    slot_onehot = (slot_ids[:, None] == jnp.arange(SLOTS, dtype=jnp.int32)[None, :]).astype(jnp.float32)
    return (keep_mask, slot_onehot)

def reference(prompt_hidden, key_weight, value_weight, key_gain, queries, response_kv, targets, ref_scores, lengths, placement_map):
    qk_scale = 1.0 / math.sqrt(HEAD_DIM)
    grouped = HEADS // KV_HEADS
    norm_gain = key_gain.astype(jnp.float32)
    losses = []
    query_grads = []
    resp_grads = []
    hidden_grads = []
    weight_total = jnp.zeros((D, 2, KV_HEADS * HEAD_DIM), jnp.float32)
    for group in range(GROUPS):
        hidden = prompt_hidden[group]
        raw_keys = jnp.dot(hidden, key_weight, preferred_element_type=jnp.float32).reshape(PROMPT, KV_HEADS, HEAD_DIM)
        inv_rms = lax.rsqrt(lax.optimization_barrier(jnp.mean(raw_keys * raw_keys, axis=-1, keepdims=True)) + NORM_EPS)
        prompt_keys = (raw_keys * inv_rms * norm_gain).astype(jnp.bfloat16)
        prompt_values = jnp.dot(hidden, value_weight, preferred_element_type=jnp.float32).astype(jnp.bfloat16).reshape(PROMPT, KV_HEADS, HEAD_DIM)
        query_dev = queries[group].reshape(N_CTX, R_DEV, KV_HEADS, grouped, HEAD_DIM)
        resp_dev = response_kv[group].reshape(N_CTX, R_DEV, 2, KV_HEADS, HEAD_DIM)
        target_dev = targets[group].reshape(N_CTX, R_DEV, HEADS * HEAD_DIM)
        map_dev = placement_map[group].reshape(N_CTX, SLOTS)
        length_dev = lengths[group]

        def device_logits(device):
            keep_mask, slot_onehot = slot_layout(length_dev[device])
            keys_all = jnp.concatenate([prompt_keys, resp_dev[device][:, 0]], axis=0).astype(jnp.float32)
            values_all = jnp.concatenate([prompt_values, resp_dev[device][:, 1]], axis=0).astype(jnp.float32)
            query_here = query_dev[device].astype(jnp.float32)
            logits = jnp.einsum('rkgd,jkd->kgrj', query_here, keys_all) * qk_scale
            logits = jnp.where(keep_mask[None, None], logits, MASK_FILL)
            return (logits, keys_all, values_all, query_here, slot_onehot)

        def forward_one(device):
            logits, keys_all, values_all, query_here, slot_onehot = device_logits(device)
            peak = lax.optimization_barrier(jnp.max(logits, axis=-1, keepdims=True))
            log_total = peak + jnp.log(lax.optimization_barrier(jnp.sum(jnp.exp(logits - peak), axis=-1, keepdims=True)))
            weights = rounded(jnp.exp(logits - log_total))
            attended = jnp.einsum('kgrj,jkd->rkgd', weights, values_all).astype(jnp.bfloat16)
            attended_f = lax.optimization_barrier(attended).astype(jnp.float32)
            token_score = lax.optimization_barrier(jnp.sum(attended_f.reshape(R_DEV, HEADS * HEAD_DIM) * target_dev[device].astype(jnp.float32), axis=1))
            slot_score = lax.optimization_barrier(jnp.sum(token_score[:, None] * slot_onehot, axis=0))
            return (attended, log_total[..., 0], slot_score)
        attended_all, lse_all, slot_all = lax.map(forward_one, jnp.arange(N_CTX, dtype=jnp.int32))
        response_scores = jnp.zeros((RESPONSES,), jnp.float32).at[map_dev.reshape(-1)].add(slot_all.reshape(-1))
        shifted = response_scores - ref_scores[group]
        margin = DPO_BETA * (shifted[:PAIRS] - shifted[PAIRS:])
        losses.append(jnp.sum(jax.nn.softplus(-margin)))
        pair_grad = -DPO_BETA * jax.nn.sigmoid(-margin)
        score_grad = jnp.concatenate([pair_grad, -pair_grad])
        slot_grad_all = score_grad[map_dev]

        def backward_one(prompt_sum, device):
            logits, keys_all, values_all, query_here, slot_onehot = device_logits(device)
            row_grad = lax.optimization_barrier(jnp.sum(slot_onehot * slot_grad_all[device][None, :], axis=1))
            out_grad = rounded(row_grad[:, None] * target_dev[device].astype(jnp.float32)).reshape(R_DEV, KV_HEADS, grouped, HEAD_DIM)
            attended_f = attended_all[device].astype(jnp.float32)
            row_dot = jnp.einsum('rkgd,rkgd->kgr', attended_f, out_grad)
            probs = jnp.exp(logits - lse_all[device][..., None])
            prob_grad = jnp.einsum('rkgd,jkd->kgrj', out_grad, values_all)
            logit_grad = rounded(probs * (prob_grad - row_dot[..., None]))
            probs_b = rounded(probs)
            query_grad = (jnp.einsum('kgrj,jkd->rkgd', logit_grad, keys_all) * qk_scale).astype(jnp.bfloat16)
            key_term = jnp.einsum('kgrj,rkgd->jkd', logit_grad, query_here) * qk_scale
            value_term = jnp.einsum('kgrj,rkgd->jkd', probs_b, out_grad)
            prompt_term = jnp.stack([key_term[:PROMPT], value_term[:PROMPT]], axis=1)
            prompt_sum = prompt_sum + rounded(prompt_term)
            resp_grad = jnp.stack([key_term[PROMPT:], value_term[PROMPT:]], axis=1).astype(jnp.bfloat16)
            return (prompt_sum, (query_grad.reshape(R_DEV, HEADS * HEAD_DIM), resp_grad.reshape(R_DEV, 2, KV_HEADS * HEAD_DIM)))
        start_sum = jnp.zeros((PROMPT, 2, KV_HEADS, HEAD_DIM), jnp.float32)
        prompt_sum, per_device = lax.scan(backward_one, start_sum, jnp.arange(N_CTX, dtype=jnp.int32))
        query_grads.append(per_device[0].reshape(RESP, HEADS * HEAD_DIM))
        resp_grads.append(per_device[1].reshape(RESP, 2, KV_HEADS * HEAD_DIM))
        gain_grad = norm_gain * prompt_sum[:, 0]
        raw_grad = inv_rms * gain_grad - raw_keys * inv_rms * inv_rms * inv_rms * lax.optimization_barrier(jnp.mean(raw_keys * gain_grad, axis=-1, keepdims=True))
        raw_b = raw_grad.astype(jnp.bfloat16).reshape(PROMPT, KV_HEADS * HEAD_DIM)
        value_b = prompt_sum[:, 1].astype(jnp.bfloat16).reshape(PROMPT, KV_HEADS * HEAD_DIM)
        hidden_part = jnp.dot(raw_b, key_weight.T, preferred_element_type=jnp.float32) + jnp.dot(value_b, value_weight.T, preferred_element_type=jnp.float32)
        hidden_grads.append(hidden_part.astype(jnp.bfloat16))
        weight_total = weight_total + jnp.stack([jnp.dot(hidden.T, raw_b, preferred_element_type=jnp.float32), jnp.dot(hidden.T, value_b, preferred_element_type=jnp.float32)], axis=1)
    return (jnp.stack(losses), jnp.stack(query_grads), jnp.stack(resp_grads), jnp.stack(hidden_grads), weight_total)
```

```python
import functools
import math

import jax
import jax.numpy as jnp
from jax import lax
from jax.experimental import pallas as pl
from jax.experimental.pallas import tpu as pltpu
from jax.sharding import PartitionSpec as P

NORM_EPS = 1e-06
DPO_BETA = 0.5
MASK_FILL = -1e30
LOG2E = 1.4426950408889634
NT = (((1,), (1,)), ((), ()))
TN = (((0,), (0,)), ((), ()))
F32 = jnp.float32
BF16 = jnp.bfloat16


def attend_kernel(
    scale,
    q_ref,
    t_ref,
    k_ref,
    v_ref,
    rk_ref,
    rv_ref,
    bias_ref,
    e_ref,
    g_ref,
    er_ref,
    gr_ref,
    inv_ref,
    dq_ref,
    tok_ref,
):
    heads = q_ref.shape[1] // 128
    rows = q_ref.shape[0]
    q = jnp.concatenate([q_ref[:, i * 128 : (i + 1) * 128] for i in range(heads)], axis=0)
    t = jnp.concatenate([t_ref[:, i * 128 : (i + 1) * 128] for i in range(heads)], axis=0)
    bias = jnp.concatenate([bias_ref[...]] * heads, axis=0)
    k, v, rk, rv = k_ref[...], v_ref[...], rk_ref[...], rv_ref[...]
    s = lax.dot_general(q, k, NT, preferred_element_type=F32)
    sr = lax.dot_general(q, rk, NT, preferred_element_type=F32) + bias
    peak = jnp.maximum(
        jnp.max(s, axis=1, keepdims=True), jnp.max(sr, axis=1, keepdims=True)
    )
    factor = scale * LOG2E
    top = peak * factor
    e = jnp.exp2(s * factor - top)
    er = jnp.exp2(sr * factor - top)
    inv = 1.0 / (jnp.sum(e, axis=1, keepdims=True) + jnp.sum(er, axis=1, keepdims=True))
    eb, erb = e.astype(BF16), er.astype(BF16)
    e_ref[0] = eb
    er_ref[0] = erb
    attended = (
        jnp.dot(eb, v, preferred_element_type=F32) + jnp.dot(erb, rv, preferred_element_type=F32)
    ) * inv
    dot = jnp.sum(attended * t.astype(F32), axis=1, keepdims=True)
    dp = lax.dot_general(t, v, NT, preferred_element_type=F32)
    dpr = lax.dot_general(t, rv, NT, preferred_element_type=F32)
    gb = (e_ref[0].astype(F32) * (dp - dot)).astype(BF16)
    grb = (er_ref[0].astype(F32) * (dpr - dot)).astype(BF16)
    g_ref[0] = gb
    gr_ref[0] = grb
    dq = (
        jnp.dot(gb, k, preferred_element_type=F32) + jnp.dot(grb, rk, preferred_element_type=F32)
    ) * (inv * scale)
    inv_ref[0] = inv
    for i in range(heads):
        dq_ref[:, i * 128 : (i + 1) * 128] = dq[i * rows : (i + 1) * rows].astype(BF16)

    @pl.when((pl.program_id(0) == 0) & (pl.program_id(1) == 0))
    def _():
        tok_ref[...] = jnp.zeros_like(tok_ref)

    total = dot[:rows]
    for i in range(1, heads):
        total = total + dot[i * rows : (i + 1) * rows]
    tok_ref[...] += total


def attend(q, t, prompt_keys, prompt_values, rk, rv, bias, scale, grouped, chunk):
    rows = q.shape[0]
    tokens, kv_width = prompt_keys.shape
    kv_heads = kv_width // 128
    pad = rk.shape[0]
    steps = grouped // chunk
    m = chunk * rows
    total = grouped * rows
    row_block = pl.BlockSpec((rows, chunk * 128), lambda h, c: (0, h * steps + c))
    head_block = pl.BlockSpec((tokens, 128), lambda h, c: (0, h))
    resp_block = pl.BlockSpec((pad, 128), lambda h, c: (0, h))

    def score_block(width):
        return pl.BlockSpec((1, m, width), lambda h, c: (h, c, 0))

    return pl.pallas_call(
        functools.partial(attend_kernel, scale),
        grid=(kv_heads, steps),
        in_specs=[
            row_block,
            row_block,
            head_block,
            head_block,
            resp_block,
            resp_block,
            pl.BlockSpec((rows, pad), lambda h, c: (0, 0)),
        ],
        out_specs=[
            score_block(tokens),
            score_block(tokens),
            score_block(pad),
            score_block(pad),
            score_block(1),
            row_block,
            pl.BlockSpec((rows, 1), lambda h, c: (0, 0)),
        ],
        out_shape=[
            jax.ShapeDtypeStruct((kv_heads, total, tokens), BF16),
            jax.ShapeDtypeStruct((kv_heads, total, tokens), BF16),
            jax.ShapeDtypeStruct((kv_heads, total, pad), BF16),
            jax.ShapeDtypeStruct((kv_heads, total, pad), BF16),
            jax.ShapeDtypeStruct((kv_heads, total, 1), F32),
            jax.ShapeDtypeStruct(q.shape, BF16),
            jax.ShapeDtypeStruct((rows, 1), F32),
        ],
        compiler_params=pltpu.CompilerParams(vmem_limit_bytes=50 * 1024 * 1024),
        name="attend",
    )(q, t, prompt_keys, prompt_values, rk, rv, bias)


def keygrad_kernel(
    scale,
    e_ref,
    g_ref,
    er_ref,
    gr_ref,
    q_ref,
    t_ref,
    inv_ref,
    row_ref,
    dq_in_ref,
    dkv_ref,
    drkv_ref,
    dq_ref,
):
    heads = q_ref.shape[1] // 128
    rows = q_ref.shape[0]
    row_grad = row_ref[...]
    factor = inv_ref[0] * jnp.concatenate([row_grad] * heads, axis=0)
    q = jnp.concatenate([q_ref[:, i * 128 : (i + 1) * 128] for i in range(heads)], axis=0)
    t = jnp.concatenate([t_ref[:, i * 128 : (i + 1) * 128] for i in range(heads)], axis=0)
    qs = (q.astype(F32) * (factor * scale)).astype(BF16)
    ts = (t.astype(F32) * factor).astype(BF16)
    dkv_ref[0] = lax.dot_general(g_ref[0], qs, TN, preferred_element_type=F32).astype(BF16)
    dkv_ref[1] = lax.dot_general(e_ref[0], ts, TN, preferred_element_type=F32).astype(BF16)
    drkv_ref[0] = lax.dot_general(gr_ref[0], qs, TN, preferred_element_type=F32).astype(BF16)
    drkv_ref[1] = lax.dot_general(er_ref[0], ts, TN, preferred_element_type=F32).astype(BF16)
    dq_ref[...] = (dq_in_ref[...].astype(F32) * row_grad).astype(BF16)


def keygrad(e, g, er, gr, q, t, inv, row_grad, dq, scale):
    kv_heads, total, tokens = e.shape
    pad = er.shape[2]
    rows = q.shape[0]
    width = q.shape[1] // kv_heads

    def score_block(w):
        return pl.BlockSpec((1, total, w), lambda h: (h, 0, 0))

    row_block = pl.BlockSpec((rows, width), lambda h: (0, h))
    return pl.pallas_call(
        functools.partial(keygrad_kernel, scale),
        grid=(kv_heads,),
        in_specs=[
            score_block(tokens),
            score_block(tokens),
            score_block(pad),
            score_block(pad),
            row_block,
            row_block,
            score_block(1),
            pl.BlockSpec((rows, 1), lambda h: (0, 0)),
            row_block,
        ],
        out_specs=[
            pl.BlockSpec((2, tokens, 128), lambda h: (0, 0, h)),
            pl.BlockSpec((2, pad, 128), lambda h: (0, 0, h)),
            row_block,
        ],
        out_shape=[
            jax.ShapeDtypeStruct((2, tokens, kv_heads * 128), BF16),
            jax.ShapeDtypeStruct((2, pad, kv_heads * 128), BF16),
            jax.ShapeDtypeStruct(q.shape, BF16),
        ],
        compiler_params=pltpu.CompilerParams(vmem_limit_bytes=50 * 1024 * 1024),
        name="keygrad",
    )(e, g, er, gr, q, t, inv, row_grad, dq)


def shards(
    prompt_hidden,
    key_weight,
    value_weight,
    key_gain,
    queries,
    response_kv,
    targets,
    ref_scores,
    lengths,
    placement_map,
):
    hidden = prompt_hidden[0]
    prompt_rows, model_width = hidden.shape
    head_width = key_gain.shape[0]
    kv_width = key_weight.shape[1]
    kv_heads = kv_width // head_width
    resp_rows = queries.shape[1]
    query_heads = queries.shape[2] // head_width
    grouped = query_heads // kv_heads
    slot_count = lengths.shape[2]
    responses = ref_scores.shape[1]
    pair_count = responses // 2
    n_ctx = lax.axis_size("ctx")
    qk_scale = 1.0 / math.sqrt(head_width)

    hidden_columns = lax.all_to_all(
        hidden.reshape(prompt_rows, n_ctx, model_width // n_ctx).transpose(1, 0, 2),
        "ctx",
        split_axis=0,
        concat_axis=0,
        tiled=True,
    ).reshape(n_ctx * prompt_rows, model_width // n_ctx)

    raw_keys = jnp.dot(hidden, key_weight, preferred_element_type=F32).reshape(
        prompt_rows, kv_heads, head_width
    )
    inv_rms = lax.rsqrt(jnp.mean(raw_keys * raw_keys, axis=-1, keepdims=True) + NORM_EPS)
    prompt_keys = (raw_keys * inv_rms * key_gain).astype(BF16).reshape(prompt_rows, kv_width)
    prompt_values = jnp.dot(hidden, value_weight, preferred_element_type=F32).astype(BF16)
    gathered = lax.all_gather(
        jnp.stack([prompt_keys, prompt_values], axis=0), "ctx", axis=1, tiled=True
    )

    ends = jnp.cumsum(lengths[0, 0], dtype=jnp.int32)
    row_ids = lax.iota(jnp.int32, resp_rows)
    slot_ids = jnp.sum(
        (row_ids[:, None] >= ends[None, :]).astype(jnp.int32), axis=1, dtype=jnp.int32
    )
    same_slot = (slot_ids[:, None] == slot_ids[None, :]) & (row_ids[None, :] <= row_ids[:, None])
    slot_onehot = (slot_ids[:, None] == lax.iota(jnp.int32, slot_count)[None, :]).astype(F32)
    place_onehot = (placement_map[0][:, None] == lax.iota(jnp.int32, responses)[None, :]).astype(
        F32
    )
    pad = -resp_rows % 128
    bias = jnp.pad(
        jnp.where(same_slot, 0.0, MASK_FILL).astype(F32),
        ((0, 0), (0, pad)),
        constant_values=MASK_FILL,
    )
    resp = jnp.pad(response_kv[0], ((0, pad), (0, 0), (0, 0)))
    q, t = queries[0], targets[0]
    e, g, er, gr, inv, dq, token_part = attend(
        q, t, gathered[0], gathered[1], resp[:, 0], resp[:, 1], bias, qk_scale, grouped, 2
    )

    slot_part = jnp.sum(token_part * slot_onehot, axis=0)
    scores = lax.psum(
        jnp.sum(slot_part[:, None] * place_onehot, axis=0), ("ctx", "tp")
    )
    shifted = scores - ref_scores[0]
    margin = DPO_BETA * (shifted[:pair_count] - shifted[pair_count:])
    dpo_loss = jnp.sum(jax.nn.softplus(-margin))
    pair_grad = -DPO_BETA * jax.nn.sigmoid(-margin)
    score_grad = jnp.concatenate([pair_grad, -pair_grad])
    slot_grad = jnp.sum(place_onehot * score_grad[None, :], axis=1)
    row_grad = jnp.sum(slot_onehot * slot_grad[None, :], axis=1)

    dkv, drkv, query_grad = keygrad(e, g, er, gr, q, t, inv, row_grad[:, None], dq, qk_scale)
    response_kv_grad = jnp.stack([drkv[0, :resp_rows], drkv[1, :resp_rows]], axis=1)

    owned_grad = lax.psum_scatter(dkv, "ctx", scatter_dimension=1, tiled=True).astype(F32)
    gain_grad = key_gain * owned_grad[0].reshape(prompt_rows, kv_heads, head_width)
    raw_grad = inv_rms * gain_grad - raw_keys * inv_rms * inv_rms * inv_rms * jnp.mean(
        raw_keys * gain_grad, axis=-1, keepdims=True
    )
    kv_grad_b = jnp.stack([raw_grad.reshape(prompt_rows, kv_width), owned_grad[1]], axis=0).astype(
        BF16
    )
    gathered_grad = lax.all_gather(kv_grad_b, "ctx", axis=1, tiled=True)
    hidden_part = lax.dot_general(kv_grad_b[0], key_weight, NT, preferred_element_type=F32)
    hidden_part = hidden_part + lax.dot_general(
        kv_grad_b[1], value_weight, NT, preferred_element_type=F32
    )
    prompt_grad = lax.psum_scatter(
        hidden_part.astype(BF16), "tp", scatter_dimension=1, tiled=True
    )
    weight_part = jnp.stack(
        [
            lax.dot_general(hidden_columns, gathered_grad[0], TN, preferred_element_type=F32),
            lax.dot_general(hidden_columns, gathered_grad[1], TN, preferred_element_type=F32),
        ],
        axis=1,
    )
    weight_grad = lax.psum_scatter(weight_part, "dp", scatter_dimension=0, tiled=True)
    return (
        dpo_loss[None],
        query_grad[None],
        response_kv_grad[None],
        prompt_grad[None],
        weight_grad,
    )


def solution(mesh):
    in_specs = (
        P("dp", "ctx", None),
        P(None, "tp"),
        P(None, "tp"),
        P(),
        P("dp", "ctx", "tp"),
        P("dp", "ctx", None, "tp"),
        P("dp", "ctx", "tp"),
        P("dp", None),
        P("dp", "ctx", None),
        P("dp", "ctx"),
    )
    out_specs = (
        P("dp"),
        P("dp", "ctx", "tp"),
        P("dp", "ctx", None, "tp"),
        P("dp", "ctx", "tp"),
        P(("ctx", "dp"), None, "tp"),
    )
    return jax.shard_map(shards, mesh=mesh, in_specs=in_specs, out_specs=out_specs, check_vma=False)
```

```python
import functools
import math

import jax
import jax.numpy as jnp
from jax import lax
from jax.experimental import pallas as pl
from jax.experimental.pallas import tpu as pltpu
from jax.sharding import PartitionSpec as P

NORM_EPS = 1e-06
DPO_BETA = 0.5
MASK_FILL = -1e30
LOG2E = 1.4426950408889634
NT = (((1,), (1,)), ((), ()))
TN = (((0,), (0,)), ((), ()))
F32 = jnp.float32
BF16 = jnp.bfloat16


MESH = pl.DeviceIdType.MESH
SIDE = 4


def params(limit_mib, **more):
    return pltpu.CompilerParams(vmem_limit_bytes=limit_mib * 1024 * 1024, **more)


def place():
    me = lax.axis_index("ctx")
    return me // (2 * SIDE), (me // 2) % SIDE, me % 2


def ctx_id(x, z, core):
    return {"ctx": (x * SIDE + z) * 2 + core}


def greet(peers):
    barrier = pltpu.get_barrier_semaphore()
    for peer in peers:
        pl.semaphore_signal(barrier, inc=1, device_id=peer, device_id_type=MESH)
    pl.semaphore_wait(barrier, len(peers))


def plane_peers():
    x, z, core = place()
    return [
        ctx_id((x + 1) % SIDE, z, core),
        ctx_id((x + SIDE - 1) % SIDE, z, core),
        ctx_id(x, (z + 1) % SIDE, core),
        ctx_id(x, (z + SIDE - 1) % SIDE, core),
        ctx_id(x, z, 1 - core),
    ]


def ring(axis):
    x, z, core = place()
    if axis == 0:
        return x, lambda p: ctx_id(p, z, core)
    return z, lambda p: ctx_id(x, p, core)


def around(p):
    return (p + 1) % SIDE, (p + SIDE - 1) % SIDE, (p + 2) % SIDE


class Copies:
    def __init__(self, send_sem, recv_sem):
        self.send_sem, self.recv_sem, self.started = send_sem, recv_sem, []

    def make(self, src, dst, peer, slot):
        return pltpu.make_async_remote_copy(
            src_ref=src,
            dst_ref=dst,
            send_sem=self.send_sem.at[slot],
            recv_sem=self.recv_sem.at[slot],
            device_id=peer,
            device_id_type=MESH,
        )

    def send(self, src, dst, peer, slot):
        one = self.make(src, dst, peer, slot)
        one.start()
        self.started.append(one)

    def arrived(self, dst, slot):
        x, z, core = place()
        self.make(dst, dst, ctx_id(x, z, 1 - core), slot).wait_recv()

    def finish(self):
        for one in self.started:
            one.wait_send()


GATHER_COPIES = 72


def gather_stages(refs, copies):
    x, z, core = place()
    partner = ctx_id(x, z, 1 - core)
    rows = refs[0].shape[3]
    full, low, high = pl.ds(0, rows), pl.ds(0, rows // 2), pl.ds(rows // 2, rows // 2)
    rings = {}
    for kv in range(2):
        for level in range(2):
            p, at = ring(kv if level == 0 else 1 - kv)
            right, left, opposite = around(p)
            rings[kv, level] = ((p, left, right, opposite), at(right), at(left))

    def block(kv, i, j, part=full, of_core=None):
        of_core = core if of_core is None else of_core
        i, j = rings[kv, 0][0][i], rings[kv, 1][0][j]
        spot = (i, j) if kv == 0 else (j, i)
        return refs[kv].at[spot[0], spot[1], of_core, part]

    def first(kv, k):
        return kv * 36 + k

    def second(kv, i, k):
        return kv * 36 + 4 + i * 4 + k

    def swap_slot(kv, i, j):
        return kv * 36 + 20 + i * 4 + j

    def send(ref, peer, slot):
        copies.send(ref, ref, peer, slot)

    def to_core(kv, i, j):
        send(block(kv, i, j), partner, swap_slot(kv, i, j))

    def onward(kv, i):
        _, right, left = rings[kv, 1]
        send(block(kv, i, 0), right, second(kv, i, 0))
        send(block(kv, i, 0), left, second(kv, i, 1))
        to_core(kv, i, 0)

    def open_all():
        for kv in range(2):
            _, right, left = rings[kv, 0]
            send(block(kv, 0, 0), right, first(kv, 0))
            send(block(kv, 0, 0), left, first(kv, 1))
        for kv in range(2):
            onward(kv, 0)

    def first_neighbours():
        for kv in range(2):
            _, right, left = rings[kv, 0]
            copies.arrived(block(kv, 1, 0), first(kv, 0))
            send(block(kv, 1, 0, low), right, first(kv, 2))
            onward(kv, 1)
            copies.arrived(block(kv, 2, 0), first(kv, 1))
            send(block(kv, 2, 0, high), left, first(kv, 3))
            onward(kv, 2)

    def first_opposite():
        for kv in range(2):
            copies.arrived(block(kv, 3, 0, low), first(kv, 2))
            copies.arrived(block(kv, 3, 0, high), first(kv, 3))
            onward(kv, 3)

    def second_neighbours(i):
        for kv in range(2):
            _, right, left = rings[kv, 1]
            copies.arrived(block(kv, i, 1), second(kv, i, 0))
            send(block(kv, i, 1, low), right, second(kv, i, 2))
            to_core(kv, i, 1)
            copies.arrived(block(kv, i, 2), second(kv, i, 1))
            send(block(kv, i, 2, high), left, second(kv, i, 3))
            to_core(kv, i, 2)

    def second_opposite(i):
        for kv in range(2):
            copies.arrived(block(kv, i, 3, low), second(kv, i, 2))
            copies.arrived(block(kv, i, 3, high), second(kv, i, 3))
            to_core(kv, i, 3)

    def from_core(kv):
        for i in range(4):
            for j in range(4):
                copies.arrived(block(kv, i, j, full, 1 - core), swap_slot(kv, i, j))

    return [
        open_all,
        first_neighbours,
        lambda: second_neighbours(0),
        first_opposite,
        lambda: second_neighbours(1),
        lambda: second_opposite(0),
        lambda: second_neighbours(2),
        lambda: second_opposite(1),
        lambda: second_neighbours(3),
        lambda: second_opposite(2),
        lambda: second_opposite(3),
        lambda: from_core(0),
        lambda: from_core(1),
    ]


def project_kernel(
    h_ref,
    kw_ref,
    vw_ref,
    gain_ref,
    raw_ref,
    gk_ref,
    gv_ref,
    w_ref,
    load_sem,
    send_sem,
    recv_sem,
):
    x, z, core = place()
    steps, tile, width = w_ref.shape[1:]

    def load(kv, i):
        src = (kw_ref, vw_ref)[kv].at[pl.ds(i * tile, tile)]
        return pltpu.make_async_copy(src, w_ref.at[kv, i], load_sem.at[kv, i])

    for i in range(steps):
        for kv in range(2):
            load(kv, i).start()
    greet(plane_peers())
    sums = [jnp.zeros((h_ref.shape[0], width), F32)] * 2
    for i in range(steps):
        part = h_ref[:, i * tile : (i + 1) * tile]
        for kv in range(2):
            load(kv, i).wait()
            sums[kv] = sums[kv] + jnp.dot(part, w_ref[kv, i], preferred_element_type=F32)
    raw_ref[...] = sums[0]
    gv_ref[x, z, core] = sums[1].astype(BF16)
    parts = []
    for i in range(width // 128):
        keys = sums[0][:, i * 128 : (i + 1) * 128]
        inv = lax.rsqrt(jnp.mean(keys * keys, axis=1, keepdims=True) + NORM_EPS)
        parts.append((keys * inv * gain_ref[...]).astype(BF16))
    gk_ref[x, z, core] = jnp.concatenate(parts, axis=1)
    copies = Copies(send_sem, recv_sem)
    for stage in gather_stages((gk_ref, gv_ref), copies):
        stage()
    copies.finish()


def project_and_gather(hidden, key_weight, value_weight, gain):
    rows, depth = hidden.shape
    width = key_weight.shape[1]
    tile = 1024
    steps = depth // tile
    vmem, anywhere = pl.BlockSpec(memory_space=pltpu.VMEM), pl.BlockSpec(memory_space=pl.ANY)
    plane = jax.ShapeDtypeStruct((SIDE, SIDE, 2, rows, width), BF16)
    raw, keys, values = pl.pallas_call(
        project_kernel,
        out_shape=[jax.ShapeDtypeStruct((rows, width), F32), plane, plane],
        in_specs=[vmem, anywhere, anywhere, vmem],
        out_specs=[vmem] * 3,
        scratch_shapes=[
            pltpu.VMEM((2, steps, tile, width), BF16),
            pltpu.SemaphoreType.DMA((2, steps)),
            pltpu.SemaphoreType.DMA((GATHER_COPIES,)),
            pltpu.SemaphoreType.DMA((GATHER_COPIES,)),
        ],
        compiler_params=params(60, collective_id=0, has_side_effects=True),
        name="project_and_gather",
    )(hidden, key_weight, value_weight, gain)
    total = SIDE * SIDE * 2 * rows
    return raw, keys.reshape(total, width), values.reshape(total, width)


def attend_kernel(
    scale,
    q_ref,
    t_ref,
    k_ref,
    v_ref,
    rk_ref,
    rv_ref,
    bias_ref,
    h_ref,
    e_ref,
    g_ref,
    inv_ref,
    dq_ref,
    tok_ref,
    o_ref,
    own_sem,
    send_sem,
    recv_sem,
):
    me = lax.axis_index("ctx")
    n = o_ref.shape[0]

    def window(peer):
        tile = 5 * (peer // 4) + peer % 4
        return h_ref.at[:, pl.ds(pl.multiple_of(tile * 128, 128), WINDOW)]

    def copy(k):
        peer = (me + k) % n
        return pltpu.make_async_remote_copy(
            src_ref=window(peer),
            dst_ref=o_ref.at[me],
            send_sem=send_sem.at[k - 1],
            recv_sem=recv_sem.at[k - 1],
            device_id={"ctx": peer},
            device_id_type=MESH,
        )

    own_copy = pltpu.make_async_copy(window(me), o_ref.at[me], own_sem)

    @pl.when((pl.program_id(0) == 0) & (pl.program_id(1) == 0))
    def _():
        barrier = pltpu.get_barrier_semaphore()

        def hello(k, carry):
            pl.semaphore_signal(
                barrier, inc=1, device_id={"ctx": (me + k) % n}, device_id_type=MESH
            )
            return carry

        def go(k, carry):
            copy(k).start()
            return carry

        lax.fori_loop(1, n, hello, 0)
        pl.semaphore_wait(barrier, n - 1)
        lax.fori_loop(1, n, go, 0)
        own_copy.start()

    heads = q_ref.shape[1] // 128
    rows = q_ref.shape[0]
    q = jnp.concatenate([q_ref[:, i * 128 : (i + 1) * 128] for i in range(heads)], axis=0)
    t = jnp.concatenate([t_ref[:, i * 128 : (i + 1) * 128] for i in range(heads)], axis=0)
    bias = jnp.concatenate([bias_ref[...]] * heads, axis=0)
    k, v, rk, rv = k_ref[...], v_ref[...], rk_ref[...], rv_ref[...]
    s = lax.dot_general(q, k, NT, preferred_element_type=F32)
    sr = lax.dot_general(q, rk, NT, preferred_element_type=F32) + bias
    peak = jnp.maximum(
        jnp.max(s, axis=1, keepdims=True), jnp.max(sr, axis=1, keepdims=True)
    )
    factor = scale * LOG2E
    top = peak * factor
    e = jnp.exp2(s * factor - top)
    er = jnp.exp2(sr * factor - top)
    inv = 1.0 / (jnp.sum(e, axis=1, keepdims=True) + jnp.sum(er, axis=1, keepdims=True))
    eb, erb = e.astype(BF16), er.astype(BF16)
    tokens = k.shape[0]
    e_ref[0, :, :tokens] = eb
    e_ref[0, :, tokens:] = erb
    attended = (
        jnp.dot(eb, v, preferred_element_type=F32) + jnp.dot(erb, rv, preferred_element_type=F32)
    ) * inv
    dot = jnp.sum(attended * t.astype(F32), axis=1, keepdims=True)
    dp = lax.dot_general(t, v, NT, preferred_element_type=F32)
    dpr = lax.dot_general(t, rv, NT, preferred_element_type=F32)
    gb = (eb.astype(F32) * (dp - dot)).astype(BF16)
    grb = (erb.astype(F32) * (dpr - dot)).astype(BF16)
    g_ref[0, :, :tokens] = gb
    g_ref[0, :, tokens:] = grb
    dq = (
        jnp.dot(gb, k, preferred_element_type=F32) + jnp.dot(grb, rk, preferred_element_type=F32)
    ) * (inv * scale)
    inv_ref[0] = inv
    for i in range(heads):
        dq_ref[:, i * 128 : (i + 1) * 128] = dq[i * rows : (i + 1) * rows].astype(BF16)

    @pl.when((pl.program_id(0) == 0) & (pl.program_id(1) == 0))
    def _():
        tok_ref[...] = jnp.zeros_like(tok_ref)

    total = dot[:rows]
    for i in range(1, heads):
        total = total + dot[i * rows : (i + 1) * rows]
    tok_ref[...] += total

    @pl.when(
        (pl.program_id(0) == pl.num_programs(0) - 1) & (pl.program_id(1) == pl.num_programs(1) - 1)
    )
    def _():
        def done(k, carry):
            copy(k).wait()
            return carry

        own_copy.wait()
        lax.fori_loop(1, n, done, 0)


WINDOW = 256


def attend(q, t, prompt_keys, prompt_values, rk, rv, bias, hidden, n, scale, grouped, chunk):
    rows = q.shape[0]
    tokens, kv_width = prompt_keys.shape
    kv_heads = kv_width // 128
    pad = rk.shape[0]
    steps = grouped // chunk
    m = chunk * rows
    total = grouped * rows
    row_block = pl.BlockSpec((rows, chunk * 128), lambda h, c: (0, h * steps + c))
    head_block = pl.BlockSpec((tokens, 128), lambda h, c: (0, h))
    resp_block = pl.BlockSpec((pad, 128), lambda h, c: (0, h))

    def score_block(width):
        return pl.BlockSpec((1, m, width), lambda h, c: (h, c, 0))

    return pl.pallas_call(
        functools.partial(attend_kernel, scale),
        grid=(kv_heads, steps),
        in_specs=[
            row_block,
            row_block,
            head_block,
            head_block,
            resp_block,
            resp_block,
            pl.BlockSpec((rows, pad), lambda h, c: (0, 0)),
            pl.BlockSpec(memory_space=pl.ANY),
        ],
        out_specs=[
            score_block(tokens + pad),
            score_block(tokens + pad),
            score_block(1),
            row_block,
            pl.BlockSpec((rows, 1), lambda h, c: (0, 0)),
            pl.BlockSpec(memory_space=pl.ANY),
        ],
        out_shape=[
            jax.ShapeDtypeStruct((kv_heads, total, tokens + pad), BF16),
            jax.ShapeDtypeStruct((kv_heads, total, tokens + pad), BF16),
            jax.ShapeDtypeStruct((kv_heads, total, 1), F32),
            jax.ShapeDtypeStruct(q.shape, BF16),
            jax.ShapeDtypeStruct((rows, 1), F32),
            jax.ShapeDtypeStruct((n, hidden.shape[0], WINDOW), BF16),
        ],
        scratch_shapes=[
            pltpu.SemaphoreType.DMA,
            pltpu.SemaphoreType.DMA((n - 1,)),
            pltpu.SemaphoreType.DMA((n - 1,)),
        ],
        compiler_params=params(56, collective_id=3, has_side_effects=True),
        name="attend",
    )(q, t, prompt_keys, prompt_values, rk, rv, bias, hidden)


def norm_backward(raw, gain, grad):
    parts = []
    for h in range(raw.shape[1] // 128):
        keys = raw[:, h * 128 : (h + 1) * 128]
        kg = gain * grad[:, h * 128 : (h + 1) * 128]
        inv = lax.rsqrt(jnp.mean(keys * keys, axis=1, keepdims=True) + NORM_EPS)
        mix = jnp.mean(keys * kg, axis=1, keepdims=True)
        parts.append(inv * kg - keys * (inv * inv * inv) * mix)
    return jnp.concatenate(parts, axis=1)


def total_of(*refs):
    value = refs[0][...].astype(F32)
    for ref in refs[1:]:
        value = value + ref[...].astype(F32)
    return value


REDUCE_COPIES = 68


class Reduce:
    def __init__(self, d_ref, c_ref, a_ref, b_ref, r_ref, s_ref, copies):
        self.d, self.c, self.a, self.b, self.r, self.s = d_ref, c_ref, a_ref, b_ref, r_ref, s_ref
        self.copies = copies
        x, z, self.core = place()
        self.partner = ctx_id(x, z, 1 - self.core)
        rows = a_ref.shape[3]
        self.low, self.high = pl.ds(0, rows // 2), pl.ds(rows // 2, rows // 2)
        self.rings = {}
        for kv in range(2):
            for inner in range(2):
                p, at = ring(1 - kv if inner else kv)
                right, left, opposite = around(p)
                self.rings[kv, inner] = ((opposite, right, left, p), at(right), at(left))

    def place_of(self, kv, i):
        return self.rings[kv, 0][0][i]

    def to_core(self, kv, i):
        self.copies.send(
            self.d.at[kv, i, :, 1 - self.core], self.c.at[kv, i], self.partner, kv * 4 + i
        )

    def landing(self, kv, i, k):
        return self.s.at[kv, k] if i is None else self.b.at[kv, i, k]

    def slot(self, kv, i, k):
        return 56 + kv * 6 + k if i is None else 8 + (kv * 4 + i) * 6 + k

    def unit(self, kv, i, j, part):
        if i is None:
            return self.r.at[kv, j, part]
        return self.a.at[kv, i, self.rings[kv, 1][0][j], part]

    def message(self, kv, i, k, ref):
        _, right, left = self.rings[kv, 0 if i is None else 1]
        peer = right if k in (0, 2, 4) else left
        self.copies.send(ref, self.landing(kv, i, k), peer, self.slot(kv, i, k))

    def landed(self, kv, i, k):
        ref = self.landing(kv, i, k)
        self.copies.arrived(ref, self.slot(kv, i, k))
        return ref

    def opening(self, kv, i, j):
        if j == 0:
            self.message(kv, i, 0, self.unit(kv, i, 0, self.low))
            self.message(kv, i, 1, self.unit(kv, i, 0, self.high))
        if j == 1:
            self.message(kv, i, 2, self.unit(kv, i, 1, self.high))
        if j == 2:
            self.message(kv, i, 3, self.unit(kv, i, 2, self.low))

    def passing(self, kv, i):
        for k, j, part in ((0, 1, self.low), (1, 2, self.high)):
            came = self.landed(kv, i, k)
            mine = self.unit(kv, i, j, part)
            mine[...] = total_of(mine, came).astype(BF16)
            self.message(kv, i, 4 + k, mine)

    def result(self, kv, i):
        lows = total_of(
            self.unit(kv, i, 3, self.low), self.landed(kv, i, 3), self.landed(kv, i, 4)
        )
        highs = total_of(
            self.unit(kv, i, 3, self.high), self.landed(kv, i, 2), self.landed(kv, i, 5)
        )
        return jnp.concatenate([lows, highs], axis=0)

    def start_inner(self, kv, i):
        self.copies.arrived(self.c.at[kv, i], kv * 4 + i)
        self.a[kv, i] = total_of(self.d.at[kv, i, :, self.core], self.c.at[kv, i]).astype(BF16)
        for j in range(3):
            self.opening(kv, i, j)

    def end_inner(self, kv, i):
        self.r[kv, i] = self.result(kv, i).astype(BF16)
        self.opening(kv, None, i)


def share_scores(buf, me, peer, copies, base):
    sent = []
    for k in range(1, 8):
        copies.send(buf.at[me], buf.at[me], peer(k), base + k - 1)
    for k in range(1, 8):
        copies.arrived(buf.at[(me - k + 8) % 8], base + k - 1)
    value = buf[0]
    for i in range(1, 8):
        value = value + buf[i]
    return value


def backward_kernel(
    scale,
    token_ref,
    pick_ref,
    ref_ref,
    q_ref,
    t_ref,
    inv_ref,
    raw_ref,
    gain_ref,
    e_ref,
    g_ref,
    kw_ref,
    vw_ref,
    hw_ref,
    loss_ref,
    row_ref,
    resp_ref,
    pgrad_ref,
    wgrad_ref,
    one_ref,
    two_ref,
    qs_ref,
    ts_ref,
    gbuf_ref,
    ebuf_ref,
    rbuf_ref,
    d_ref,
    c_ref,
    a_ref,
    b_ref,
    r_ref,
    s_ref,
    gk_ref,
    gv_ref,
    w_ref,
    h_ref,
    paway_ref,
    pcame_ref,
    pown_ref,
    wpart_ref,
    waway_ref,
    wcame_ref,
    load_sem,
    score_send,
    score_recv,
    reduce_send,
    reduce_recv,
    gather_send,
    gather_recv,
    last_send,
    last_recv,
):
    x, z, core = place()
    ctx, tp, dp = lax.axis_index("ctx"), lax.axis_index("tp"), lax.axis_index("dp")
    kv_heads, total, _ = qs_ref.shape
    rows = q_ref.shape[0]
    grouped = total // rows
    tokens = e_ref.shape[2] - rbuf_ref.shape[3]
    chunk = gbuf_ref.shape[3]
    unit = chunk // SIDE

    reduce_copies = Copies(reduce_send, reduce_recv)
    reduce = Reduce(d_ref, c_ref, a_ref, b_ref, r_ref, s_ref, reduce_copies)

    def loads(i):
        buf = i % 2
        start = pl.multiple_of(reduce.place_of(0, i) * chunk, chunk)
        parts = [
            pltpu.make_async_copy(
                g_ref.at[:, :, pl.ds(start, chunk)], gbuf_ref.at[buf], load_sem.at[buf, 0]
            )
        ]
        for j in range(SIDE):
            start = pl.multiple_of(j * chunk + reduce.place_of(1, i) * unit, unit)
            parts.append(
                pltpu.make_async_copy(
                    e_ref.at[:, :, pl.ds(start, unit)],
                    ebuf_ref.at[buf, :, :, pl.ds(j * unit, unit)],
                    load_sem.at[buf, 1 + j],
                )
            )
        return parts

    def start(parts):
        for one in parts:
            one.start()

    def wait(parts):
        for one in parts:
            one.wait()

    tail = pl.ds(tokens, rbuf_ref.shape[3])
    more = [
        pltpu.make_async_copy(g_ref.at[:, :, tail], rbuf_ref.at[0], load_sem.at[2, 0]),
        pltpu.make_async_copy(e_ref.at[:, :, tail], rbuf_ref.at[1], load_sem.at[2, 1]),
    ]
    late = [
        pltpu.make_async_copy(kw_ref, w_ref.at[0], load_sem.at[2, 2]),
        pltpu.make_async_copy(vw_ref, w_ref.at[1], load_sem.at[2, 3]),
        pltpu.make_async_copy(hw_ref, h_ref, load_sem.at[2, 4]),
    ]
    for i in range(2):
        start(loads(i))

    def first(k):
        q = (x * 2 + tp + k) % 8
        return {"ctx": ((q // 2) * SIDE + z) * 2 + core, "tp": q % 2}

    def second(k):
        q = (z * 2 + core + k) % 8
        return {"ctx": x * SIDE * 2 + q}

    other_dp = {"dp": 1 - dp}
    greet([first(k) for k in range(1, 8)] + [second(k) for k in range(1, 8)] + [other_dp])
    score_copies = Copies(score_send, score_recv)
    pick = pick_ref[...]
    part = jnp.sum(pick * token_ref[...], axis=0, keepdims=True)
    one_ref[x * 2 + tp] = jnp.broadcast_to(part, one_ref.shape[1:])
    half_sum = share_scores(one_ref, x * 2 + tp, first, score_copies, 0)
    two_ref[z * 2 + core] = half_sum
    scores = share_scores(two_ref, z * 2 + core, second, score_copies, 7)[:1]
    pairs = scores.shape[1] // 2
    shifted = scores - ref_ref[...]
    margin = DPO_BETA * (shifted[:, :pairs] - shifted[:, pairs:])
    small = jnp.exp(-jnp.abs(margin))
    pair_grad = -DPO_BETA * jnp.where(margin >= 0.0, small, 1.0) / (1.0 + small)
    score_grad = jnp.concatenate([pair_grad, -pair_grad], axis=1)
    row_grad = jnp.sum(pick * score_grad, axis=1, keepdims=True)
    row_ref[...] = row_grad
    row_factor = jnp.concatenate([row_grad] * grouped, axis=0)
    start(more)
    for h in range(kv_heads):
        factor = inv_ref[h] * row_factor
        base = h * grouped * 128
        pieces = [q_ref[:, base + i * 128 : base + (i + 1) * 128] for i in range(grouped)]
        q = jnp.concatenate(pieces, axis=0).astype(F32)
        qs_ref[h] = (q * (factor * scale)).astype(BF16)
        pieces = [t_ref[:, base + i * 128 : base + (i + 1) * 128] for i in range(grouped)]
        t = jnp.concatenate(pieces, axis=0).astype(F32)
        ts_ref[h] = (t * factor).astype(BF16)

    def chunk_grads(i):
        buf = i % 2
        for kv, (kept, scaled) in enumerate(((gbuf_ref, qs_ref), (ebuf_ref, ts_ref))):
            for h in range(kv_heads):
                grads = lax.dot_general(kept[buf, h], scaled[h], TN, preferred_element_type=F32)
                grads = grads.astype(BF16).reshape(SIDE, 2, unit // 2, 128)
                d_ref[kv, i, :, :, :, h * 128 : (h + 1) * 128] = grads
            reduce.to_core(kv, i)

    for i in range(SIDE):
        wait(loads(i))
        chunk_grads(i)
        if i + 2 < SIDE:
            start(loads(i + 2))
        if i == SIDE - 2:
            start(late)
        if i >= 1:
            for kv in range(2):
                reduce.start_inner(kv, i - 1)
        if i >= 2:
            for kv in range(2):
                reduce.passing(kv, i - 2)
        if i >= 3:
            for kv in range(2):
                reduce.end_inner(kv, i - 3)
    for kv in range(2):
        reduce.start_inner(kv, 3)
    for kv in range(2):
        reduce.passing(kv, 2)
    for kv in range(2):
        reduce.end_inner(kv, 1)
    for kv in range(2):
        reduce.passing(kv, 3)
    wait(more)
    for kv, scaled in enumerate((qs_ref, ts_ref)):
        for h in range(kv_heads):
            grads = lax.dot_general(rbuf_ref[kv, h], scaled[h], TN, preferred_element_type=F32)
            resp_ref[kv, :, h * 128 : (h + 1) * 128] = grads[:rows].astype(BF16)
    loss = jnp.maximum(-margin, 0.0) + jnp.log1p(small)
    loss_ref[...] = jnp.sum(loss, axis=1, keepdims=True)
    for kv in range(2):
        reduce.end_inner(kv, 2)
    for kv in range(2):
        reduce.passing(kv, None)
    for kv in range(2):
        reduce.end_inner(kv, 3)
    key_sum = reduce.result(0, None)
    gk_ref[x, z, core] = norm_backward(raw_ref[...], gain_ref[...], key_sum).astype(BF16)
    gv_ref[x, z, core] = reduce.result(1, None).astype(BF16)

    gather_copies = Copies(gather_send, gather_recv)
    stages = gather_stages((gk_ref, gv_ref), gather_copies)
    last_copies = Copies(last_send, last_recv)
    stages[0]()
    wait(late)
    tile = 512
    half = paway_ref.shape[1]

    def input_grad(side, store):
        key_grad, value_grad = gk_ref[x, z, core], gv_ref[x, z, core]

        def step(i, carry):
            here = pl.ds(pl.multiple_of(side * half + i * tile, tile), tile)
            value = lax.dot_general(key_grad, w_ref[0, here], NT, preferred_element_type=F32)
            value += lax.dot_general(value_grad, w_ref[1, here], NT, preferred_element_type=F32)
            store(pl.ds(pl.multiple_of(i * tile, tile), tile), value)
            return carry

        lax.fori_loop(0, half // tile, step, 0)

    def store_away(here, value):
        paway_ref[:, here] = value.astype(BF16)

    def store_own(here, value):
        pown_ref[:, here] = value

    input_grad(1 - tp, store_away)
    last_copies.send(paway_ref, pcame_ref, {"tp": 1 - tp}, 0)
    for stage in stages[1:5]:
        stage()
    input_grad(tp, store_own)
    for stage in stages[5:-2]:
        stage()
    last_copies.arrived(pcame_ref, 0)
    pgrad_ref[...] = (pown_ref[...] + pcame_ref[...].astype(F32)).astype(BF16)

    out_rows = wgrad_ref.shape[1]
    shift = (ctx % 4) * 32
    hidden = h_ref[...].reshape(-1, h_ref.shape[2])
    for kv, ref in enumerate((gk_ref, gv_ref)):
        stages[-2 + kv]()
        grads = ref[...].reshape(-1, ref.shape[4])
        wpart_ref[kv] = lax.dot_general(hidden, grads, TN, preferred_element_type=F32)
        away = pl.ds(pl.multiple_of(shift + (1 - dp) * out_rows, 16), out_rows)
        waway_ref[kv] = wpart_ref[kv, away].astype(BF16)
        last_copies.send(waway_ref.at[kv], wcame_ref.at[kv], other_dp, 1 + kv)
    for copies in (score_copies, reduce_copies, gather_copies):
        copies.finish()
    own = pl.ds(pl.multiple_of(shift + dp * out_rows, 16), out_rows)
    for kv in range(2):
        last_copies.arrived(wcame_ref.at[kv], 1 + kv)
        wgrad_ref[kv] = wpart_ref[kv, own] + wcame_ref[kv].astype(F32)
    last_copies.finish()


def backward(
    token_part, pick, ref_scores, q, t, inv, raw_keys, gain, e, g, kw, vw, windows, scale, out_rows
):
    rows, responses = pick.shape
    kv_heads, total, width = e.shape
    prompt_rows, kv_width = raw_keys.shape
    depth = kw.shape[0]
    n = windows.shape[0]
    tokens = n * prompt_rows
    pad = width - tokens
    chunk = tokens // SIDE
    half = depth // 2
    vmem, anywhere = pl.BlockSpec(memory_space=pltpu.VMEM), pl.BlockSpec(memory_space=pl.ANY)
    dma = pltpu.SemaphoreType.DMA
    small = (prompt_rows // 2, kv_width)
    return pl.pallas_call(
        functools.partial(backward_kernel, scale),
        out_shape=[
            jax.ShapeDtypeStruct((1, 1), F32),
            jax.ShapeDtypeStruct((rows, 1), F32),
            jax.ShapeDtypeStruct((2, rows, kv_width), BF16),
            jax.ShapeDtypeStruct((prompt_rows, half), BF16),
            jax.ShapeDtypeStruct((2, out_rows, kv_width), F32),
        ],
        in_specs=[vmem] * 8 + [anywhere] * 5,
        out_specs=[vmem] * 5,
        scratch_shapes=[
            pltpu.VMEM((8, 8, responses), F32),
            pltpu.VMEM((8, 8, responses), F32),
            pltpu.VMEM((kv_heads, total, 128), BF16),
            pltpu.VMEM((kv_heads, total, 128), BF16),
            pltpu.VMEM((2, kv_heads, total, chunk), BF16),
            pltpu.VMEM((2, kv_heads, total, chunk), BF16),
            pltpu.VMEM((2, kv_heads, total, pad), BF16),
            pltpu.VMEM((2, SIDE, SIDE, 2, prompt_rows, kv_width), BF16),
            pltpu.VMEM((2, SIDE, SIDE, prompt_rows, kv_width), BF16),
            pltpu.VMEM((2, SIDE, SIDE, prompt_rows, kv_width), BF16),
            pltpu.VMEM((2, SIDE, 6) + small, BF16),
            pltpu.VMEM((2, SIDE, prompt_rows, kv_width), BF16),
            pltpu.VMEM((2, 6) + small, BF16),
            pltpu.VMEM((SIDE, SIDE, 2, prompt_rows, kv_width), BF16),
            pltpu.VMEM((SIDE, SIDE, 2, prompt_rows, kv_width), BF16),
            pltpu.VMEM((2, depth, kv_width), BF16),
            pltpu.VMEM(windows.shape, BF16),
            pltpu.VMEM((prompt_rows, half), BF16),
            pltpu.VMEM((prompt_rows, half), BF16),
            pltpu.VMEM((prompt_rows, half), F32),
            pltpu.VMEM((2, WINDOW, kv_width), F32),
            pltpu.VMEM((2, out_rows, kv_width), BF16),
            pltpu.VMEM((2, out_rows, kv_width), BF16),
            dma((3, 5)),
            dma((14,)),
            dma((14,)),
            dma((REDUCE_COPIES,)),
            dma((REDUCE_COPIES,)),
            dma((GATHER_COPIES,)),
            dma((GATHER_COPIES,)),
            dma((3,)),
            dma((3,)),
        ],
        compiler_params=params(60, collective_id=1, has_side_effects=True),
        name="backward",
    )(token_part, pick, ref_scores, q, t, inv, raw_keys, gain, e, g, kw, vw, windows)


def shards(
    prompt_hidden,
    key_weight,
    value_weight,
    key_gain,
    queries,
    response_kv,
    targets,
    ref_scores,
    lengths,
    placement_map,
):
    hidden = prompt_hidden[0]
    prompt_rows, model_width = hidden.shape
    head_width = key_gain.shape[0]
    kv_width = key_weight.shape[1]
    kv_heads = kv_width // head_width
    resp_rows = queries.shape[1]
    query_heads = queries.shape[2] // head_width
    grouped = query_heads // kv_heads
    slot_count = lengths.shape[2]
    responses = ref_scores.shape[1]
    n_ctx = lax.axis_size("ctx")
    qk_scale = 1.0 / math.sqrt(head_width)
    gain = key_gain[None]

    raw_keys, prompt_keys, prompt_values = project_and_gather(
        hidden, key_weight, value_weight, gain
    )

    ends = jnp.cumsum(lengths[0, 0], dtype=jnp.int32)
    row_ids = lax.iota(jnp.int32, resp_rows)
    slot_ids = jnp.sum(
        (row_ids[:, None] >= ends[None, :]).astype(jnp.int32), axis=1, dtype=jnp.int32
    )
    same_slot = (slot_ids[:, None] == slot_ids[None, :]) & (row_ids[None, :] <= row_ids[:, None])
    in_slot = slot_ids[:, None] == lax.iota(jnp.int32, slot_count)[None, :]
    response_ids = jnp.sum(
        jnp.where(in_slot, placement_map[0][None, :], 0), axis=1, dtype=jnp.int32
    )
    pick = (response_ids[:, None] == lax.iota(jnp.int32, responses)[None, :]).astype(F32)
    pad = -resp_rows % 128
    bias = jnp.pad(
        jnp.where(same_slot, 0.0, MASK_FILL).astype(F32),
        ((0, 0), (0, pad)),
        constant_values=MASK_FILL,
    )
    resp = jnp.pad(response_kv[0], ((0, pad), (0, 0), (0, 0)))
    q, t = queries[0], targets[0]
    e, g, inv, dq, token_part, windows = attend(
        q,
        t,
        prompt_keys,
        prompt_values,
        resp[:, 0],
        resp[:, 1],
        bias,
        hidden,
        n_ctx,
        qk_scale,
        grouped,
        2,
    )
    dpo_loss, row_grad, resp_grad, prompt_grad, weight_grad = backward(
        token_part,
        pick,
        ref_scores,
        q,
        t,
        inv,
        raw_keys,
        gain,
        e,
        g,
        key_weight,
        value_weight,
        windows,
        qk_scale,
        model_width // n_ctx // 2,
    )
    query_grad = (dq.astype(F32) * row_grad).astype(BF16)
    return (
        dpo_loss[0],
        query_grad[None],
        resp_grad.transpose(1, 0, 2)[None],
        prompt_grad[None],
        weight_grad.transpose(1, 0, 2),
    )


def solution(mesh):
    in_specs = (
        P("dp", "ctx", None),
        P(None, "tp"),
        P(None, "tp"),
        P(),
        P("dp", "ctx", "tp"),
        P("dp", "ctx", None, "tp"),
        P("dp", "ctx", "tp"),
        P("dp", None),
        P("dp", "ctx", None),
        P("dp", "ctx"),
    )
    out_specs = (
        P("dp"),
        P("dp", "ctx", "tp"),
        P("dp", "ctx", None, "tp"),
        P("dp", "ctx", "tp"),
        P(("ctx", "dp"), None, "tp"),
    )
    return jax.shard_map(shards, mesh=mesh, in_specs=in_specs, out_specs=out_specs, check_vma=False)
```

```python
import functools
import math

import jax
import jax.numpy as jnp
from jax import lax
from jax.experimental import pallas as pl
from jax.experimental.pallas import tpu as pltpu
from jax.sharding import PartitionSpec as P

NORM_EPS = 1e-06
DPO_BETA = 0.5
MASK_FILL = -1e30
LOG2E = 1.4426950408889634
NT = (((1,), (1,)), ((), ()))
TN = (((0,), (0,)), ((), ()))
F32 = jnp.float32
BF16 = jnp.bfloat16


MESH = pl.DeviceIdType.MESH
SIDE = 4


def params(limit_mib, **more):
    return pltpu.CompilerParams(vmem_limit_bytes=limit_mib * 1024 * 1024, **more)


def place():
    me = lax.axis_index("ctx")
    return me // (2 * SIDE), (me // 2) % SIDE, me % 2


def ctx_id(x, z, core):
    return {"ctx": (x * SIDE + z) * 2 + core}


def greet(peers):
    barrier = pltpu.get_barrier_semaphore()
    for peer in peers:
        pl.semaphore_signal(barrier, inc=1, device_id=peer, device_id_type=MESH)
    pl.semaphore_wait(barrier, len(peers))


def plane_peers():
    x, z, core = place()
    return [
        ctx_id((x + 1) % SIDE, z, core),
        ctx_id((x + SIDE - 1) % SIDE, z, core),
        ctx_id(x, (z + 1) % SIDE, core),
        ctx_id(x, (z + SIDE - 1) % SIDE, core),
        ctx_id(x, z, 1 - core),
    ]


def ring(axis):
    x, z, core = place()
    if axis == 0:
        return x, lambda p: ctx_id(p, z, core)
    return z, lambda p: ctx_id(x, p, core)


def around(p):
    return (p + 1) % SIDE, (p + SIDE - 1) % SIDE, (p + 2) % SIDE


class Copies:
    def __init__(self, send_sem, recv_sem):
        self.send_sem, self.recv_sem, self.started = send_sem, recv_sem, []

    def make(self, src, dst, peer, slot):
        return pltpu.make_async_remote_copy(
            src_ref=src,
            dst_ref=dst,
            send_sem=self.send_sem.at[slot],
            recv_sem=self.recv_sem.at[slot],
            device_id=peer,
            device_id_type=MESH,
        )

    def send(self, src, dst, peer, slot):
        one = self.make(src, dst, peer, slot)
        one.start()
        self.started.append(one)

    def arrived(self, dst, slot):
        x, z, core = place()
        self.make(dst, dst, ctx_id(x, z, 1 - core), slot).wait_recv()

    def finish(self):
        for one in self.started:
            one.wait_send()


GATHER_COPIES = 72


def gather_stages(refs, copies):
    x, z, core = place()
    partner = ctx_id(x, z, 1 - core)
    rows = refs[0].shape[3]
    full, low, high = pl.ds(0, rows), pl.ds(0, rows // 2), pl.ds(rows // 2, rows // 2)
    rings = {}
    for kv in range(2):
        for level in range(2):
            p, at = ring(kv if level == 0 else 1 - kv)
            right, left, opposite = around(p)
            rings[kv, level] = ((p, left, right, opposite), at(right), at(left))

    def block(kv, i, j, part=full, of_core=None):
        of_core = core if of_core is None else of_core
        i, j = rings[kv, 0][0][i], rings[kv, 1][0][j]
        spot = (i, j) if kv == 0 else (j, i)
        return refs[kv].at[spot[0], spot[1], of_core, part]

    def first(kv, k):
        return kv * 36 + k

    def second(kv, i, k):
        return kv * 36 + 4 + i * 4 + k

    def swap_slot(kv, i, j):
        return kv * 36 + 20 + i * 4 + j

    def send(ref, peer, slot):
        copies.send(ref, ref, peer, slot)

    def to_core(kv, i, j):
        send(block(kv, i, j), partner, swap_slot(kv, i, j))

    def onward(kv, i):
        _, right, left = rings[kv, 1]
        send(block(kv, i, 0), right, second(kv, i, 0))
        send(block(kv, i, 0), left, second(kv, i, 1))
        to_core(kv, i, 0)

    def open_all():
        for kv in range(2):
            _, right, left = rings[kv, 0]
            send(block(kv, 0, 0), right, first(kv, 0))
            send(block(kv, 0, 0), left, first(kv, 1))
        for kv in range(2):
            onward(kv, 0)

    def first_neighbours():
        for kv in range(2):
            _, right, left = rings[kv, 0]
            copies.arrived(block(kv, 1, 0), first(kv, 0))
            send(block(kv, 1, 0, low), right, first(kv, 2))
            onward(kv, 1)
            copies.arrived(block(kv, 2, 0), first(kv, 1))
            send(block(kv, 2, 0, high), left, first(kv, 3))
            onward(kv, 2)

    def first_opposite():
        for kv in range(2):
            copies.arrived(block(kv, 3, 0, low), first(kv, 2))
            copies.arrived(block(kv, 3, 0, high), first(kv, 3))
            onward(kv, 3)

    def second_neighbours(i):
        for kv in range(2):
            _, right, left = rings[kv, 1]
            copies.arrived(block(kv, i, 1), second(kv, i, 0))
            send(block(kv, i, 1, low), right, second(kv, i, 2))
            to_core(kv, i, 1)
            copies.arrived(block(kv, i, 2), second(kv, i, 1))
            send(block(kv, i, 2, high), left, second(kv, i, 3))
            to_core(kv, i, 2)

    def second_opposite(i):
        for kv in range(2):
            copies.arrived(block(kv, i, 3, low), second(kv, i, 2))
            copies.arrived(block(kv, i, 3, high), second(kv, i, 3))
            to_core(kv, i, 3)

    def from_core(kv):
        for i in range(4):
            for j in range(4):
                copies.arrived(block(kv, i, j, full, 1 - core), swap_slot(kv, i, j))

    return [
        open_all,
        first_neighbours,
        lambda: second_neighbours(0),
        first_opposite,
        lambda: second_neighbours(1),
        lambda: second_opposite(0),
        lambda: second_neighbours(2),
        lambda: second_opposite(1),
        lambda: second_neighbours(3),
        lambda: second_opposite(2),
        lambda: second_opposite(3),
        lambda: from_core(0),
        lambda: from_core(1),
    ]


def project_kernel(
    h_ref,
    kw_ref,
    vw_ref,
    gain_ref,
    raw_ref,
    gk_ref,
    gv_ref,
    w_ref,
    load_sem,
    send_sem,
    recv_sem,
):
    x, z, core = place()
    steps, tile, width = w_ref.shape[1:]

    def load(kv, i):
        src = (kw_ref, vw_ref)[kv].at[pl.ds(i * tile, tile)]
        return pltpu.make_async_copy(src, w_ref.at[kv, i], load_sem.at[kv, i])

    for i in range(steps):
        for kv in range(2):
            load(kv, i).start()
    greet(plane_peers())
    sums = [jnp.zeros((h_ref.shape[0], width), F32)] * 2
    for i in range(steps):
        part = h_ref[:, i * tile : (i + 1) * tile]
        for kv in range(2):
            load(kv, i).wait()
            sums[kv] = sums[kv] + jnp.dot(part, w_ref[kv, i], preferred_element_type=F32)
    raw_ref[...] = sums[0]
    gv_ref[x, z, core] = sums[1].astype(BF16)
    parts = []
    for i in range(width // 128):
        keys = sums[0][:, i * 128 : (i + 1) * 128]
        inv = lax.rsqrt(jnp.mean(keys * keys, axis=1, keepdims=True) + NORM_EPS)
        parts.append((keys * inv * gain_ref[...]).astype(BF16))
    gk_ref[x, z, core] = jnp.concatenate(parts, axis=1)
    copies = Copies(send_sem, recv_sem)
    for stage in gather_stages((gk_ref, gv_ref), copies):
        stage()
    copies.finish()


def project_and_gather(hidden, key_weight, value_weight, gain):
    rows, depth = hidden.shape
    width = key_weight.shape[1]
    tile = 1024
    steps = depth // tile
    vmem, anywhere = pl.BlockSpec(memory_space=pltpu.VMEM), pl.BlockSpec(memory_space=pl.ANY)
    plane = jax.ShapeDtypeStruct((SIDE, SIDE, 2, rows, width), BF16)
    raw, keys, values = pl.pallas_call(
        project_kernel,
        out_shape=[jax.ShapeDtypeStruct((rows, width), F32), plane, plane],
        in_specs=[vmem, anywhere, anywhere, vmem],
        out_specs=[vmem] * 3,
        scratch_shapes=[
            pltpu.VMEM((2, steps, tile, width), BF16),
            pltpu.SemaphoreType.DMA((2, steps)),
            pltpu.SemaphoreType.DMA((GATHER_COPIES,)),
            pltpu.SemaphoreType.DMA((GATHER_COPIES,)),
        ],
        compiler_params=params(60, collective_id=0, has_side_effects=True),
        name="project_and_gather",
    )(hidden, key_weight, value_weight, gain)
    total = SIDE * SIDE * 2 * rows
    return raw, keys.reshape(total, width), values.reshape(total, width)


def slots_of(lengths_ref, ids):
    slots, end = jnp.zeros(ids.shape, jnp.int32), 0
    for i in range(lengths_ref.shape[0]):
        end = end + lengths_ref[i]
        slots = slots + jnp.where(ids >= end, 1, 0)
    return slots


def slot_bias(lengths_ref, rows, pad):
    row = lax.broadcasted_iota(jnp.int32, (rows, pad), 0)
    key = lax.broadcasted_iota(jnp.int32, (rows, pad), 1)
    seen = (slots_of(lengths_ref, row) == slots_of(lengths_ref, key)) & (key <= row)
    return jnp.where(seen, 0.0, MASK_FILL)


def response_pick(lengths_ref, map_ref, rows, responses):
    slots = slots_of(lengths_ref, lax.broadcasted_iota(jnp.int32, (rows, responses), 0))
    ids = jnp.zeros((rows, responses), jnp.int32)
    for i in range(map_ref.shape[0]):
        ids = jnp.where(slots == i, map_ref[i], ids)
    return jnp.where(ids == lax.broadcasted_iota(jnp.int32, (rows, responses), 1), 1.0, 0.0)


def attend_kernel(
    scale,
    q_ref,
    t_ref,
    k_ref,
    v_ref,
    r_ref,
    lengths_ref,
    h_ref,
    e_ref,
    g_ref,
    inv_ref,
    dq_ref,
    tok_ref,
    o_ref,
    own_sem,
    send_sem,
    recv_sem,
):
    me = lax.axis_index("ctx")
    n = o_ref.shape[0]

    def window(peer):
        tile = 5 * (peer // 4) + peer % 4
        return h_ref.at[:, pl.ds(pl.multiple_of(tile * 128, 128), WINDOW)]

    def copy(k):
        peer = (me + k) % n
        return pltpu.make_async_remote_copy(
            src_ref=window(peer),
            dst_ref=o_ref.at[me],
            send_sem=send_sem.at[k - 1],
            recv_sem=recv_sem.at[k - 1],
            device_id={"ctx": peer},
            device_id_type=MESH,
        )

    own_copy = pltpu.make_async_copy(window(me), o_ref.at[me], own_sem)

    @pl.when((pl.program_id(0) == 0) & (pl.program_id(1) == 0))
    def _():
        barrier = pltpu.get_barrier_semaphore()

        def hello(k, carry):
            pl.semaphore_signal(
                barrier, inc=1, device_id={"ctx": (me + k) % n}, device_id_type=MESH
            )
            return carry

        def go(k, carry):
            copy(k).start()
            return carry

        lax.fori_loop(1, n, hello, 0)
        pl.semaphore_wait(barrier, n - 1)
        lax.fori_loop(1, n, go, 0)
        own_copy.start()
        tok_ref[...] = jnp.zeros_like(tok_ref)

    rows, heads = q_ref.shape[0], q_ref.shape[1] // 128
    tokens = k_ref.shape[0]
    pad = -rows % 128
    filler = jnp.zeros((pad, 128), BF16)
    k, v = k_ref[...], v_ref[...]
    rk = jnp.concatenate([r_ref[0], filler], axis=0)
    rv = jnp.concatenate([r_ref[1], filler], axis=0)
    bias = slot_bias(lengths_ref, rows, rows + pad)
    factor = scale * LOG2E
    parts = range(0, heads, 2)
    bias = jnp.concatenate([bias, bias], axis=0)

    def two(ref, i):
        return jnp.concatenate([ref[:, i * 128 : (i + 1) * 128], ref[:, (i + 1) * 128 : (i + 2) * 128]], axis=0)

    def out_rows(i):
        return slice(i * rows, (i + 2) * rows)

    def logits(i):
        q = two(q_ref, i)
        s = lax.dot_general(q, k, NT, preferred_element_type=F32)
        return s, lax.dot_general(q, rk, NT, preferred_element_type=F32) + bias

    def weigh(i, s, sr):
        peak = jnp.maximum(
            jnp.max(s, axis=1, keepdims=True), jnp.max(sr, axis=1, keepdims=True)
        )
        top = peak * factor
        e = jnp.exp2(s * factor - top)
        er = jnp.exp2(sr * factor - top)
        inv = 1.0 / (
            jnp.sum(e, axis=1, keepdims=True) + jnp.sum(er, axis=1, keepdims=True)
        )
        e_ref[0, out_rows(i), :tokens] = e.astype(BF16)
        e_ref[0, out_rows(i), tokens:] = er.astype(BF16)
        inv_ref[0, out_rows(i)] = inv
        return inv

    def read(i, inv):
        t = two(t_ref, i)
        e, er = e_ref[0, out_rows(i), :tokens], e_ref[0, out_rows(i), tokens:]
        dp = lax.dot_general(t, v, NT, preferred_element_type=F32)
        dpr = lax.dot_general(t, rv, NT, preferred_element_type=F32)
        attended = jnp.dot(e, v, preferred_element_type=F32)
        attended = (attended + jnp.dot(er, rv, preferred_element_type=F32)) * inv
        dot = jnp.sum(attended * t.astype(F32), axis=1, keepdims=True)
        return dp, dpr, dot

    def differ(i, dp, dpr, dot):
        e, er = e_ref[0, out_rows(i), :tokens], e_ref[0, out_rows(i), tokens:]
        g_ref[0, out_rows(i), :tokens] = (e.astype(F32) * (dp - dot)).astype(BF16)
        g_ref[0, out_rows(i), tokens:] = (er.astype(F32) * (dpr - dot)).astype(BF16)

    def query_grad(i, inv):
        g, gr = g_ref[0, out_rows(i), :tokens], g_ref[0, out_rows(i), tokens:]
        dq = jnp.dot(g, k, preferred_element_type=F32)
        dq = (dq + jnp.dot(gr, rk, preferred_element_type=F32)) * (inv * scale)
        dq_ref[:, i * 128 : (i + 1) * 128] = dq[:rows].astype(BF16)
        dq_ref[:, (i + 1) * 128 : (i + 2) * 128] = dq[rows:].astype(BF16)

    scores = {i: logits(i) for i in parts}
    invs, reads, total = {}, {}, jnp.zeros((rows, 1), F32)
    for i in parts:
        invs[i] = weigh(i, *scores[i])
        reads[i] = read(i, invs[i])
        if i >= 2:
            differ(i - 2, *reads[i - 2])
            query_grad(i - 2, invs[i - 2])
    last = heads - 2
    differ(last, *reads[last])
    query_grad(last, invs[last])
    for i in parts:
        dot = reads[i][2]
        total = total + dot[:rows] + dot[rows:]
    tok_ref[...] += total

    @pl.when(
        (pl.program_id(0) == pl.num_programs(0) - 1) & (pl.program_id(1) == pl.num_programs(1) - 1)
    )
    def _():
        def done(k, carry):
            copy(k).wait()
            return carry

        own_copy.wait()
        lax.fori_loop(1, n, done, 0)


WINDOW = 256


def attend(q, t, prompt_keys, prompt_values, resp, lengths, hidden, n, scale, grouped, chunk):
    rows = q.shape[0]
    tokens, kv_width = prompt_keys.shape
    kv_heads = kv_width // 128
    pad = rows + -rows % 128
    steps = grouped // chunk
    m = chunk * rows
    total = grouped * rows
    row_block = pl.BlockSpec((rows, chunk * 128), lambda h, c: (0, h * steps + c))
    head_block = pl.BlockSpec((tokens, 128), lambda h, c: (0, h))

    def score_block(width):
        return pl.BlockSpec((1, m, width), lambda h, c: (h, c, 0))

    return pl.pallas_call(
        functools.partial(attend_kernel, scale),
        grid=(kv_heads, steps),
        in_specs=[
            row_block,
            row_block,
            head_block,
            head_block,
            pl.BlockSpec((2, rows, 128), lambda h, c: (0, 0, h)),
            pl.BlockSpec(memory_space=pltpu.SMEM),
            pl.BlockSpec(memory_space=pl.ANY),
        ],
        out_specs=[
            score_block(tokens + pad),
            score_block(tokens + pad),
            score_block(1),
            row_block,
            pl.BlockSpec((rows, 1), lambda h, c: (0, 0)),
            pl.BlockSpec(memory_space=pl.ANY),
        ],
        out_shape=[
            jax.ShapeDtypeStruct((kv_heads, total, tokens + pad), BF16),
            jax.ShapeDtypeStruct((kv_heads, total, tokens + pad), BF16),
            jax.ShapeDtypeStruct((kv_heads, total, 1), F32),
            jax.ShapeDtypeStruct(q.shape, BF16),
            jax.ShapeDtypeStruct((rows, 1), F32),
            jax.ShapeDtypeStruct((n, hidden.shape[0], WINDOW), BF16),
        ],
        scratch_shapes=[
            pltpu.SemaphoreType.DMA,
            pltpu.SemaphoreType.DMA((n - 1,)),
            pltpu.SemaphoreType.DMA((n - 1,)),
        ],
        compiler_params=params(56, collective_id=3, has_side_effects=True),
        name="attend",
    )(q, t, prompt_keys, prompt_values, resp, lengths, hidden)


def norm_backward(raw, gain, grad):
    parts = []
    for h in range(raw.shape[1] // 128):
        keys = raw[:, h * 128 : (h + 1) * 128]
        kg = gain * grad[:, h * 128 : (h + 1) * 128]
        inv = lax.rsqrt(jnp.mean(keys * keys, axis=1, keepdims=True) + NORM_EPS)
        mix = jnp.mean(keys * kg, axis=1, keepdims=True)
        parts.append(inv * kg - keys * (inv * inv * inv) * mix)
    return jnp.concatenate(parts, axis=1)


def total_of(*refs):
    value = refs[0][...].astype(F32)
    for ref in refs[1:]:
        value = value + ref[...].astype(F32)
    return value


REDUCE_COPIES = 68


class Reduce:
    def __init__(self, d_ref, c_ref, a_ref, b_ref, r_ref, s_ref, copies):
        self.d, self.c, self.a, self.b, self.r, self.s = d_ref, c_ref, a_ref, b_ref, r_ref, s_ref
        self.copies = copies
        x, z, self.core = place()
        self.partner = ctx_id(x, z, 1 - self.core)
        rows = a_ref.shape[3]
        self.low, self.high = pl.ds(0, rows // 2), pl.ds(rows // 2, rows // 2)
        self.rings = {}
        for kv in range(2):
            for inner in range(2):
                p, at = ring(1 - kv if inner else kv)
                right, left, opposite = around(p)
                self.rings[kv, inner] = ((opposite, right, left, p), at(right), at(left))

    def place_of(self, kv, i):
        return self.rings[kv, 0][0][i]

    def to_core(self, kv, i):
        self.copies.send(
            self.d.at[kv, i, :, 1 - self.core], self.c.at[kv, i], self.partner, kv * 4 + i
        )

    def landing(self, kv, i, k):
        return self.s.at[kv, k] if i is None else self.b.at[kv, i, k]

    def slot(self, kv, i, k):
        return 56 + kv * 6 + k if i is None else 8 + (kv * 4 + i) * 6 + k

    def unit(self, kv, i, j, part):
        if i is None:
            return self.r.at[kv, j, part]
        return self.a.at[kv, i, self.rings[kv, 1][0][j], part]

    def message(self, kv, i, k, ref):
        _, right, left = self.rings[kv, 0 if i is None else 1]
        peer = right if k in (0, 2, 4) else left
        self.copies.send(ref, self.landing(kv, i, k), peer, self.slot(kv, i, k))

    def landed(self, kv, i, k):
        ref = self.landing(kv, i, k)
        self.copies.arrived(ref, self.slot(kv, i, k))
        return ref

    def opening(self, kv, i, j):
        if j == 0:
            self.message(kv, i, 0, self.unit(kv, i, 0, self.low))
            self.message(kv, i, 1, self.unit(kv, i, 0, self.high))
        if j == 1:
            self.message(kv, i, 2, self.unit(kv, i, 1, self.high))
        if j == 2:
            self.message(kv, i, 3, self.unit(kv, i, 2, self.low))

    def passing(self, kv, i):
        for k, j, part in ((0, 1, self.low), (1, 2, self.high)):
            came = self.landed(kv, i, k)
            mine = self.unit(kv, i, j, part)
            mine[...] = total_of(mine, came).astype(BF16)
            self.message(kv, i, 4 + k, mine)

    def result(self, kv, i):
        lows = total_of(
            self.unit(kv, i, 3, self.low), self.landed(kv, i, 3), self.landed(kv, i, 4)
        )
        highs = total_of(
            self.unit(kv, i, 3, self.high), self.landed(kv, i, 2), self.landed(kv, i, 5)
        )
        return jnp.concatenate([lows, highs], axis=0)

    def start_inner(self, kv, i):
        self.copies.arrived(self.c.at[kv, i], kv * 4 + i)
        self.a[kv, i] = total_of(self.d.at[kv, i, :, self.core], self.c.at[kv, i]).astype(BF16)
        for j in range(3):
            self.opening(kv, i, j)

    def end_inner(self, kv, i):
        self.r[kv, i] = self.result(kv, i).astype(BF16)
        self.opening(kv, None, i)


def share_scores(buf, me, peer, copies, base):
    sent = []
    for k in range(1, 8):
        copies.send(buf.at[me], buf.at[me], peer(k), base + k - 1)
    for k in range(1, 8):
        copies.arrived(buf.at[(me - k + 8) % 8], base + k - 1)
    value = buf[0]
    for i in range(1, 8):
        value = value + buf[i]
    return value


def backward_kernel(
    scale,
    token_ref,
    lengths_ref,
    map_ref,
    ref_ref,
    q_ref,
    t_ref,
    inv_ref,
    dq_ref,
    raw_ref,
    gain_ref,
    e_ref,
    g_ref,
    kw_ref,
    vw_ref,
    hw_ref,
    loss_ref,
    qgrad_ref,
    resp_ref,
    pgrad_ref,
    wgrad_ref,
    one_ref,
    two_ref,
    qs_ref,
    ts_ref,
    gbuf_ref,
    ebuf_ref,
    rbuf_ref,
    d_ref,
    c_ref,
    a_ref,
    b_ref,
    r_ref,
    s_ref,
    gk_ref,
    gv_ref,
    w_ref,
    h_ref,
    paway_ref,
    pcame_ref,
    pown_ref,
    wpart_ref,
    waway_ref,
    wcame_ref,
    load_sem,
    score_send,
    score_recv,
    reduce_send,
    reduce_recv,
    gather_send,
    gather_recv,
    last_send,
    last_recv,
):
    x, z, core = place()
    ctx, tp, dp = lax.axis_index("ctx"), lax.axis_index("tp"), lax.axis_index("dp")
    kv_heads, total, _ = qs_ref.shape
    rows = q_ref.shape[0]
    grouped = total // rows
    tokens = e_ref.shape[2] - rbuf_ref.shape[3]
    chunk = gbuf_ref.shape[3]
    unit = chunk // SIDE

    reduce_copies = Copies(reduce_send, reduce_recv)
    reduce = Reduce(d_ref, c_ref, a_ref, b_ref, r_ref, s_ref, reduce_copies)

    def loads(i):
        buf = i % 2
        start = pl.multiple_of(reduce.place_of(0, i) * chunk, chunk)
        parts = [
            pltpu.make_async_copy(
                g_ref.at[:, :, pl.ds(start, chunk)], gbuf_ref.at[buf], load_sem.at[buf, 0]
            )
        ]
        for j in range(SIDE):
            start = pl.multiple_of(j * chunk + reduce.place_of(1, i) * unit, unit)
            parts.append(
                pltpu.make_async_copy(
                    e_ref.at[:, :, pl.ds(start, unit)],
                    ebuf_ref.at[buf, :, :, pl.ds(j * unit, unit)],
                    load_sem.at[buf, 1 + j],
                )
            )
        return parts

    def start(parts):
        for one in parts:
            one.start()

    def wait(parts):
        for one in parts:
            one.wait()

    tail = pl.ds(tokens, rbuf_ref.shape[3])
    more = [
        pltpu.make_async_copy(g_ref.at[:, :, tail], rbuf_ref.at[0], load_sem.at[2, 0]),
        pltpu.make_async_copy(e_ref.at[:, :, tail], rbuf_ref.at[1], load_sem.at[2, 1]),
    ]
    late = [
        pltpu.make_async_copy(kw_ref, w_ref.at[0], load_sem.at[2, 2]),
        pltpu.make_async_copy(vw_ref, w_ref.at[1], load_sem.at[2, 3]),
        pltpu.make_async_copy(hw_ref, h_ref, load_sem.at[2, 4]),
    ]
    for i in range(2):
        start(loads(i))

    def first(k):
        q = (x * 2 + tp + k) % 8
        return {"ctx": ((q // 2) * SIDE + z) * 2 + core, "tp": q % 2}

    def second(k):
        q = (z * 2 + core + k) % 8
        return {"ctx": x * SIDE * 2 + q}

    other_dp = {"dp": 1 - dp}
    greet([first(k) for k in range(1, 8)] + [second(k) for k in range(1, 8)] + [other_dp])
    score_copies = Copies(score_send, score_recv)
    pick = response_pick(lengths_ref, map_ref, rows, ref_ref.shape[1])
    part = jnp.sum(pick * token_ref[...], axis=0, keepdims=True)
    one_ref[x * 2 + tp] = jnp.broadcast_to(part, one_ref.shape[1:])
    half_sum = share_scores(one_ref, x * 2 + tp, first, score_copies, 0)
    two_ref[z * 2 + core] = half_sum
    scores = share_scores(two_ref, z * 2 + core, second, score_copies, 7)[:1]
    pairs = scores.shape[1] // 2
    shifted = scores - ref_ref[...]
    margin = DPO_BETA * (shifted[:, :pairs] - shifted[:, pairs:])
    small = jnp.exp(-jnp.abs(margin))
    pair_grad = -DPO_BETA * jnp.where(margin >= 0.0, small, 1.0) / (1.0 + small)
    score_grad = jnp.concatenate([pair_grad, -pair_grad], axis=1)
    row_grad = jnp.sum(pick * score_grad, axis=1, keepdims=True)
    row_factor = jnp.concatenate([row_grad] * grouped, axis=0)
    start(more)
    for h in range(kv_heads):
        factor = inv_ref[h] * row_factor
        base = h * grouped * 128
        pieces = [q_ref[:, base + i * 128 : base + (i + 1) * 128] for i in range(grouped)]
        q = jnp.concatenate(pieces, axis=0).astype(F32)
        qs_ref[h] = (q * (factor * scale)).astype(BF16)
        pieces = [t_ref[:, base + i * 128 : base + (i + 1) * 128] for i in range(grouped)]
        t = jnp.concatenate(pieces, axis=0).astype(F32)
        ts_ref[h] = (t * factor).astype(BF16)

    def chunk_grads(i):
        buf = i % 2
        for kv, (kept, scaled) in enumerate(((gbuf_ref, qs_ref), (ebuf_ref, ts_ref))):
            for h in range(kv_heads):
                grads = lax.dot_general(kept[buf, h], scaled[h], TN, preferred_element_type=F32)
                grads = grads.astype(BF16).reshape(SIDE, 2, unit // 2, 128)
                d_ref[kv, i, :, :, :, h * 128 : (h + 1) * 128] = grads
            reduce.to_core(kv, i)

    for i in range(SIDE):
        wait(loads(i))
        chunk_grads(i)
        if i + 2 < SIDE:
            start(loads(i + 2))
        if i == SIDE - 2:
            start(late)
        if i >= 1:
            for kv in range(2):
                reduce.start_inner(kv, i - 1)
        if i >= 2:
            for kv in range(2):
                reduce.passing(kv, i - 2)
        if i >= 3:
            for kv in range(2):
                reduce.end_inner(kv, i - 3)
    for kv in range(2):
        reduce.start_inner(kv, 3)
    for kv in range(2):
        reduce.passing(kv, 2)
    for kv in range(2):
        reduce.end_inner(kv, 1)
    for kv in range(2):
        reduce.passing(kv, 3)
    wait(more)
    for kv, scaled in enumerate((qs_ref, ts_ref)):
        for h in range(kv_heads):
            grads = lax.dot_general(rbuf_ref[kv, h], scaled[h], TN, preferred_element_type=F32)
            resp_ref[kv, :, h * 128 : (h + 1) * 128] = grads[:rows].astype(BF16)
    qgrad_ref[...] = (dq_ref[...].astype(F32) * row_grad).astype(BF16)
    loss = jnp.maximum(-margin, 0.0) + jnp.log1p(small)
    loss_ref[...] = jnp.sum(loss, axis=1, keepdims=True)
    for kv in range(2):
        reduce.end_inner(kv, 2)
    for kv in range(2):
        reduce.passing(kv, None)
    for kv in range(2):
        reduce.end_inner(kv, 3)
    key_sum = reduce.result(0, None)
    gk_ref[x, z, core] = norm_backward(raw_ref[...], gain_ref[...], key_sum).astype(BF16)
    gv_ref[x, z, core] = reduce.result(1, None).astype(BF16)

    gather_copies = Copies(gather_send, gather_recv)
    stages = gather_stages((gk_ref, gv_ref), gather_copies)
    last_copies = Copies(last_send, last_recv)
    stages[0]()
    wait(late)
    tile = 512
    half = paway_ref.shape[1]

    def input_grad(side, store):
        key_grad, value_grad = gk_ref[x, z, core], gv_ref[x, z, core]

        def step(i, carry):
            here = pl.ds(pl.multiple_of(side * half + i * tile, tile), tile)
            value = lax.dot_general(key_grad, w_ref[0, here], NT, preferred_element_type=F32)
            value += lax.dot_general(value_grad, w_ref[1, here], NT, preferred_element_type=F32)
            store(pl.ds(pl.multiple_of(i * tile, tile), tile), value)
            return carry

        lax.fori_loop(0, half // tile, step, 0)

    def store_away(here, value):
        paway_ref[:, here] = value.astype(BF16)

    def store_own(here, value):
        pown_ref[:, here] = value

    input_grad(1 - tp, store_away)
    last_copies.send(paway_ref, pcame_ref, {"tp": 1 - tp}, 0)
    for stage in stages[1:5]:
        stage()
    input_grad(tp, store_own)
    for stage in stages[5:-2]:
        stage()
    last_copies.arrived(pcame_ref, 0)
    pgrad_ref[...] = (pown_ref[...] + pcame_ref[...].astype(F32)).astype(BF16)

    out_rows = wgrad_ref.shape[0]
    shift = (ctx % 4) * 32
    hidden = h_ref[...].reshape(-1, h_ref.shape[2])
    for kv, ref in enumerate((gk_ref, gv_ref)):
        stages[-2 + kv]()
        grads = ref[...].reshape(-1, ref.shape[4])
        wpart_ref[kv] = lax.dot_general(hidden, grads, TN, preferred_element_type=F32)
        away = pl.ds(pl.multiple_of(shift + (1 - dp) * out_rows, 16), out_rows)
        waway_ref[kv] = wpart_ref[kv, away].astype(BF16)
        last_copies.send(waway_ref.at[kv], wcame_ref.at[kv], other_dp, 1 + kv)
    for copies in (score_copies, reduce_copies, gather_copies):
        copies.finish()
    own = pl.ds(pl.multiple_of(shift + dp * out_rows, 16), out_rows)
    for kv in range(2):
        last_copies.arrived(wcame_ref.at[kv], 1 + kv)
        wgrad_ref[:, kv] = wpart_ref[kv, own] + wcame_ref[kv].astype(F32)
    last_copies.finish()


def backward(
    token_part,
    lengths,
    places,
    ref_scores,
    q,
    t,
    inv,
    dq,
    raw_keys,
    gain,
    e,
    g,
    kw,
    vw,
    windows,
    scale,
    out_rows,
):
    rows, responses = q.shape[0], ref_scores.shape[1]
    kv_heads, total, width = e.shape
    prompt_rows, kv_width = raw_keys.shape
    depth = kw.shape[0]
    n = windows.shape[0]
    tokens = n * prompt_rows
    pad = width - tokens
    chunk = tokens // SIDE
    half = depth // 2
    vmem, anywhere = pl.BlockSpec(memory_space=pltpu.VMEM), pl.BlockSpec(memory_space=pl.ANY)
    smem = pl.BlockSpec(memory_space=pltpu.SMEM)
    dma = pltpu.SemaphoreType.DMA
    small = (prompt_rows // 2, kv_width)
    return pl.pallas_call(
        functools.partial(backward_kernel, scale),
        out_shape=[
            jax.ShapeDtypeStruct((1, 1), F32),
            jax.ShapeDtypeStruct(q.shape, BF16),
            jax.ShapeDtypeStruct((2, rows, kv_width), BF16),
            jax.ShapeDtypeStruct((prompt_rows, half), BF16),
            jax.ShapeDtypeStruct((out_rows, 2, kv_width), F32),
        ],
        in_specs=[vmem, smem, smem] + [vmem] * 7 + [anywhere] * 5,
        out_specs=[vmem] * 5,
        scratch_shapes=[
            pltpu.VMEM((8, 8, responses), F32),
            pltpu.VMEM((8, 8, responses), F32),
            pltpu.VMEM((kv_heads, total, 128), BF16),
            pltpu.VMEM((kv_heads, total, 128), BF16),
            pltpu.VMEM((2, kv_heads, total, chunk), BF16),
            pltpu.VMEM((2, kv_heads, total, chunk), BF16),
            pltpu.VMEM((2, kv_heads, total, pad), BF16),
            pltpu.VMEM((2, SIDE, SIDE, 2, prompt_rows, kv_width), BF16),
            pltpu.VMEM((2, SIDE, SIDE, prompt_rows, kv_width), BF16),
            pltpu.VMEM((2, SIDE, SIDE, prompt_rows, kv_width), BF16),
            pltpu.VMEM((2, SIDE, 6) + small, BF16),
            pltpu.VMEM((2, SIDE, prompt_rows, kv_width), BF16),
            pltpu.VMEM((2, 6) + small, BF16),
            pltpu.VMEM((SIDE, SIDE, 2, prompt_rows, kv_width), BF16),
            pltpu.VMEM((SIDE, SIDE, 2, prompt_rows, kv_width), BF16),
            pltpu.VMEM((2, depth, kv_width), BF16),
            pltpu.VMEM(windows.shape, BF16),
            pltpu.VMEM((prompt_rows, half), BF16),
            pltpu.VMEM((prompt_rows, half), BF16),
            pltpu.VMEM((prompt_rows, half), F32),
            pltpu.VMEM((2, WINDOW, kv_width), F32),
            pltpu.VMEM((2, out_rows, kv_width), BF16),
            pltpu.VMEM((2, out_rows, kv_width), BF16),
            dma((3, 5)),
            dma((14,)),
            dma((14,)),
            dma((REDUCE_COPIES,)),
            dma((REDUCE_COPIES,)),
            dma((GATHER_COPIES,)),
            dma((GATHER_COPIES,)),
            dma((3,)),
            dma((3,)),
        ],
        compiler_params=params(60, collective_id=1, has_side_effects=True),
        name="backward",
    )(
        token_part,
        lengths,
        places,
        ref_scores,
        q,
        t,
        inv,
        dq,
        raw_keys,
        gain,
        e,
        g,
        kw,
        vw,
        windows,
    )


def shards(
    prompt_hidden,
    key_weight,
    value_weight,
    key_gain,
    queries,
    response_kv,
    targets,
    ref_scores,
    lengths,
    placement_map,
):
    hidden = prompt_hidden[0]
    prompt_rows, model_width = hidden.shape
    head_width = key_gain.shape[0]
    kv_width = key_weight.shape[1]
    kv_heads = kv_width // head_width
    query_heads = queries.shape[2] // head_width
    grouped = query_heads // kv_heads
    n_ctx = lax.axis_size("ctx")
    qk_scale = 1.0 / math.sqrt(head_width)
    gain = key_gain[None]

    raw_keys, prompt_keys, prompt_values = project_and_gather(
        hidden, key_weight, value_weight, gain
    )

    resp = response_kv[0].transpose(1, 0, 2)
    q, t = queries[0], targets[0]
    e, g, inv, dq, token_part, windows = attend(
        q,
        t,
        prompt_keys,
        prompt_values,
        resp,
        lengths[0, 0],
        hidden,
        n_ctx,
        qk_scale,
        grouped,
        4,
    )
    dpo_loss, query_grad, resp_grad, prompt_grad, weight_grad = backward(
        token_part,
        lengths[0, 0],
        placement_map[0],
        ref_scores,
        q,
        t,
        inv,
        dq,
        raw_keys,
        gain,
        e,
        g,
        key_weight,
        value_weight,
        windows,
        qk_scale,
        model_width // n_ctx // 2,
    )
    return (
        dpo_loss.reshape(1),
        query_grad[None],
        resp_grad.transpose(1, 0, 2)[None],
        prompt_grad[None],
        weight_grad,
    )


def solution(mesh):
    in_specs = (
        P("dp", "ctx", None),
        P(None, "tp"),
        P(None, "tp"),
        P(),
        P("dp", "ctx", "tp"),
        P("dp", "ctx", None, "tp"),
        P("dp", "ctx", "tp"),
        P("dp", None),
        P("dp", "ctx", None),
        P("dp", "ctx"),
    )
    out_specs = (
        P("dp"),
        P("dp", "ctx", "tp"),
        P("dp", "ctx", None, "tp"),
        P("dp", "ctx", "tp"),
        P(("ctx", "dp"), None, "tp"),
    )
    return jax.shard_map(shards, mesh=mesh, in_specs=in_specs, out_specs=out_specs, check_vma=False)
```

```python
import functools
import math

import jax
import jax.numpy as jnp
from jax import lax
from jax.experimental import pallas as pl
from jax.experimental.pallas import tpu as pltpu
from jax.sharding import PartitionSpec as P

NORM_EPS = 1e-06
DPO_BETA = 0.5
MASK_FILL = -1e30
LOG2E = 1.4426950408889634
NT = (((1,), (1,)), ((), ()))
TN = (((0,), (0,)), ((), ()))
F32 = jnp.float32
BF16 = jnp.bfloat16


MESH = pl.DeviceIdType.MESH
SIDE = 4


def params(limit_mib, **more):
    return pltpu.CompilerParams(vmem_limit_bytes=limit_mib * 1024 * 1024, **more)


def place():
    me = lax.axis_index("ctx")
    return me // (2 * SIDE), (me // 2) % SIDE, me % 2


def ctx_id(x, z, core):
    return {"ctx": (x * SIDE + z) * 2 + core}


def greet(peers):
    barrier = pltpu.get_barrier_semaphore()
    for peer in peers:
        pl.semaphore_signal(barrier, inc=1, device_id=peer, device_id_type=MESH)
    pl.semaphore_wait(barrier, len(peers))


def plane_peers():
    x, z, core = place()
    return [
        ctx_id((x + 1) % SIDE, z, core),
        ctx_id((x + SIDE - 1) % SIDE, z, core),
        ctx_id(x, (z + 1) % SIDE, core),
        ctx_id(x, (z + SIDE - 1) % SIDE, core),
        ctx_id(x, z, 1 - core),
    ]


def ring(axis):
    x, z, core = place()
    if axis == 0:
        return x, lambda p: ctx_id(p, z, core)
    return z, lambda p: ctx_id(x, p, core)


def around(p):
    return (p + 1) % SIDE, (p + SIDE - 1) % SIDE, (p + 2) % SIDE


class Copies:
    def __init__(self, send_sem, recv_sem):
        self.send_sem, self.recv_sem, self.started = send_sem, recv_sem, []
        self.draining = False

    def make(self, src, dst, peer, slot):
        return pltpu.make_async_remote_copy(
            src_ref=src,
            dst_ref=dst,
            send_sem=self.send_sem.at[slot],
            recv_sem=self.recv_sem.at[slot],
            device_id=peer,
            device_id_type=MESH,
        )

    def send(self, src, dst, peer, slot):
        one = self.make(src, dst, peer, slot)
        if self.draining:
            one.wait_send()
            return
        one.start()
        self.started.append(one)

    def arrived(self, dst, slot):
        if self.draining:
            return
        x, z, core = place()
        self.make(dst, dst, ctx_id(x, z, 1 - core), slot).wait_recv()

    def finish(self):
        for one in self.started:
            one.wait_send()


GATHER_COPIES = 24


def gather_stages(ref_of, rows, copies, base):
    x, z, core = place()
    partner = ctx_id(x, z, 1 - core)
    full, low, high = pl.ds(0, rows), pl.ds(0, rows // 2), pl.ds(rows // 2, rows // 2)
    rings = {}
    for kv in range(2):
        for phase in range(2):
            p, at = ring(kv if phase == 0 else 1 - kv)
            right, left, opposite = around(p)
            rings[kv, phase] = ((p, left, right, opposite), at(right), at(left))

    def block(kv, phase, i, part=full, of_core=core):
        p = rings[kv, phase][0][i]
        if phase == 1:
            x_at, z_at = (slice(None), p) if kv == 0 else (p, slice(None))
        else:
            x_at, z_at = (p, z) if kv == 0 else (x, p)
        return ref_of(kv).at[:, x_at, z_at, of_core, part]

    def slot(kv, phase, k):
        return base + (kv * 2 + phase) * 4 + k

    def send(ref, peer, at):
        copies.send(ref, ref, peer, at)

    def to_core(kv, i):
        send(block(kv, 1, i), partner, base + 16 + kv * 4 + i)

    def start(phase):
        for kv in range(2):
            _, right, left = rings[kv, phase]
            send(block(kv, phase, 0), right, slot(kv, phase, 0))
            send(block(kv, phase, 0), left, slot(kv, phase, 1))
        if phase == 1:
            for kv in range(2):
                to_core(kv, 0)

    def forward(phase):
        for kv in range(2):
            _, right, left = rings[kv, phase]
            copies.arrived(block(kv, phase, 1), slot(kv, phase, 0))
            send(block(kv, phase, 1, low), right, slot(kv, phase, 2))
            copies.arrived(block(kv, phase, 2), slot(kv, phase, 1))
            send(block(kv, phase, 2, high), left, slot(kv, phase, 3))
        if phase == 1:
            for kv in range(2):
                to_core(kv, 1)
                to_core(kv, 2)

    def close(phase):
        for kv in range(2):
            copies.arrived(block(kv, phase, 3, low), slot(kv, phase, 2))
            copies.arrived(block(kv, phase, 3, high), slot(kv, phase, 3))
            if phase == 1:
                to_core(kv, 3)

    def turn():
        close(0)
        start(1)

    def from_core():
        for kv in range(2):
            for i in range(4):
                copies.arrived(block(kv, 1, i, full, 1 - core), base + 16 + kv * 4 + i)

    return [
        lambda: start(0),
        lambda: forward(0),
        turn,
        lambda: forward(1),
        lambda: close(1),
        from_core,
    ]


def slots_of(lengths_ref, ids):
    slots, end = jnp.zeros(ids.shape, jnp.int32), 0
    for i in range(lengths_ref.shape[0]):
        end = end + lengths_ref[i]
        slots = slots + jnp.where(ids >= end, 1, 0)
    return slots


def slot_bias(lengths_ref, rows, pad):
    row = lax.broadcasted_iota(jnp.int32, (rows, pad), 0)
    key = lax.broadcasted_iota(jnp.int32, (rows, pad), 1)
    seen = (slots_of(lengths_ref, row) == slots_of(lengths_ref, key)) & (key <= row)
    return jnp.where(seen, 0.0, MASK_FILL)


def response_pick(lengths_ref, map_ref, rows, responses):
    slots = slots_of(lengths_ref, lax.broadcasted_iota(jnp.int32, (rows, responses), 0))
    ids = jnp.zeros((rows, responses), jnp.int32)
    for i in range(map_ref.shape[0]):
        ids = jnp.where(slots == i, map_ref[i], ids)
    return jnp.where(ids == lax.broadcasted_iota(jnp.int32, (rows, responses), 1), 1.0, 0.0)


WINDOW = 256


def forward_kernel(
    scale,
    hidden_ref,
    kw_ref,
    vw_ref,
    gain_ref,
    q_ref,
    t_ref,
    r_ref,
    lengths_ref,
    h_ref,
    raw_ref,
    e_out,
    g_ref,
    inv_ref,
    dq_ref,
    tok_ref,
    o_ref,
    w_ref,
    kv_ref,
    e_ref,
    dot_ref,
    load_sem,
    gather_send,
    gather_recv,
    own_sem,
    spread_send,
    spread_recv,
    e_sem,
):
    x, z, core = place()
    me = lax.axis_index("ctx")
    n = o_ref.shape[0]
    second_pass, head, part = (pl.program_id(i) for i in range(3))
    kv_heads, steps = e_ref.shape[:2]
    at_step = (second_pass * kv_heads + head) * steps + part
    half = kv_heads * steps
    rows, heads = q_ref.shape[0], q_ref.shape[1] // 128
    prompt_rows = raw_ref.shape[0]
    tokens = n * prompt_rows
    factor = scale * LOG2E

    def load(kv, i):
        tile = w_ref.shape[2]
        src = (kw_ref, vw_ref)[kv].at[pl.ds(i * tile, tile)]
        return pltpu.make_async_copy(src, w_ref.at[kv, i], load_sem.at[kv, i])

    gather_copies = Copies(gather_send, gather_recv)
    per = kv_heads // 2
    gathers = [
        gather_stages(
            lambda kv, i=i: kv_ref.at[kv, pl.ds(i, 1)],
            prompt_rows,
            gather_copies,
            i * GATHER_COPIES,
        )
        for i in range(2)
    ]

    def window(peer):
        tile = 5 * (peer // 4) + peer % 4
        return h_ref.at[:, pl.ds(pl.multiple_of(tile * 128, 128), WINDOW)]

    def spread(k):
        peer = (me + k) % n
        return pltpu.make_async_remote_copy(
            src_ref=window(peer),
            dst_ref=o_ref.at[me],
            send_sem=spread_send.at[k - 1],
            recv_sem=spread_recv.at[k - 1],
            device_id={"ctx": peer},
            device_id_type=MESH,
        )

    own_copy = pltpu.make_async_copy(window(me), o_ref.at[me], own_sem)

    def keep(i):
        place_of = (i // steps, i % steps)
        return pltpu.make_async_copy(e_ref.at[place_of], e_out.at[place_of], e_sem.at[i])

    @pl.when(at_step == 0)
    def _():
        for i in range(w_ref.shape[1]):
            for kv in range(2):
                load(kv, i).start()
        barrier = pltpu.get_barrier_semaphore()

        def hello(k, carry):
            pl.semaphore_signal(
                barrier, inc=1, device_id={"ctx": (me + k) % n}, device_id_type=MESH
            )
            return carry

        lax.fori_loop(1, n, hello, 0)
        tile, width = w_ref.shape[2:]
        sums = [jnp.zeros((prompt_rows, width), F32)] * 2
        for i in range(w_ref.shape[1]):
            piece = hidden_ref[:, i * tile : (i + 1) * tile]
            for kv in range(2):
                load(kv, i).wait()
                sums[kv] = sums[kv] + jnp.dot(piece, w_ref[kv, i], preferred_element_type=F32)
        raw_ref[...] = sums[0]
        for i in range(kv_heads):
            keys = sums[0][:, i * 128 : (i + 1) * 128]
            inv = lax.rsqrt(jnp.mean(keys * keys, axis=1, keepdims=True) + NORM_EPS)
            lanes = slice(i % per * 128, (i % per + 1) * 128)
            kv_ref[0, i // per, x, z, core, :, lanes] = (keys * inv * gain_ref[...]).astype(BF16)
            kv_ref[1, i // per, x, z, core, :, lanes] = sums[1][:, i * 128 : (i + 1) * 128].astype(BF16)
        tok_ref[...] = jnp.zeros_like(tok_ref)
        pl.semaphore_wait(barrier, n - 1)
        now, later = gathers
        for stage in (now[0], now[1], now[2], later[0], now[3], later[1], now[4], later[2], now[5]):
            stage()

    pad = -rows % 128
    filler = jnp.zeros((pad, 128), BF16)

    def gathered(kv):
        lanes = pl.ds(pl.multiple_of(head % per * 128, 128), 128)
        return kv_ref[kv, head // per, :, :, :, :, lanes].reshape(tokens, 128)

    def keys_of():
        k = gathered(0)
        return k, jnp.concatenate([r_ref[0], filler], axis=0)

    def values_of():
        v = gathered(1)
        return v, jnp.concatenate([r_ref[1], filler], axis=0)

    def two(ref, i):
        return jnp.concatenate(
            [ref[:, i * 128 : (i + 1) * 128], ref[:, (i + 1) * 128 : (i + 2) * 128]], axis=0
        )

    def these(i):
        return slice(i * rows, (i + 2) * rows)

    pairs = range(0, heads, 2)

    @pl.when(second_pass == 0)
    def _():
        (k, rk), (v, rv) = keys_of(), values_of()
        bias = slot_bias(lengths_ref, rows, rows + pad)
        bias = jnp.concatenate([bias, bias], axis=0)

        def logits(i):
            q = two(q_ref, i)
            s = lax.dot_general(q, k, NT, preferred_element_type=F32)
            return s, lax.dot_general(q, rk, NT, preferred_element_type=F32) + bias

        def weigh(i, s, sr):
            peak = jnp.maximum(
                jnp.max(s, axis=1, keepdims=True), jnp.max(sr, axis=1, keepdims=True)
            )
            top = peak * factor
            e = jnp.exp2(s * factor - top)
            er = jnp.exp2(sr * factor - top)
            inv = 1.0 / (
                jnp.sum(e, axis=1, keepdims=True) + jnp.sum(er, axis=1, keepdims=True)
            )
            e_ref[head, part, these(i), :tokens] = e.astype(BF16)
            e_ref[head, part, these(i), tokens:] = er.astype(BF16)
            inv_ref[head, part, these(i)] = inv
            return inv

        def read(i, inv):
            t = two(t_ref, i)
            e = e_ref[head, part, these(i), :tokens]
            er = e_ref[head, part, these(i), tokens:]
            attended = jnp.dot(e, v, preferred_element_type=F32)
            attended = (attended + jnp.dot(er, rv, preferred_element_type=F32)) * inv
            dot = jnp.sum(attended * t.astype(F32), axis=1, keepdims=True)
            dot_ref[head, part, these(i)] = dot
            return dot[:rows] + dot[rows:]

        scores = {i: logits(i) for i in pairs}
        total = jnp.zeros((rows, 1), F32)
        for i in pairs:
            total = total + read(i, weigh(i, *scores[i]))
        tok_ref[...] += total
        keep(at_step).start()

    @pl.when(second_pass == 1)
    def _():
        (k, rk), (v, rv) = keys_of(), values_of()

        def products(i):
            t = two(t_ref, i)
            return (
                lax.dot_general(t, v, NT, preferred_element_type=F32),
                lax.dot_general(t, rv, NT, preferred_element_type=F32),
            )

        def differ(i, dp, dpr):
            dot = dot_ref[head, part, these(i)]
            e = e_ref[head, part, these(i), :tokens]
            er = e_ref[head, part, these(i), tokens:]
            g_ref[0, 0, these(i), :tokens] = (e.astype(F32) * (dp - dot)).astype(BF16)
            g_ref[0, 0, these(i), tokens:] = (er.astype(F32) * (dpr - dot)).astype(BF16)

        def query_grad(i):
            g, gr = g_ref[0, 0, these(i), :tokens], g_ref[0, 0, these(i), tokens:]
            dq = jnp.dot(g, k, preferred_element_type=F32)
            dq = dq + jnp.dot(gr, rk, preferred_element_type=F32)
            dq = dq * (inv_ref[head, part, these(i)] * scale)
            dq_ref[:, i * 128 : (i + 1) * 128] = dq[:rows].astype(BF16)
            dq_ref[:, (i + 1) * 128 : (i + 2) * 128] = dq[rows:].astype(BF16)

        dps = {i: products(i) for i in pairs}
        for i in pairs:
            differ(i, *dps[i])
            query_grad(i)

    def after(step, work):
        pl.when(at_step == step)(work)

    def hidden_columns():
        def go(k, carry):
            spread(k).start()
            return carry

        lax.fori_loop(1, n, go, 0)
        own_copy.start()

    def last():
        for i in range(half):
            keep(i).wait()
        own_copy.wait()

        def done(k, carry):
            spread(k).wait()
            return carry

        lax.fori_loop(1, n, done, 0)
        gather_copies.draining = True
        for gather in gathers:
            for stage in gather:
                stage()

    after(0, gathers[1][3])
    after(1, gathers[1][4])
    after(half // 2 - 1, gathers[1][5])
    after(half // 2, hidden_columns)
    after(2 * half - 1, last)


def forward(
    hidden, kw, vw, gain, q, t, resp, lengths, n, scale, grouped, chunk
):
    rows, depth = q.shape[0], hidden.shape[1]
    prompt_rows, kv_width = hidden.shape[0], kw.shape[1]
    kv_heads = kv_width // 128
    width = n * prompt_rows + rows + -rows % 128
    steps = grouped // chunk
    m = chunk * rows
    tile = 1024
    last = kv_heads * steps - 1
    dma = pltpu.SemaphoreType.DMA
    smem, anywhere = pl.BlockSpec(memory_space=pltpu.SMEM), pl.BlockSpec(memory_space=pl.ANY)

    def whole(*shape):
        return pl.BlockSpec(shape, lambda p, h, c: (0,) * len(shape))

    def step_of(h, c):
        return h * steps + c

    first_only = pl.BlockSpec(
        (rows, chunk * 128), lambda p, h, c: (0, step_of(h, c) * (1 - p) + last * p)
    )
    both = pl.BlockSpec((rows, chunk * 128), lambda p, h, c: (0, step_of(h, c)))
    second_only = pl.BlockSpec((rows, chunk * 128), lambda p, h, c: (0, step_of(h, c) * p))
    return pl.pallas_call(
        functools.partial(forward_kernel, scale),
        grid=(2, kv_heads, steps),
        in_specs=[
            whole(prompt_rows, depth),
            anywhere,
            anywhere,
            whole(1, 128),
            first_only,
            both,
            pl.BlockSpec((2, rows, 128), lambda p, h, c: (0, 0, h)),
            smem,
            anywhere,
        ],
        out_specs=[
            whole(prompt_rows, kv_width),
            anywhere,
            pl.BlockSpec((1, 1, m, width), lambda p, h, c: (h * p, c * p, 0, 0)),
            whole(kv_heads, steps, m, 1),
            second_only,
            whole(rows, 1),
            anywhere,
        ],
        out_shape=[
            jax.ShapeDtypeStruct((prompt_rows, kv_width), F32),
            jax.ShapeDtypeStruct((kv_heads, steps, m, width), BF16),
            jax.ShapeDtypeStruct((kv_heads, steps, m, width), BF16),
            jax.ShapeDtypeStruct((kv_heads, steps, m, 1), F32),
            jax.ShapeDtypeStruct(q.shape, BF16),
            jax.ShapeDtypeStruct((rows, 1), F32),
            jax.ShapeDtypeStruct((n, prompt_rows, WINDOW), BF16),
        ],
        scratch_shapes=[
            pltpu.VMEM((2, depth // tile, tile, kv_width), BF16),
            pltpu.VMEM((2, 2, SIDE, SIDE, 2, prompt_rows, kv_width // 2), BF16),
            pltpu.VMEM((kv_heads, steps, m, width), BF16),
            pltpu.VMEM((kv_heads, steps, m, 1), F32),
            dma((2, depth // tile)),
            dma((2 * GATHER_COPIES,)),
            dma((2 * GATHER_COPIES,)),
            dma,
            dma((n - 1,)),
            dma((n - 1,)),
            dma((kv_heads * steps,)),
        ],
        compiler_params=params(60, collective_id=0, has_side_effects=True),
        name="forward",
    )(hidden, kw, vw, gain, q, t, resp, lengths, hidden)


def norm_backward(raw, gain, grad):
    parts = []
    for h in range(raw.shape[1] // 128):
        keys = raw[:, h * 128 : (h + 1) * 128]
        kg = gain * grad[:, h * 128 : (h + 1) * 128]
        inv = lax.rsqrt(jnp.mean(keys * keys, axis=1, keepdims=True) + NORM_EPS)
        mix = jnp.mean(keys * kg, axis=1, keepdims=True)
        parts.append(inv * kg - keys * (inv * inv * inv) * mix)
    return jnp.concatenate(parts, axis=1)


def total_of(*refs):
    value = refs[0][...].astype(F32)
    for ref in refs[1:]:
        value = value + ref[...].astype(F32)
    return value


REDUCE_COPIES = 68


class Reduce:
    def __init__(self, d_ref, c_ref, a_ref, b_ref, r_ref, s_ref, copies):
        self.d, self.c, self.a, self.b, self.r, self.s = d_ref, c_ref, a_ref, b_ref, r_ref, s_ref
        self.copies = copies
        x, z, self.core = place()
        self.partner = ctx_id(x, z, 1 - self.core)
        rows = a_ref.shape[3]
        self.low, self.high = pl.ds(0, rows // 2), pl.ds(rows // 2, rows // 2)
        self.rings = {}
        for kv in range(2):
            for inner in range(2):
                p, at = ring(1 - kv if inner else kv)
                right, left, opposite = around(p)
                self.rings[kv, inner] = ((opposite, right, left, p), at(right), at(left))

    def place_of(self, kv, i):
        return self.rings[kv, 0][0][i]

    def to_core(self, kv, i):
        self.copies.send(
            self.d.at[kv, i, :, 1 - self.core], self.c.at[kv, i], self.partner, kv * 4 + i
        )

    def landing(self, kv, i, k):
        return self.s.at[kv, k] if i is None else self.b.at[kv, i, k]

    def slot(self, kv, i, k):
        return 56 + kv * 6 + k if i is None else 8 + (kv * 4 + i) * 6 + k

    def unit(self, kv, i, j, part):
        if i is None:
            return self.r.at[kv, j, part]
        return self.a.at[kv, i, self.rings[kv, 1][0][j], part]

    def message(self, kv, i, k, ref):
        _, right, left = self.rings[kv, 0 if i is None else 1]
        peer = right if k in (0, 2, 4) else left
        self.copies.send(ref, self.landing(kv, i, k), peer, self.slot(kv, i, k))

    def landed(self, kv, i, k):
        ref = self.landing(kv, i, k)
        self.copies.arrived(ref, self.slot(kv, i, k))
        return ref

    def opening(self, kv, i, j):
        if j == 0:
            self.message(kv, i, 0, self.unit(kv, i, 0, self.low))
            self.message(kv, i, 1, self.unit(kv, i, 0, self.high))
        if j == 1:
            self.message(kv, i, 2, self.unit(kv, i, 1, self.high))
        if j == 2:
            self.message(kv, i, 3, self.unit(kv, i, 2, self.low))

    def passing(self, kv, i):
        for k, j, part in ((0, 1, self.low), (1, 2, self.high)):
            came = self.landed(kv, i, k)
            mine = self.unit(kv, i, j, part)
            mine[...] = total_of(mine, came).astype(BF16)
            self.message(kv, i, 4 + k, mine)

    def result(self, kv, i):
        lows = total_of(
            self.unit(kv, i, 3, self.low), self.landed(kv, i, 3), self.landed(kv, i, 4)
        )
        highs = total_of(
            self.unit(kv, i, 3, self.high), self.landed(kv, i, 2), self.landed(kv, i, 5)
        )
        return jnp.concatenate([lows, highs], axis=0)

    def start_inner(self, kv, i):
        self.copies.arrived(self.c.at[kv, i], kv * 4 + i)
        self.a[kv, i] = total_of(self.d.at[kv, i, :, self.core], self.c.at[kv, i]).astype(BF16)
        for j in range(3):
            self.opening(kv, i, j)

    def end_inner(self, kv, i):
        self.r[kv, i] = self.result(kv, i).astype(BF16)
        self.opening(kv, None, i)


def share_scores(buf, me, peer, copies, base):
    sent = []
    for k in range(1, 8):
        copies.send(buf.at[me], buf.at[me], peer(k), base + k - 1)
    for k in range(1, 8):
        copies.arrived(buf.at[(me - k + 8) % 8], base + k - 1)
    value = buf[0]
    for i in range(1, 8):
        value = value + buf[i]
    return value


def backward_kernel(
    scale,
    token_ref,
    lengths_ref,
    map_ref,
    ref_ref,
    q_ref,
    t_ref,
    inv_ref,
    dq_ref,
    raw_ref,
    gain_ref,
    e_ref,
    g_ref,
    kw_ref,
    vw_ref,
    hw_ref,
    loss_ref,
    qgrad_ref,
    resp_ref,
    pgrad_ref,
    wgrad_ref,
    one_ref,
    two_ref,
    qs_ref,
    ts_ref,
    gbuf_ref,
    ebuf_ref,
    rbuf_ref,
    d_ref,
    c_ref,
    a_ref,
    b_ref,
    r_ref,
    s_ref,
    gk_ref,
    gv_ref,
    w_ref,
    h_ref,
    paway_ref,
    pcame_ref,
    pown_ref,
    wpart_ref,
    waway_ref,
    wcame_ref,
    load_sem,
    score_send,
    score_recv,
    reduce_send,
    reduce_recv,
    gather_send,
    gather_recv,
    last_send,
    last_recv,
):
    x, z, core = place()
    ctx, tp, dp = lax.axis_index("ctx"), lax.axis_index("tp"), lax.axis_index("dp")
    kv_heads, total, _ = qs_ref.shape
    rows = q_ref.shape[0]
    grouped = total // rows
    tokens = e_ref.shape[2] - rbuf_ref.shape[3]
    chunk = gbuf_ref.shape[3]
    unit = chunk // SIDE

    reduce_copies = Copies(reduce_send, reduce_recv)
    reduce = Reduce(d_ref, c_ref, a_ref, b_ref, r_ref, s_ref, reduce_copies)

    def loads(i):
        buf = i % 2
        start = pl.multiple_of(reduce.place_of(0, i) * chunk, chunk)
        parts = [
            pltpu.make_async_copy(
                g_ref.at[:, :, pl.ds(start, chunk)], gbuf_ref.at[buf], load_sem.at[buf, 0]
            )
        ]
        for j in range(SIDE):
            start = pl.multiple_of(j * chunk + reduce.place_of(1, i) * unit, unit)
            parts.append(
                pltpu.make_async_copy(
                    e_ref.at[:, :, pl.ds(start, unit)],
                    ebuf_ref.at[buf, :, :, pl.ds(j * unit, unit)],
                    load_sem.at[buf, 1 + j],
                )
            )
        return parts

    def start(parts):
        for one in parts:
            one.start()

    def wait(parts):
        for one in parts:
            one.wait()

    tail = pl.ds(tokens, rbuf_ref.shape[3])
    more = [
        pltpu.make_async_copy(g_ref.at[:, :, tail], rbuf_ref.at[0], load_sem.at[2, 0]),
        pltpu.make_async_copy(e_ref.at[:, :, tail], rbuf_ref.at[1], load_sem.at[2, 1]),
    ]
    late = [
        pltpu.make_async_copy(kw_ref, w_ref.at[0], load_sem.at[2, 2]),
        pltpu.make_async_copy(vw_ref, w_ref.at[1], load_sem.at[2, 3]),
        pltpu.make_async_copy(hw_ref, h_ref, load_sem.at[2, 4]),
    ]
    for i in range(2):
        start(loads(i))

    def first(k):
        q = (x * 2 + tp + k) % 8
        return {"ctx": ((q // 2) * SIDE + z) * 2 + core, "tp": q % 2}

    def second(k):
        q = (z * 2 + core + k) % 8
        return {"ctx": x * SIDE * 2 + q}

    other_dp = {"dp": 1 - dp}
    greet([first(k) for k in range(1, 8)] + [second(k) for k in range(1, 8)] + [other_dp])
    score_copies = Copies(score_send, score_recv)
    pick = response_pick(lengths_ref, map_ref, rows, ref_ref.shape[1])
    part = jnp.sum(pick * token_ref[...], axis=0, keepdims=True)
    one_ref[x * 2 + tp] = jnp.broadcast_to(part, one_ref.shape[1:])
    half_sum = share_scores(one_ref, x * 2 + tp, first, score_copies, 0)
    two_ref[z * 2 + core] = half_sum
    scores = share_scores(two_ref, z * 2 + core, second, score_copies, 7)[:1]
    pairs = scores.shape[1] // 2
    shifted = scores - ref_ref[...]
    margin = DPO_BETA * (shifted[:, :pairs] - shifted[:, pairs:])
    small = jnp.exp(-jnp.abs(margin))
    pair_grad = -DPO_BETA * jnp.where(margin >= 0.0, small, 1.0) / (1.0 + small)
    score_grad = jnp.concatenate([pair_grad, -pair_grad], axis=1)
    row_grad = jnp.sum(pick * score_grad, axis=1, keepdims=True)
    row_factor = jnp.concatenate([row_grad] * grouped, axis=0)
    start(more)
    for h in range(kv_heads):
        factor = inv_ref[h] * row_factor
        base = h * grouped * 128
        pieces = [q_ref[:, base + i * 128 : base + (i + 1) * 128] for i in range(grouped)]
        q = jnp.concatenate(pieces, axis=0).astype(F32)
        qs_ref[h] = (q * (factor * scale)).astype(BF16)
        pieces = [t_ref[:, base + i * 128 : base + (i + 1) * 128] for i in range(grouped)]
        t = jnp.concatenate(pieces, axis=0).astype(F32)
        ts_ref[h] = (t * factor).astype(BF16)

    def chunk_grads(i):
        buf = i % 2
        for kv, (kept, scaled) in enumerate(((gbuf_ref, qs_ref), (ebuf_ref, ts_ref))):
            for h in range(kv_heads):
                grads = lax.dot_general(kept[buf, h], scaled[h], TN, preferred_element_type=F32)
                grads = grads.astype(BF16).reshape(SIDE, 2, unit // 2, 128)
                d_ref[kv, i, :, :, :, h * 128 : (h + 1) * 128] = grads
            reduce.to_core(kv, i)

    for i in range(SIDE):
        wait(loads(i))
        chunk_grads(i)
        if i + 2 < SIDE:
            start(loads(i + 2))
        if i == SIDE - 2:
            start(late)
        if i >= 1:
            for kv in range(2):
                reduce.start_inner(kv, i - 1)
        if i >= 2:
            for kv in range(2):
                reduce.passing(kv, i - 2)
        if i >= 3:
            for kv in range(2):
                reduce.end_inner(kv, i - 3)
    for kv in range(2):
        reduce.start_inner(kv, 3)
    for kv in range(2):
        reduce.passing(kv, 2)
    for kv in range(2):
        reduce.end_inner(kv, 1)
    for kv in range(2):
        reduce.passing(kv, 3)
    wait(more)
    for kv, scaled in enumerate((qs_ref, ts_ref)):
        for h in range(kv_heads):
            grads = lax.dot_general(rbuf_ref[kv, h], scaled[h], TN, preferred_element_type=F32)
            resp_ref[kv, :, h * 128 : (h + 1) * 128] = grads[:rows].astype(BF16)
    loss = jnp.maximum(-margin, 0.0) + jnp.log1p(small)
    loss_ref[...] = jnp.sum(loss, axis=1, keepdims=True)
    qgrad_ref[...] = (dq_ref[...].astype(F32) * row_grad).astype(BF16)
    for kv in range(2):
        reduce.end_inner(kv, 2)
    for kv in range(2):
        reduce.passing(kv, None)
    for kv in range(2):
        reduce.end_inner(kv, 3)
    key_sum = reduce.result(0, None)
    gk_ref[0, x, z, core] = norm_backward(raw_ref[...], gain_ref[...], key_sum).astype(BF16)
    gv_ref[0, x, z, core] = reduce.result(1, None).astype(BF16)

    gather_copies = Copies(gather_send, gather_recv)
    stages = gather_stages(
        lambda kv: (gk_ref, gv_ref)[kv], raw_ref.shape[0], gather_copies, 0
    )
    last_copies = Copies(last_send, last_recv)
    stages[0]()
    wait(late)
    tile = 512
    half = paway_ref.shape[1]

    def input_grad(side, store):
        key_grad, value_grad = gk_ref[0, x, z, core], gv_ref[0, x, z, core]

        def step(i, carry):
            here = pl.ds(pl.multiple_of(side * half + i * tile, tile), tile)
            value = lax.dot_general(key_grad, w_ref[0, here], NT, preferred_element_type=F32)
            value += lax.dot_general(value_grad, w_ref[1, here], NT, preferred_element_type=F32)
            store(pl.ds(pl.multiple_of(i * tile, tile), tile), value)
            return carry

        lax.fori_loop(0, half // tile, step, 0)

    def store_away(here, value):
        paway_ref[:, here] = value.astype(BF16)

    def store_own(here, value):
        pown_ref[:, here] = value

    input_grad(1 - tp, store_away)
    last_copies.send(paway_ref, pcame_ref, {"tp": 1 - tp}, 0)
    stages[1]()
    stages[2]()
    input_grad(tp, store_own)
    stages[3]()
    stages[4]()
    last_copies.arrived(pcame_ref, 0)
    pgrad_ref[...] = (pown_ref[...] + pcame_ref[...].astype(F32)).astype(BF16)

    out_rows = wgrad_ref.shape[0]
    shift = (ctx % 4) * 32
    hidden = h_ref[...].reshape(-1, h_ref.shape[2])
    stages[5]()
    for kv, ref in enumerate((gk_ref, gv_ref)):
        grads = ref[...].reshape(-1, ref.shape[5])
        wpart_ref[kv] = lax.dot_general(hidden, grads, TN, preferred_element_type=F32)
        away = pl.ds(pl.multiple_of(shift + (1 - dp) * out_rows, 16), out_rows)
        waway_ref[kv] = wpart_ref[kv, away].astype(BF16)
        last_copies.send(waway_ref.at[kv], wcame_ref.at[kv], other_dp, 1 + kv)
    for copies in (score_copies, reduce_copies, gather_copies):
        copies.finish()
    own = pl.ds(pl.multiple_of(shift + dp * out_rows, 16), out_rows)
    for kv in range(2):
        last_copies.arrived(wcame_ref.at[kv], 1 + kv)
        wgrad_ref[:, kv] = wpart_ref[kv, own] + wcame_ref[kv].astype(F32)
    last_copies.finish()


def backward(
    token_part,
    lengths,
    places,
    ref_scores,
    q,
    t,
    inv,
    dq,
    raw_keys,
    gain,
    e,
    g,
    kw,
    vw,
    windows,
    scale,
    out_rows,
):
    rows, responses = q.shape[0], ref_scores.shape[1]
    kv_heads, total, width = e.shape
    prompt_rows, kv_width = raw_keys.shape
    depth = kw.shape[0]
    n = windows.shape[0]
    tokens = n * prompt_rows
    pad = width - tokens
    chunk = tokens // SIDE
    half = depth // 2
    vmem, anywhere = pl.BlockSpec(memory_space=pltpu.VMEM), pl.BlockSpec(memory_space=pl.ANY)
    smem = pl.BlockSpec(memory_space=pltpu.SMEM)
    dma = pltpu.SemaphoreType.DMA
    small = (prompt_rows // 2, kv_width)
    return pl.pallas_call(
        functools.partial(backward_kernel, scale),
        out_shape=[
            jax.ShapeDtypeStruct((1, 1), F32),
            jax.ShapeDtypeStruct(q.shape, BF16),
            jax.ShapeDtypeStruct((2, rows, kv_width), BF16),
            jax.ShapeDtypeStruct((prompt_rows, half), BF16),
            jax.ShapeDtypeStruct((out_rows, 2, kv_width), F32),
        ],
        in_specs=[vmem, smem, smem] + [vmem] * 7 + [anywhere] * 5,
        out_specs=[vmem] * 5,
        scratch_shapes=[
            pltpu.VMEM((8, 8, responses), F32),
            pltpu.VMEM((8, 8, responses), F32),
            pltpu.VMEM((kv_heads, total, 128), BF16),
            pltpu.VMEM((kv_heads, total, 128), BF16),
            pltpu.VMEM((2, kv_heads, total, chunk), BF16),
            pltpu.VMEM((2, kv_heads, total, chunk), BF16),
            pltpu.VMEM((2, kv_heads, total, pad), BF16),
            pltpu.VMEM((2, SIDE, SIDE, 2, prompt_rows, kv_width), BF16),
            pltpu.VMEM((2, SIDE, SIDE, prompt_rows, kv_width), BF16),
            pltpu.VMEM((2, SIDE, SIDE, prompt_rows, kv_width), BF16),
            pltpu.VMEM((2, SIDE, 6) + small, BF16),
            pltpu.VMEM((2, SIDE, prompt_rows, kv_width), BF16),
            pltpu.VMEM((2, 6) + small, BF16),
            pltpu.VMEM((1, SIDE, SIDE, 2, prompt_rows, kv_width), BF16),
            pltpu.VMEM((1, SIDE, SIDE, 2, prompt_rows, kv_width), BF16),
            pltpu.VMEM((2, depth, kv_width), BF16),
            pltpu.VMEM(windows.shape, BF16),
            pltpu.VMEM((prompt_rows, half), BF16),
            pltpu.VMEM((prompt_rows, half), BF16),
            pltpu.VMEM((prompt_rows, half), F32),
            pltpu.VMEM((2, WINDOW, kv_width), F32),
            pltpu.VMEM((2, out_rows, kv_width), BF16),
            pltpu.VMEM((2, out_rows, kv_width), BF16),
            dma((3, 5)),
            dma((14,)),
            dma((14,)),
            dma((REDUCE_COPIES,)),
            dma((REDUCE_COPIES,)),
            dma((GATHER_COPIES,)),
            dma((GATHER_COPIES,)),
            dma((3,)),
            dma((3,)),
        ],
        compiler_params=params(60, collective_id=1, has_side_effects=True),
        name="backward",
    )(
        token_part,
        lengths,
        places,
        ref_scores,
        q,
        t,
        inv,
        dq,
        raw_keys,
        gain,
        e,
        g,
        kw,
        vw,
        windows,
    )


def finish_kernel(*refs):
    count = len(refs) // 2
    copies = [
        pltpu.make_async_copy(refs[i], refs[count + i], refs[-1].at[i]) for i in range(count)
    ]
    for one in copies:
        one.start()
    for one in copies:
        one.wait()


def finish(*arrays):
    anywhere = pl.BlockSpec(memory_space=pl.ANY)
    return pl.pallas_call(
        finish_kernel,
        out_shape=[jax.ShapeDtypeStruct(a.shape, a.dtype) for a in arrays],
        in_specs=[anywhere] * len(arrays),
        out_specs=[anywhere] * len(arrays),
        scratch_shapes=[pltpu.SemaphoreType.DMA((len(arrays),))],
        compiler_params=params(16),
        name="finish",
    )(*arrays)


def shards(
    prompt_hidden,
    key_weight,
    value_weight,
    key_gain,
    queries,
    response_kv,
    targets,
    ref_scores,
    lengths,
    placement_map,
):
    hidden = prompt_hidden[0]
    model_width = hidden.shape[1]
    head_width = key_gain.shape[0]
    kv_width = key_weight.shape[1]
    grouped = queries.shape[2] // kv_width
    n_ctx = lax.axis_size("ctx")
    qk_scale = 1.0 / math.sqrt(head_width)
    gain = key_gain[None]
    q, t = queries[0], targets[0]
    raw_keys, e, g, inv, dq, token_part, windows = forward(
        hidden,
        key_weight,
        value_weight,
        gain,
        q,
        t,
        response_kv[0].transpose(1, 0, 2),
        lengths[0, 0],
        n_ctx,
        qk_scale,
        grouped,
        4,
    )

    def joined(value):
        return value.reshape(value.shape[0], -1, value.shape[3])

    dpo_loss, query_grad, resp_grad, prompt_grad, weight_grad = backward(
        token_part,
        lengths[0, 0],
        placement_map[0],
        ref_scores,
        q,
        t,
        joined(inv),
        dq,
        raw_keys,
        gain,
        joined(e),
        joined(g),
        key_weight,
        value_weight,
        windows,
        qk_scale,
        model_width // n_ctx // 2,
    )
    query_grad, prompt_grad, weight_grad = finish(query_grad, prompt_grad, weight_grad)
    return (
        dpo_loss.reshape(1),
        query_grad[None],
        resp_grad.transpose(1, 0, 2)[None],
        prompt_grad[None],
        weight_grad,
    )


def solution(mesh):
    in_specs = (
        P("dp", "ctx", None),
        P(None, "tp"),
        P(None, "tp"),
        P(),
        P("dp", "ctx", "tp"),
        P("dp", "ctx", None, "tp"),
        P("dp", "ctx", "tp"),
        P("dp", None),
        P("dp", "ctx", None),
        P("dp", "ctx"),
    )
    out_specs = (
        P("dp"),
        P("dp", "ctx", "tp"),
        P("dp", "ctx", None, "tp"),
        P("dp", "ctx", "tp"),
        P(("ctx", "dp"), None, "tp"),
    )
    return jax.shard_map(shards, mesh=mesh, in_specs=in_specs, out_specs=out_specs, check_vma=False)
```

```python
import functools
import math

import jax
import jax.numpy as jnp
from jax import lax
from jax.experimental import pallas as pl
from jax.experimental.pallas import tpu as pltpu
from jax.sharding import PartitionSpec as P

NORM_EPS = 1e-06
DPO_BETA = 0.5
MASK_FILL = -1e30
LOG2E = 1.4426950408889634
NT = (((1,), (1,)), ((), ()))
TN = (((0,), (0,)), ((), ()))
F32 = jnp.float32
BF16 = jnp.bfloat16


MESH = pl.DeviceIdType.MESH
SIDE = 4


def params(limit_mib, **more):
    return pltpu.CompilerParams(vmem_limit_bytes=limit_mib * 1024 * 1024, **more)


def place():
    me = lax.axis_index("ctx")
    return me // (2 * SIDE), (me // 2) % SIDE, me % 2


def ctx_id(x, z, core):
    return {"ctx": (x * SIDE + z) * 2 + core}


def greet(peers):
    barrier = pltpu.get_barrier_semaphore()
    for peer in peers:
        pl.semaphore_signal(barrier, inc=1, device_id=peer, device_id_type=MESH)
    pl.semaphore_wait(barrier, len(peers))


def plane_peers():
    x, z, core = place()
    return [
        ctx_id((x + 1) % SIDE, z, core),
        ctx_id((x + SIDE - 1) % SIDE, z, core),
        ctx_id(x, (z + 1) % SIDE, core),
        ctx_id(x, (z + SIDE - 1) % SIDE, core),
        ctx_id(x, z, 1 - core),
    ]


def ring(axis):
    x, z, core = place()
    if axis == 0:
        return x, lambda p: ctx_id(p, z, core)
    return z, lambda p: ctx_id(x, p, core)


def around(p):
    return (p + 1) % SIDE, (p + SIDE - 1) % SIDE, (p + 2) % SIDE


class Copies:
    def __init__(self, send_sem, recv_sem):
        self.send_sem, self.recv_sem, self.started = send_sem, recv_sem, []
        self.draining = False

    def make(self, src, dst, peer, slot):
        return pltpu.make_async_remote_copy(
            src_ref=src,
            dst_ref=dst,
            send_sem=self.send_sem.at[slot],
            recv_sem=self.recv_sem.at[slot],
            device_id=peer,
            device_id_type=MESH,
        )

    def send(self, src, dst, peer, slot):
        one = self.make(src, dst, peer, slot)
        if self.draining:
            one.wait_send()
            return
        one.start()
        self.started.append(one)

    def arrived(self, dst, slot):
        if self.draining:
            return
        x, z, core = place()
        self.make(dst, dst, ctx_id(x, z, 1 - core), slot).wait_recv()

    def finish(self):
        for one in self.started:
            one.wait_send()


GATHER_COPIES = 24


def gather_stages(ref_of, rows, copies, base):
    x, z, core = place()
    partner = ctx_id(x, z, 1 - core)
    full, low, high = pl.ds(0, rows), pl.ds(0, rows // 2), pl.ds(rows // 2, rows // 2)
    rings = {}
    for kv in range(2):
        for phase in range(2):
            p, at = ring(kv if phase == 0 else 1 - kv)
            right, left, opposite = around(p)
            rings[kv, phase] = ((p, left, right, opposite), at(right), at(left))

    def block(kv, phase, i, part=full, of_core=core):
        p = rings[kv, phase][0][i]
        if phase == 1:
            x_at, z_at = (slice(None), p) if kv == 0 else (p, slice(None))
        else:
            x_at, z_at = (p, z) if kv == 0 else (x, p)
        return ref_of(kv).at[:, x_at, z_at, of_core, part]

    def slot(kv, phase, k):
        return base + (kv * 2 + phase) * 4 + k

    def send(ref, peer, at):
        copies.send(ref, ref, peer, at)

    def to_core(kv, i):
        send(block(kv, 1, i), partner, base + 16 + kv * 4 + i)

    def start(phase):
        for kv in range(2):
            _, right, left = rings[kv, phase]
            send(block(kv, phase, 0), right, slot(kv, phase, 0))
            send(block(kv, phase, 0), left, slot(kv, phase, 1))
        if phase == 1:
            for kv in range(2):
                to_core(kv, 0)

    def forward(phase):
        for kv in range(2):
            _, right, left = rings[kv, phase]
            copies.arrived(block(kv, phase, 1), slot(kv, phase, 0))
            send(block(kv, phase, 1, low), right, slot(kv, phase, 2))
            copies.arrived(block(kv, phase, 2), slot(kv, phase, 1))
            send(block(kv, phase, 2, high), left, slot(kv, phase, 3))
        if phase == 1:
            for kv in range(2):
                to_core(kv, 1)
                to_core(kv, 2)

    def close(phase):
        for kv in range(2):
            copies.arrived(block(kv, phase, 3, low), slot(kv, phase, 2))
            copies.arrived(block(kv, phase, 3, high), slot(kv, phase, 3))
            if phase == 1:
                to_core(kv, 3)

    def turn():
        close(0)
        start(1)

    def from_core():
        for kv in range(2):
            for i in range(4):
                copies.arrived(block(kv, 1, i, full, 1 - core), base + 16 + kv * 4 + i)

    return [
        lambda: start(0),
        lambda: forward(0),
        turn,
        lambda: forward(1),
        lambda: close(1),
        from_core,
    ]


def slots_of(lengths_ref, ids):
    slots, end = jnp.zeros(ids.shape, jnp.int32), 0
    for i in range(lengths_ref.shape[0]):
        end = end + lengths_ref[i]
        slots = slots + jnp.where(ids >= end, 1, 0)
    return slots


def slot_bias(lengths_ref, rows, pad):
    row = lax.broadcasted_iota(jnp.int32, (rows, pad), 0)
    key = lax.broadcasted_iota(jnp.int32, (rows, pad), 1)
    seen = (slots_of(lengths_ref, row) == slots_of(lengths_ref, key)) & (key <= row)
    return jnp.where(seen, 0.0, MASK_FILL)


def response_pick(lengths_ref, map_ref, rows, responses):
    slots = slots_of(lengths_ref, lax.broadcasted_iota(jnp.int32, (rows, responses), 0))
    ids = jnp.zeros((rows, responses), jnp.int32)
    for i in range(map_ref.shape[0]):
        ids = jnp.where(slots == i, map_ref[i], ids)
    return jnp.where(ids == lax.broadcasted_iota(jnp.int32, (rows, responses), 1), 1.0, 0.0)


WINDOW = 256


def forward_kernel(
    scale,
    hidden_ref,
    kw_ref,
    vw_ref,
    gain_ref,
    q_ref,
    t_ref,
    r_ref,
    lengths_ref,
    h_ref,
    raw_ref,
    e_ref,
    g_ref,
    inv_ref,
    dq_ref,
    tok_ref,
    o_ref,
    w_ref,
    kv_ref,
    load_sem,
    gather_send,
    gather_recv,
    own_sem,
    spread_send,
    spread_recv,
):
    x, z, core = place()
    me = lax.axis_index("ctx")
    n = o_ref.shape[0]
    head, part = pl.program_id(0), pl.program_id(1)
    kv_heads, steps = inv_ref.shape[:2]
    at_step = head * steps + part
    half = kv_heads * steps // 2
    rows, heads = q_ref.shape[0], q_ref.shape[1] // 128
    prompt_rows = raw_ref.shape[0]
    tokens = n * prompt_rows
    factor = scale * LOG2E

    def load(kv, i):
        tile = w_ref.shape[2]
        src = (kw_ref, vw_ref)[kv].at[pl.ds(i * tile, tile)]
        return pltpu.make_async_copy(src, w_ref.at[kv, i], load_sem.at[kv, i])

    gather_copies = Copies(gather_send, gather_recv)
    per = kv_heads // 2
    gathers = [
        gather_stages(
            lambda kv, i=i: kv_ref.at[kv, pl.ds(i, 1)],
            prompt_rows,
            gather_copies,
            i * GATHER_COPIES,
        )
        for i in range(2)
    ]

    def window(peer):
        tile = 5 * (peer // 4) + peer % 4
        return h_ref.at[:, pl.ds(pl.multiple_of(tile * 128, 128), WINDOW)]

    def spread(k):
        peer = (me + k) % n
        return pltpu.make_async_remote_copy(
            src_ref=window(peer),
            dst_ref=o_ref.at[me],
            send_sem=spread_send.at[k - 1],
            recv_sem=spread_recv.at[k - 1],
            device_id={"ctx": peer},
            device_id_type=MESH,
        )

    own_copy = pltpu.make_async_copy(window(me), o_ref.at[me], own_sem)

    @pl.when(at_step == 0)
    def _():
        for i in range(w_ref.shape[1]):
            for kv in range(2):
                load(kv, i).start()
        barrier = pltpu.get_barrier_semaphore()

        def hello(k, carry):
            pl.semaphore_signal(
                barrier, inc=1, device_id={"ctx": (me + k) % n}, device_id_type=MESH
            )
            return carry

        lax.fori_loop(1, n, hello, 0)
        tile, width = w_ref.shape[2:]
        sums = [jnp.zeros((prompt_rows, width), F32)] * 2
        for i in range(w_ref.shape[1]):
            piece = hidden_ref[:, i * tile : (i + 1) * tile]
            for kv in range(2):
                load(kv, i).wait()
                sums[kv] = sums[kv] + jnp.dot(piece, w_ref[kv, i], preferred_element_type=F32)
        raw_ref[...] = sums[0]
        for i in range(kv_heads):
            keys = sums[0][:, i * 128 : (i + 1) * 128]
            inv = lax.rsqrt(jnp.mean(keys * keys, axis=1, keepdims=True) + NORM_EPS)
            lanes = slice(i % per * 128, (i % per + 1) * 128)
            kv_ref[0, i // per, x, z, core, :, lanes] = (keys * inv * gain_ref[...]).astype(BF16)
            kv_ref[1, i // per, x, z, core, :, lanes] = sums[1][:, i * 128 : (i + 1) * 128].astype(BF16)
        tok_ref[...] = jnp.zeros_like(tok_ref)
        pl.semaphore_wait(barrier, n - 1)
        now, later = gathers
        for stage in (now[0], now[1], now[2], later[0], now[3], later[1], now[4], later[2], now[5]):
            stage()

    pad = -rows % 128
    filler = jnp.zeros((pad, 128), BF16)

    def gathered(kv):
        lanes = pl.ds(pl.multiple_of(head % per * 128, 128), 128)
        return kv_ref[kv, head // per, :, :, :, :, lanes].reshape(tokens, 128)

    def keys_of():
        k = gathered(0)
        return k, jnp.concatenate([r_ref[0], filler], axis=0)

    def values_of():
        v = gathered(1)
        return v, jnp.concatenate([r_ref[1], filler], axis=0)

    def two(ref, i):
        return jnp.concatenate(
            [ref[:, i * 128 : (i + 1) * 128], ref[:, (i + 1) * 128 : (i + 2) * 128]], axis=0
        )

    def these(i):
        return slice(i * rows, (i + 2) * rows)

    pairs = range(0, heads, 2)
    (k, rk), (v, rv) = keys_of(), values_of()
    bias = slot_bias(lengths_ref, rows, rows + pad)
    bias = jnp.concatenate([bias, bias], axis=0)

    def logits(i):
        q = two(q_ref, i)
        s = lax.dot_general(q, k, NT, preferred_element_type=F32)
        return s, lax.dot_general(q, rk, NT, preferred_element_type=F32) + bias

    def weigh(i, s, sr):
        peak = jnp.maximum(
            jnp.max(s, axis=1, keepdims=True), jnp.max(sr, axis=1, keepdims=True)
        )
        top = peak * factor
        e = jnp.exp2(s * factor - top)
        er = jnp.exp2(sr * factor - top)
        inv = 1.0 / (jnp.sum(e, axis=1, keepdims=True) + jnp.sum(er, axis=1, keepdims=True))
        e_ref[0, 0, these(i), :tokens] = e.astype(BF16)
        e_ref[0, 0, these(i), tokens:] = er.astype(BF16)
        inv_ref[head, part, these(i)] = inv
        return inv

    def read(i, inv):
        t = two(t_ref, i)
        e, er = e_ref[0, 0, these(i), :tokens], e_ref[0, 0, these(i), tokens:]
        dp = lax.dot_general(t, v, NT, preferred_element_type=F32)
        dpr = lax.dot_general(t, rv, NT, preferred_element_type=F32)
        attended = jnp.dot(e, v, preferred_element_type=F32)
        attended = (attended + jnp.dot(er, rv, preferred_element_type=F32)) * inv
        dot = jnp.sum(attended * t.astype(F32), axis=1, keepdims=True)
        return dp, dpr, dot

    def differ(i, dp, dpr, dot):
        e, er = e_ref[0, 0, these(i), :tokens], e_ref[0, 0, these(i), tokens:]
        g_ref[0, 0, these(i), :tokens] = (e.astype(F32) * (dp - dot)).astype(BF16)
        g_ref[0, 0, these(i), tokens:] = (er.astype(F32) * (dpr - dot)).astype(BF16)

    def query_grad(i, inv):
        g, gr = g_ref[0, 0, these(i), :tokens], g_ref[0, 0, these(i), tokens:]
        dq = jnp.dot(g, k, preferred_element_type=F32)
        dq = (dq + jnp.dot(gr, rk, preferred_element_type=F32)) * (inv * scale)
        dq_ref[:, i * 128 : (i + 1) * 128] = dq[:rows].astype(BF16)
        dq_ref[:, (i + 1) * 128 : (i + 2) * 128] = dq[rows:].astype(BF16)

    scores = {i: logits(i) for i in pairs}
    invs, reads, total = {}, {}, jnp.zeros((rows, 1), F32)
    for i in pairs:
        invs[i] = weigh(i, *scores[i])
        reads[i] = read(i, invs[i])
        if i >= 2:
            differ(i - 2, *reads[i - 2])
            query_grad(i - 2, invs[i - 2])
    final = heads - 2
    differ(final, *reads[final])
    query_grad(final, invs[final])
    for i in pairs:
        dot = reads[i][2]
        total = total + dot[:rows] + dot[rows:]
    tok_ref[...] += total

    def after(step, work):
        pl.when(at_step == step)(work)

    def hidden_columns():
        def go(k, carry):
            spread(k).start()
            return carry

        lax.fori_loop(1, n, go, 0)
        own_copy.start()

    def last():
        own_copy.wait()

        def done(k, carry):
            spread(k).wait()
            return carry

        lax.fori_loop(1, n, done, 0)
        gather_copies.draining = True
        for gather in gathers:
            for stage in gather:
                stage()

    after(0, gathers[1][3])
    after(1, gathers[1][4])
    after(half - 2, gathers[1][5])
    after(half - 1, hidden_columns)
    after(2 * half - 1, last)


def forward(
    hidden, kw, vw, gain, q, t, resp, lengths, n, scale, grouped, chunk
):
    rows, depth = q.shape[0], hidden.shape[1]
    prompt_rows, kv_width = hidden.shape[0], kw.shape[1]
    kv_heads = kv_width // 128
    width = n * prompt_rows + rows + -rows % 128
    steps = grouped // chunk
    m = chunk * rows
    tile = 1024
    dma = pltpu.SemaphoreType.DMA
    smem, anywhere = pl.BlockSpec(memory_space=pltpu.SMEM), pl.BlockSpec(memory_space=pl.ANY)

    def whole(*shape):
        return pl.BlockSpec(shape, lambda h, c: (0,) * len(shape))

    row_block = pl.BlockSpec((rows, chunk * 128), lambda h, c: (0, h * steps + c))
    kept_block = pl.BlockSpec((1, 1, m, width), lambda h, c: (h, c, 0, 0))
    return pl.pallas_call(
        functools.partial(forward_kernel, scale),
        grid=(kv_heads, steps),
        in_specs=[
            whole(prompt_rows, depth),
            anywhere,
            anywhere,
            whole(1, 128),
            row_block,
            row_block,
            pl.BlockSpec((2, rows, 128), lambda h, c: (0, 0, h)),
            smem,
            anywhere,
        ],
        out_specs=[
            whole(prompt_rows, kv_width),
            kept_block,
            kept_block,
            whole(kv_heads, steps, m, 1),
            row_block,
            whole(rows, 1),
            anywhere,
        ],
        out_shape=[
            jax.ShapeDtypeStruct((prompt_rows, kv_width), F32),
            jax.ShapeDtypeStruct((kv_heads, steps, m, width), BF16),
            jax.ShapeDtypeStruct((kv_heads, steps, m, width), BF16),
            jax.ShapeDtypeStruct((kv_heads, steps, m, 1), F32),
            jax.ShapeDtypeStruct(q.shape, BF16),
            jax.ShapeDtypeStruct((rows, 1), F32),
            jax.ShapeDtypeStruct((n, prompt_rows, WINDOW), BF16),
        ],
        scratch_shapes=[
            pltpu.VMEM((2, depth // tile, tile, kv_width), BF16),
            pltpu.VMEM((2, 2, SIDE, SIDE, 2, prompt_rows, kv_width // 2), BF16),
            dma((2, depth // tile)),
            dma((2 * GATHER_COPIES,)),
            dma((2 * GATHER_COPIES,)),
            dma,
            dma((n - 1,)),
            dma((n - 1,)),
        ],
        compiler_params=params(60, collective_id=0, has_side_effects=True),
        name="forward",
    )(hidden, kw, vw, gain, q, t, resp, lengths, hidden)


def norm_backward(raw, gain, grad):
    parts = []
    for h in range(raw.shape[1] // 128):
        keys = raw[:, h * 128 : (h + 1) * 128]
        kg = gain * grad[:, h * 128 : (h + 1) * 128]
        inv = lax.rsqrt(jnp.mean(keys * keys, axis=1, keepdims=True) + NORM_EPS)
        mix = jnp.mean(keys * kg, axis=1, keepdims=True)
        parts.append(inv * kg - keys * (inv * inv * inv) * mix)
    return jnp.concatenate(parts, axis=1)


def total_of(*refs):
    value = refs[0][...].astype(F32)
    for ref in refs[1:]:
        value = value + ref[...].astype(F32)
    return value


REDUCE_COPIES = 68


class Reduce:
    def __init__(self, d_ref, c_ref, a_ref, b_ref, r_ref, s_ref, copies):
        self.d, self.c, self.a, self.b, self.r, self.s = d_ref, c_ref, a_ref, b_ref, r_ref, s_ref
        self.copies = copies
        x, z, self.core = place()
        self.partner = ctx_id(x, z, 1 - self.core)
        rows = a_ref.shape[3]
        self.low, self.high = pl.ds(0, rows // 2), pl.ds(rows // 2, rows // 2)
        self.rings = {}
        for kv in range(2):
            for inner in range(2):
                p, at = ring(1 - kv if inner else kv)
                right, left, opposite = around(p)
                self.rings[kv, inner] = ((opposite, right, left, p), at(right), at(left))

    def place_of(self, kv, i):
        return self.rings[kv, 0][0][i]

    def to_core(self, kv, i):
        self.copies.send(
            self.d.at[kv, i, :, 1 - self.core], self.c.at[kv, i], self.partner, kv * 4 + i
        )

    def landing(self, kv, i, k):
        return self.s.at[kv, k] if i is None else self.b.at[kv, i, k]

    def slot(self, kv, i, k):
        return 56 + kv * 6 + k if i is None else 8 + (kv * 4 + i) * 6 + k

    def unit(self, kv, i, j, part):
        if i is None:
            return self.r.at[kv, j, part]
        return self.a.at[kv, i, self.rings[kv, 1][0][j], part]

    def message(self, kv, i, k, ref):
        _, right, left = self.rings[kv, 0 if i is None else 1]
        peer = right if k in (0, 2, 4) else left
        self.copies.send(ref, self.landing(kv, i, k), peer, self.slot(kv, i, k))

    def landed(self, kv, i, k):
        ref = self.landing(kv, i, k)
        self.copies.arrived(ref, self.slot(kv, i, k))
        return ref

    def opening(self, kv, i, j):
        if j == 0:
            self.message(kv, i, 0, self.unit(kv, i, 0, self.low))
            self.message(kv, i, 1, self.unit(kv, i, 0, self.high))
        if j == 1:
            self.message(kv, i, 2, self.unit(kv, i, 1, self.high))
        if j == 2:
            self.message(kv, i, 3, self.unit(kv, i, 2, self.low))

    def passing(self, kv, i):
        for k, j, part in ((0, 1, self.low), (1, 2, self.high)):
            came = self.landed(kv, i, k)
            mine = self.unit(kv, i, j, part)
            mine[...] = total_of(mine, came).astype(BF16)
            self.message(kv, i, 4 + k, mine)

    def result(self, kv, i):
        lows = total_of(
            self.unit(kv, i, 3, self.low), self.landed(kv, i, 3), self.landed(kv, i, 4)
        )
        highs = total_of(
            self.unit(kv, i, 3, self.high), self.landed(kv, i, 2), self.landed(kv, i, 5)
        )
        return jnp.concatenate([lows, highs], axis=0)

    def start_inner(self, kv, i):
        self.copies.arrived(self.c.at[kv, i], kv * 4 + i)
        self.a[kv, i] = total_of(self.d.at[kv, i, :, self.core], self.c.at[kv, i]).astype(BF16)
        for j in range(3):
            self.opening(kv, i, j)

    def end_inner(self, kv, i):
        self.r[kv, i] = self.result(kv, i).astype(BF16)
        self.opening(kv, None, i)


def share_scores(buf, me, peer, copies, base):
    sent = []
    for k in range(1, 8):
        copies.send(buf.at[me], buf.at[me], peer(k), base + k - 1)
    for k in range(1, 8):
        copies.arrived(buf.at[(me - k + 8) % 8], base + k - 1)
    value = buf[0]
    for i in range(1, 8):
        value = value + buf[i]
    return value


def backward_kernel(
    scale,
    token_ref,
    lengths_ref,
    map_ref,
    ref_ref,
    q_ref,
    t_ref,
    inv_ref,
    dq_ref,
    raw_ref,
    gain_ref,
    e_ref,
    g_ref,
    kw_ref,
    vw_ref,
    hw_ref,
    loss_ref,
    qgrad_ref,
    resp_ref,
    pgrad_ref,
    wgrad_ref,
    one_ref,
    two_ref,
    qs_ref,
    ts_ref,
    gbuf_ref,
    ebuf_ref,
    rbuf_ref,
    d_ref,
    c_ref,
    a_ref,
    b_ref,
    r_ref,
    s_ref,
    gk_ref,
    gv_ref,
    w_ref,
    h_ref,
    paway_ref,
    pcame_ref,
    pown_ref,
    wpart_ref,
    waway_ref,
    wcame_ref,
    load_sem,
    score_send,
    score_recv,
    reduce_send,
    reduce_recv,
    gather_send,
    gather_recv,
    last_send,
    last_recv,
):
    x, z, core = place()
    ctx, tp, dp = lax.axis_index("ctx"), lax.axis_index("tp"), lax.axis_index("dp")
    kv_heads, total, _ = qs_ref.shape
    rows = q_ref.shape[0]
    grouped = total // rows
    tokens = e_ref.shape[2] - rbuf_ref.shape[3]
    chunk = gbuf_ref.shape[3]
    unit = chunk // SIDE

    reduce_copies = Copies(reduce_send, reduce_recv)
    reduce = Reduce(d_ref, c_ref, a_ref, b_ref, r_ref, s_ref, reduce_copies)

    def loads(i):
        buf = i % 2
        start = pl.multiple_of(reduce.place_of(0, i) * chunk, chunk)
        parts = [
            pltpu.make_async_copy(
                g_ref.at[:, :, pl.ds(start, chunk)], gbuf_ref.at[buf], load_sem.at[buf, 0]
            )
        ]
        for j in range(SIDE):
            start = pl.multiple_of(j * chunk + reduce.place_of(1, i) * unit, unit)
            parts.append(
                pltpu.make_async_copy(
                    e_ref.at[:, :, pl.ds(start, unit)],
                    ebuf_ref.at[buf, :, :, pl.ds(j * unit, unit)],
                    load_sem.at[buf, 1 + j],
                )
            )
        return parts

    def start(parts):
        for one in parts:
            one.start()

    def wait(parts):
        for one in parts:
            one.wait()

    tail = pl.ds(tokens, rbuf_ref.shape[3])
    more = [
        pltpu.make_async_copy(g_ref.at[:, :, tail], rbuf_ref.at[0], load_sem.at[2, 0]),
        pltpu.make_async_copy(e_ref.at[:, :, tail], rbuf_ref.at[1], load_sem.at[2, 1]),
    ]
    late = [
        pltpu.make_async_copy(kw_ref, w_ref.at[0], load_sem.at[2, 2]),
        pltpu.make_async_copy(vw_ref, w_ref.at[1], load_sem.at[2, 3]),
        pltpu.make_async_copy(hw_ref, h_ref, load_sem.at[2, 4]),
    ]
    for i in range(2):
        start(loads(i))

    def first(k):
        q = (x * 2 + tp + k) % 8
        return {"ctx": ((q // 2) * SIDE + z) * 2 + core, "tp": q % 2}

    def second(k):
        q = (z * 2 + core + k) % 8
        return {"ctx": x * SIDE * 2 + q}

    other_dp = {"dp": 1 - dp}
    greet([first(k) for k in range(1, 8)] + [second(k) for k in range(1, 8)] + [other_dp])
    score_copies = Copies(score_send, score_recv)
    pick = response_pick(lengths_ref, map_ref, rows, ref_ref.shape[1])
    part = jnp.sum(pick * token_ref[...], axis=0, keepdims=True)
    one_ref[x * 2 + tp] = jnp.broadcast_to(part, one_ref.shape[1:])
    half_sum = share_scores(one_ref, x * 2 + tp, first, score_copies, 0)
    two_ref[z * 2 + core] = half_sum
    scores = share_scores(two_ref, z * 2 + core, second, score_copies, 7)[:1]
    pairs = scores.shape[1] // 2
    shifted = scores - ref_ref[...]
    margin = DPO_BETA * (shifted[:, :pairs] - shifted[:, pairs:])
    small = jnp.exp(-jnp.abs(margin))
    pair_grad = -DPO_BETA * jnp.where(margin >= 0.0, small, 1.0) / (1.0 + small)
    score_grad = jnp.concatenate([pair_grad, -pair_grad], axis=1)
    row_grad = jnp.sum(pick * score_grad, axis=1, keepdims=True)
    row_factor = jnp.concatenate([row_grad] * grouped, axis=0)
    start(more)
    for h in range(kv_heads):
        factor = inv_ref[h] * row_factor
        base = h * grouped * 128
        pieces = [q_ref[:, base + i * 128 : base + (i + 1) * 128] for i in range(grouped)]
        q = jnp.concatenate(pieces, axis=0).astype(F32)
        qs_ref[h] = (q * (factor * scale)).astype(BF16)
        pieces = [t_ref[:, base + i * 128 : base + (i + 1) * 128] for i in range(grouped)]
        t = jnp.concatenate(pieces, axis=0).astype(F32)
        ts_ref[h] = (t * factor).astype(BF16)

    def chunk_grads(i):
        buf = i % 2
        for kv, (kept, scaled) in enumerate(((gbuf_ref, qs_ref), (ebuf_ref, ts_ref))):
            for h in range(kv_heads):
                grads = lax.dot_general(kept[buf, h], scaled[h], TN, preferred_element_type=F32)
                grads = grads.astype(BF16).reshape(SIDE, 2, unit // 2, 128)
                d_ref[kv, i, :, :, :, h * 128 : (h + 1) * 128] = grads
            reduce.to_core(kv, i)

    for i in range(SIDE):
        wait(loads(i))
        chunk_grads(i)
        if i + 2 < SIDE:
            start(loads(i + 2))
        if i == SIDE - 2:
            start(late)
        if i >= 1:
            for kv in range(2):
                reduce.start_inner(kv, i - 1)
        if i >= 2:
            for kv in range(2):
                reduce.passing(kv, i - 2)
        if i >= 3:
            for kv in range(2):
                reduce.end_inner(kv, i - 3)
    for kv in range(2):
        reduce.start_inner(kv, 3)
    for kv in range(2):
        reduce.passing(kv, 2)
    for kv in range(2):
        reduce.end_inner(kv, 1)
    for kv in range(2):
        reduce.passing(kv, 3)
    wait(more)
    for kv, scaled in enumerate((qs_ref, ts_ref)):
        for h in range(kv_heads):
            grads = lax.dot_general(rbuf_ref[kv, h], scaled[h], TN, preferred_element_type=F32)
            resp_ref[kv, :, h * 128 : (h + 1) * 128] = grads[:rows].astype(BF16)
    loss = jnp.maximum(-margin, 0.0) + jnp.log1p(small)
    loss_ref[...] = jnp.sum(loss, axis=1, keepdims=True)
    qgrad_ref[...] = (dq_ref[...].astype(F32) * row_grad).astype(BF16)
    for kv in range(2):
        reduce.end_inner(kv, 2)
    for kv in range(2):
        reduce.passing(kv, None)
    for kv in range(2):
        reduce.end_inner(kv, 3)
    key_sum = reduce.result(0, None)
    gk_ref[0, x, z, core] = norm_backward(raw_ref[...], gain_ref[...], key_sum).astype(BF16)
    gv_ref[0, x, z, core] = reduce.result(1, None).astype(BF16)

    gather_copies = Copies(gather_send, gather_recv)
    stages = gather_stages(
        lambda kv: (gk_ref, gv_ref)[kv], raw_ref.shape[0], gather_copies, 0
    )
    last_copies = Copies(last_send, last_recv)
    stages[0]()
    wait(late)
    tile = 512
    half = paway_ref.shape[1]

    def input_grad(side, store):
        key_grad, value_grad = gk_ref[0, x, z, core], gv_ref[0, x, z, core]

        def step(i, carry):
            here = pl.ds(pl.multiple_of(side * half + i * tile, tile), tile)
            value = lax.dot_general(key_grad, w_ref[0, here], NT, preferred_element_type=F32)
            value += lax.dot_general(value_grad, w_ref[1, here], NT, preferred_element_type=F32)
            store(pl.ds(pl.multiple_of(i * tile, tile), tile), value)
            return carry

        lax.fori_loop(0, half // tile, step, 0)

    def store_away(here, value):
        paway_ref[:, here] = value.astype(BF16)

    def store_own(here, value):
        pown_ref[:, here] = value

    input_grad(1 - tp, store_away)
    last_copies.send(paway_ref, pcame_ref, {"tp": 1 - tp}, 0)
    stages[1]()
    stages[2]()
    input_grad(tp, store_own)
    stages[3]()
    stages[4]()
    last_copies.arrived(pcame_ref, 0)
    pgrad_ref[...] = (pown_ref[...] + pcame_ref[...].astype(F32)).astype(BF16)

    out_rows = wgrad_ref.shape[0]
    shift = (ctx % 4) * 32
    hidden = h_ref[...].reshape(-1, h_ref.shape[2])
    stages[5]()
    for kv, ref in enumerate((gk_ref, gv_ref)):
        grads = ref[...].reshape(-1, ref.shape[5])
        wpart_ref[kv] = lax.dot_general(hidden, grads, TN, preferred_element_type=F32)
        away = pl.ds(pl.multiple_of(shift + (1 - dp) * out_rows, 16), out_rows)
        waway_ref[kv] = wpart_ref[kv, away].astype(BF16)
        last_copies.send(waway_ref.at[kv], wcame_ref.at[kv], other_dp, 1 + kv)
    for copies in (score_copies, reduce_copies, gather_copies):
        copies.finish()
    own = pl.ds(pl.multiple_of(shift + dp * out_rows, 16), out_rows)
    for kv in range(2):
        last_copies.arrived(wcame_ref.at[kv], 1 + kv)
        wgrad_ref[:, kv] = wpart_ref[kv, own] + wcame_ref[kv].astype(F32)
    last_copies.finish()


def backward(
    token_part,
    lengths,
    places,
    ref_scores,
    q,
    t,
    inv,
    dq,
    raw_keys,
    gain,
    e,
    g,
    kw,
    vw,
    windows,
    scale,
    out_rows,
):
    rows, responses = q.shape[0], ref_scores.shape[1]
    kv_heads, total, width = e.shape
    prompt_rows, kv_width = raw_keys.shape
    depth = kw.shape[0]
    n = windows.shape[0]
    tokens = n * prompt_rows
    pad = width - tokens
    chunk = tokens // SIDE
    half = depth // 2
    vmem, anywhere = pl.BlockSpec(memory_space=pltpu.VMEM), pl.BlockSpec(memory_space=pl.ANY)
    smem = pl.BlockSpec(memory_space=pltpu.SMEM)
    dma = pltpu.SemaphoreType.DMA
    small = (prompt_rows // 2, kv_width)
    return pl.pallas_call(
        functools.partial(backward_kernel, scale),
        out_shape=[
            jax.ShapeDtypeStruct((1, 1), F32),
            jax.ShapeDtypeStruct(q.shape, BF16),
            jax.ShapeDtypeStruct((2, rows, kv_width), BF16),
            jax.ShapeDtypeStruct((prompt_rows, half), BF16),
            jax.ShapeDtypeStruct((out_rows, 2, kv_width), F32),
        ],
        in_specs=[vmem, smem, smem] + [vmem] * 7 + [anywhere] * 5,
        out_specs=[vmem] * 5,
        scratch_shapes=[
            pltpu.VMEM((8, 8, responses), F32),
            pltpu.VMEM((8, 8, responses), F32),
            pltpu.VMEM((kv_heads, total, 128), BF16),
            pltpu.VMEM((kv_heads, total, 128), BF16),
            pltpu.VMEM((2, kv_heads, total, chunk), BF16),
            pltpu.VMEM((2, kv_heads, total, chunk), BF16),
            pltpu.VMEM((2, kv_heads, total, pad), BF16),
            pltpu.VMEM((2, SIDE, SIDE, 2, prompt_rows, kv_width), BF16),
            pltpu.VMEM((2, SIDE, SIDE, prompt_rows, kv_width), BF16),
            pltpu.VMEM((2, SIDE, SIDE, prompt_rows, kv_width), BF16),
            pltpu.VMEM((2, SIDE, 6) + small, BF16),
            pltpu.VMEM((2, SIDE, prompt_rows, kv_width), BF16),
            pltpu.VMEM((2, 6) + small, BF16),
            pltpu.VMEM((1, SIDE, SIDE, 2, prompt_rows, kv_width), BF16),
            pltpu.VMEM((1, SIDE, SIDE, 2, prompt_rows, kv_width), BF16),
            pltpu.VMEM((2, depth, kv_width), BF16),
            pltpu.VMEM(windows.shape, BF16),
            pltpu.VMEM((prompt_rows, half), BF16),
            pltpu.VMEM((prompt_rows, half), BF16),
            pltpu.VMEM((prompt_rows, half), F32),
            pltpu.VMEM((2, WINDOW, kv_width), F32),
            pltpu.VMEM((2, out_rows, kv_width), BF16),
            pltpu.VMEM((2, out_rows, kv_width), BF16),
            dma((3, 5)),
            dma((14,)),
            dma((14,)),
            dma((REDUCE_COPIES,)),
            dma((REDUCE_COPIES,)),
            dma((GATHER_COPIES,)),
            dma((GATHER_COPIES,)),
            dma((3,)),
            dma((3,)),
        ],
        compiler_params=params(60, collective_id=1, has_side_effects=True),
        name="backward",
    )(
        token_part,
        lengths,
        places,
        ref_scores,
        q,
        t,
        inv,
        dq,
        raw_keys,
        gain,
        e,
        g,
        kw,
        vw,
        windows,
    )


def finish_kernel(*refs):
    count = len(refs) // 2
    copies = [
        pltpu.make_async_copy(refs[i], refs[count + i], refs[-1].at[i]) for i in range(count)
    ]
    for one in copies:
        one.start()
    for one in copies:
        one.wait()


def finish(*arrays):
    anywhere = pl.BlockSpec(memory_space=pl.ANY)
    return pl.pallas_call(
        finish_kernel,
        out_shape=[jax.ShapeDtypeStruct(a.shape, a.dtype) for a in arrays],
        in_specs=[anywhere] * len(arrays),
        out_specs=[anywhere] * len(arrays),
        scratch_shapes=[pltpu.SemaphoreType.DMA((len(arrays),))],
        compiler_params=params(61),
        name="finish",
    )(*arrays)


def shards(
    prompt_hidden,
    key_weight,
    value_weight,
    key_gain,
    queries,
    response_kv,
    targets,
    ref_scores,
    lengths,
    placement_map,
):
    hidden = prompt_hidden[0]
    model_width = hidden.shape[1]
    head_width = key_gain.shape[0]
    kv_width = key_weight.shape[1]
    grouped = queries.shape[2] // kv_width
    n_ctx = lax.axis_size("ctx")
    qk_scale = 1.0 / math.sqrt(head_width)
    gain = key_gain[None]
    q, t = queries[0], targets[0]
    raw_keys, e, g, inv, dq, token_part, windows = forward(
        hidden,
        key_weight,
        value_weight,
        gain,
        q,
        t,
        response_kv[0].transpose(1, 0, 2),
        lengths[0, 0],
        n_ctx,
        qk_scale,
        grouped,
        4,
    )

    def joined(value):
        return value.reshape(value.shape[0], -1, value.shape[3])

    dpo_loss, query_grad, resp_grad, prompt_grad, weight_grad = backward(
        token_part,
        lengths[0, 0],
        placement_map[0],
        ref_scores,
        q,
        t,
        joined(inv),
        dq,
        raw_keys,
        gain,
        joined(e),
        joined(g),
        key_weight,
        value_weight,
        windows,
        qk_scale,
        model_width // n_ctx // 2,
    )
    query_grad, prompt_grad, weight_grad = finish(query_grad, prompt_grad, weight_grad)
    return (
        dpo_loss.reshape(1),
        query_grad[None],
        resp_grad.transpose(1, 0, 2)[None],
        prompt_grad[None],
        weight_grad,
    )


def solution(mesh):
    in_specs = (
        P("dp", "ctx", None),
        P(None, "tp"),
        P(None, "tp"),
        P(),
        P("dp", "ctx", "tp"),
        P("dp", "ctx", None, "tp"),
        P("dp", "ctx", "tp"),
        P("dp", None),
        P("dp", "ctx", None),
        P("dp", "ctx"),
    )
    out_specs = (
        P("dp"),
        P("dp", "ctx", "tp"),
        P("dp", "ctx", None, "tp"),
        P("dp", "ctx", "tp"),
        P(("ctx", "dp"), None, "tp"),
    )
    return jax.shard_map(shards, mesh=mesh, in_specs=in_specs, out_specs=out_specs, check_vma=False)
```

```python
import functools
import math

import jax
import jax.numpy as jnp
from jax import lax
from jax.experimental import pallas as pl
from jax.experimental.pallas import tpu as pltpu
from jax.sharding import PartitionSpec as P

NORM_EPS = 1e-06
DPO_BETA = 0.5
MASK_FILL = -1e30
LOG2E = 1.4426950408889634
NT = (((1,), (1,)), ((), ()))
TN = (((0,), (0,)), ((), ()))
F32 = jnp.float32
BF16 = jnp.bfloat16


MESH = pl.DeviceIdType.MESH
SIDE = 4


def params(limit_mib, **more):
    return pltpu.CompilerParams(vmem_limit_bytes=limit_mib * 1024 * 1024, **more)


def place():
    me = lax.axis_index("ctx")
    return me // (2 * SIDE), (me // 2) % SIDE, me % 2


def ctx_id(x, z, core):
    return {"ctx": (x * SIDE + z) * 2 + core}


def greet(peers):
    barrier = pltpu.get_barrier_semaphore()
    for peer in peers:
        pl.semaphore_signal(barrier, inc=1, device_id=peer, device_id_type=MESH)
    pl.semaphore_wait(barrier, len(peers))


def plane_peers():
    x, z, core = place()
    return [
        ctx_id((x + 1) % SIDE, z, core),
        ctx_id((x + SIDE - 1) % SIDE, z, core),
        ctx_id(x, (z + 1) % SIDE, core),
        ctx_id(x, (z + SIDE - 1) % SIDE, core),
        ctx_id(x, z, 1 - core),
    ]


def ring(axis):
    x, z, core = place()
    if axis == 0:
        return x, lambda p: ctx_id(p, z, core)
    return z, lambda p: ctx_id(x, p, core)


def around(p):
    return (p + 1) % SIDE, (p + SIDE - 1) % SIDE, (p + 2) % SIDE


class Copies:
    def __init__(self, send_sem, recv_sem):
        self.send_sem, self.recv_sem, self.started = send_sem, recv_sem, []

    def make(self, src, dst, peer, slot):
        return pltpu.make_async_remote_copy(
            src_ref=src,
            dst_ref=dst,
            send_sem=self.send_sem.at[slot],
            recv_sem=self.recv_sem.at[slot],
            device_id=peer,
            device_id_type=MESH,
        )

    def send(self, src, dst, peer, slot):
        one = self.make(src, dst, peer, slot)
        one.start()
        self.started.append(one)

    def arrived(self, dst, slot):
        x, z, core = place()
        self.make(dst, dst, ctx_id(x, z, 1 - core), slot).wait_recv()

    def finish(self):
        for one in self.started:
            one.wait_send()


GATHER_COPIES = 72


def gather_stages(refs, copies):
    x, z, core = place()
    partner = ctx_id(x, z, 1 - core)
    rows = refs[0].shape[3]
    full, low, high = pl.ds(0, rows), pl.ds(0, rows // 2), pl.ds(rows // 2, rows // 2)
    rings = {}
    for kv in range(2):
        for level in range(2):
            p, at = ring(kv if level == 0 else 1 - kv)
            right, left, opposite = around(p)
            rings[kv, level] = ((p, left, right, opposite), at(right), at(left))

    def block(kv, i, j, part=full, of_core=None):
        of_core = core if of_core is None else of_core
        i, j = rings[kv, 0][0][i], rings[kv, 1][0][j]
        spot = (i, j) if kv == 0 else (j, i)
        return refs[kv].at[spot[0], spot[1], of_core, part]

    def first(kv, k):
        return kv * 36 + k

    def second(kv, i, k):
        return kv * 36 + 4 + i * 4 + k

    def swap_slot(kv, i, j):
        return kv * 36 + 20 + i * 4 + j

    def send(ref, peer, slot):
        copies.send(ref, ref, peer, slot)

    def to_core(kv, i, j):
        send(block(kv, i, j), partner, swap_slot(kv, i, j))

    def onward(kv, i):
        _, right, left = rings[kv, 1]
        send(block(kv, i, 0), right, second(kv, i, 0))
        send(block(kv, i, 0), left, second(kv, i, 1))
        to_core(kv, i, 0)

    def open_all():
        for kv in range(2):
            _, right, left = rings[kv, 0]
            send(block(kv, 0, 0), right, first(kv, 0))
            send(block(kv, 0, 0), left, first(kv, 1))
        for kv in range(2):
            onward(kv, 0)

    def first_neighbours():
        for kv in range(2):
            _, right, left = rings[kv, 0]
            copies.arrived(block(kv, 1, 0), first(kv, 0))
            send(block(kv, 1, 0, low), right, first(kv, 2))
            onward(kv, 1)
            copies.arrived(block(kv, 2, 0), first(kv, 1))
            send(block(kv, 2, 0, high), left, first(kv, 3))
            onward(kv, 2)

    def first_opposite():
        for kv in range(2):
            copies.arrived(block(kv, 3, 0, low), first(kv, 2))
            copies.arrived(block(kv, 3, 0, high), first(kv, 3))
            onward(kv, 3)

    def second_neighbours(i):
        for kv in range(2):
            _, right, left = rings[kv, 1]
            copies.arrived(block(kv, i, 1), second(kv, i, 0))
            send(block(kv, i, 1, low), right, second(kv, i, 2))
            to_core(kv, i, 1)
            copies.arrived(block(kv, i, 2), second(kv, i, 1))
            send(block(kv, i, 2, high), left, second(kv, i, 3))
            to_core(kv, i, 2)

    def second_opposite(i):
        for kv in range(2):
            copies.arrived(block(kv, i, 3, low), second(kv, i, 2))
            copies.arrived(block(kv, i, 3, high), second(kv, i, 3))
            to_core(kv, i, 3)

    def from_core(kv):
        for i in range(4):
            for j in range(4):
                copies.arrived(block(kv, i, j, full, 1 - core), swap_slot(kv, i, j))

    return [
        open_all,
        first_neighbours,
        lambda: second_neighbours(0),
        first_opposite,
        lambda: second_neighbours(1),
        lambda: second_opposite(0),
        lambda: second_neighbours(2),
        lambda: second_opposite(1),
        lambda: second_neighbours(3),
        lambda: second_opposite(2),
        lambda: second_opposite(3),
        lambda: from_core(0),
        lambda: from_core(1),
    ]


def project_kernel(
    h_ref,
    kw_ref,
    vw_ref,
    gain_ref,
    raw_ref,
    gk_ref,
    gv_ref,
    w_ref,
    load_sem,
    send_sem,
    recv_sem,
):
    x, z, core = place()
    steps, tile, width = w_ref.shape[1:]

    def load(kv, i):
        src = (kw_ref, vw_ref)[kv].at[pl.ds(i * tile, tile)]
        return pltpu.make_async_copy(src, w_ref.at[kv, i], load_sem.at[kv, i])

    for i in range(steps):
        for kv in range(2):
            load(kv, i).start()
    greet(plane_peers())
    sums = [jnp.zeros((h_ref.shape[0], width), F32)] * 2
    for i in range(steps):
        part = h_ref[:, i * tile : (i + 1) * tile]
        for kv in range(2):
            load(kv, i).wait()
            sums[kv] = sums[kv] + jnp.dot(part, w_ref[kv, i], preferred_element_type=F32)
    raw_ref[...] = sums[0]
    gv_ref[x, z, core] = sums[1].astype(BF16)
    parts = []
    for i in range(width // 128):
        keys = sums[0][:, i * 128 : (i + 1) * 128]
        inv = lax.rsqrt(jnp.mean(keys * keys, axis=1, keepdims=True) + NORM_EPS)
        parts.append((keys * inv * gain_ref[...]).astype(BF16))
    gk_ref[x, z, core] = jnp.concatenate(parts, axis=1)
    copies = Copies(send_sem, recv_sem)
    for stage in gather_stages((gk_ref, gv_ref), copies):
        stage()
    copies.finish()


def project_and_gather(hidden, key_weight, value_weight, gain):
    rows, depth = hidden.shape
    width = key_weight.shape[1]
    tile = 1024
    steps = depth // tile
    vmem, anywhere = pl.BlockSpec(memory_space=pltpu.VMEM), pl.BlockSpec(memory_space=pl.ANY)
    plane = jax.ShapeDtypeStruct((SIDE, SIDE, 2, rows, width), BF16)
    raw, keys, values = pl.pallas_call(
        project_kernel,
        out_shape=[jax.ShapeDtypeStruct((rows, width), F32), plane, plane],
        in_specs=[vmem, anywhere, anywhere, vmem],
        out_specs=[vmem] * 3,
        scratch_shapes=[
            pltpu.VMEM((2, steps, tile, width), BF16),
            pltpu.SemaphoreType.DMA((2, steps)),
            pltpu.SemaphoreType.DMA((GATHER_COPIES,)),
            pltpu.SemaphoreType.DMA((GATHER_COPIES,)),
        ],
        compiler_params=params(60, collective_id=0, has_side_effects=True),
        name="project_and_gather",
    )(hidden, key_weight, value_weight, gain)
    total = SIDE * SIDE * 2 * rows
    return raw, keys.reshape(total, width), values.reshape(total, width)


def slots_of(lengths_ref, ids):
    slots, end = jnp.zeros(ids.shape, jnp.int32), 0
    for i in range(lengths_ref.shape[0]):
        end = end + lengths_ref[i]
        slots = slots + jnp.where(ids >= end, 1, 0)
    return slots


def slot_bias(lengths_ref, rows, pad):
    row = lax.broadcasted_iota(jnp.int32, (rows, pad), 0)
    key = lax.broadcasted_iota(jnp.int32, (rows, pad), 1)
    seen = (slots_of(lengths_ref, row) == slots_of(lengths_ref, key)) & (key <= row)
    return jnp.where(seen, 0.0, MASK_FILL)


def response_pick(lengths_ref, map_ref, rows, responses):
    slots = slots_of(lengths_ref, lax.broadcasted_iota(jnp.int32, (rows, responses), 0))
    ids = jnp.zeros((rows, responses), jnp.int32)
    for i in range(map_ref.shape[0]):
        ids = jnp.where(slots == i, map_ref[i], ids)
    return jnp.where(ids == lax.broadcasted_iota(jnp.int32, (rows, responses), 1), 1.0, 0.0)


def attend_kernel(
    scale,
    q_ref,
    t_ref,
    k_ref,
    v_ref,
    r_ref,
    lengths_ref,
    h_ref,
    e_ref,
    g_ref,
    inv_ref,
    dq_ref,
    tok_ref,
    o_ref,
    own_sem,
    send_sem,
    recv_sem,
):
    me = lax.axis_index("ctx")
    n = o_ref.shape[0]

    def window(peer):
        tile = 5 * (peer // 4) + peer % 4
        return h_ref.at[:, pl.ds(pl.multiple_of(tile * 128, 128), WINDOW)]

    def copy(k):
        peer = (me + k) % n
        return pltpu.make_async_remote_copy(
            src_ref=window(peer),
            dst_ref=o_ref.at[me],
            send_sem=send_sem.at[k - 1],
            recv_sem=recv_sem.at[k - 1],
            device_id={"ctx": peer},
            device_id_type=MESH,
        )

    own_copy = pltpu.make_async_copy(window(me), o_ref.at[me], own_sem)

    @pl.when((pl.program_id(0) == 0) & (pl.program_id(1) == 0))
    def _():
        barrier = pltpu.get_barrier_semaphore()

        def hello(k, carry):
            pl.semaphore_signal(
                barrier, inc=1, device_id={"ctx": (me + k) % n}, device_id_type=MESH
            )
            return carry

        def go(k, carry):
            copy(k).start()
            return carry

        lax.fori_loop(1, n, hello, 0)
        pl.semaphore_wait(barrier, n - 1)
        lax.fori_loop(1, n, go, 0)
        own_copy.start()
        tok_ref[...] = jnp.zeros_like(tok_ref)

    rows, heads = q_ref.shape[0], q_ref.shape[1] // 128
    tokens = k_ref.shape[0]
    pad = -rows % 128
    filler = jnp.zeros((pad, 128), BF16)
    k, v = k_ref[...], v_ref[...]
    rk = jnp.concatenate([r_ref[0], filler], axis=0)
    rv = jnp.concatenate([r_ref[1], filler], axis=0)
    bias = slot_bias(lengths_ref, rows, rows + pad)
    factor = scale * LOG2E
    parts = range(0, heads, 2)
    bias = jnp.concatenate([bias, bias], axis=0)

    def two(ref, i):
        return jnp.concatenate([ref[:, i * 128 : (i + 1) * 128], ref[:, (i + 1) * 128 : (i + 2) * 128]], axis=0)

    def out_rows(i):
        return slice(i * rows, (i + 2) * rows)

    def logits(i):
        q = two(q_ref, i)
        s = lax.dot_general(q, k, NT, preferred_element_type=F32)
        return s, lax.dot_general(q, rk, NT, preferred_element_type=F32) + bias

    def weigh(i, s, sr):
        peak = jnp.maximum(
            jnp.max(s, axis=1, keepdims=True), jnp.max(sr, axis=1, keepdims=True)
        )
        top = peak * factor
        e = jnp.exp2(s * factor - top)
        er = jnp.exp2(sr * factor - top)
        inv = 1.0 / (
            jnp.sum(e, axis=1, keepdims=True) + jnp.sum(er, axis=1, keepdims=True)
        )
        e_ref[0, out_rows(i), :tokens] = e.astype(BF16)
        e_ref[0, out_rows(i), tokens:] = er.astype(BF16)
        inv_ref[0, out_rows(i)] = inv
        return inv

    def read(i, inv):
        t = two(t_ref, i)
        e, er = e_ref[0, out_rows(i), :tokens], e_ref[0, out_rows(i), tokens:]
        dp = lax.dot_general(t, v, NT, preferred_element_type=F32)
        dpr = lax.dot_general(t, rv, NT, preferred_element_type=F32)
        attended = jnp.dot(e, v, preferred_element_type=F32)
        attended = (attended + jnp.dot(er, rv, preferred_element_type=F32)) * inv
        dot = jnp.sum(attended * t.astype(F32), axis=1, keepdims=True)
        return dp, dpr, dot

    def differ(i, dp, dpr, dot):
        e, er = e_ref[0, out_rows(i), :tokens], e_ref[0, out_rows(i), tokens:]
        g_ref[0, out_rows(i), :tokens] = (e.astype(F32) * (dp - dot)).astype(BF16)
        g_ref[0, out_rows(i), tokens:] = (er.astype(F32) * (dpr - dot)).astype(BF16)

    def query_grad(i, inv):
        g, gr = g_ref[0, out_rows(i), :tokens], g_ref[0, out_rows(i), tokens:]
        dq = jnp.dot(g, k, preferred_element_type=F32)
        dq = (dq + jnp.dot(gr, rk, preferred_element_type=F32)) * (inv * scale)
        dq_ref[:, i * 128 : (i + 1) * 128] = dq[:rows].astype(BF16)
        dq_ref[:, (i + 1) * 128 : (i + 2) * 128] = dq[rows:].astype(BF16)

    scores = {i: logits(i) for i in parts}
    invs, reads, total = {}, {}, jnp.zeros((rows, 1), F32)
    for i in parts:
        invs[i] = weigh(i, *scores[i])
        reads[i] = read(i, invs[i])
        if i >= 2:
            differ(i - 2, *reads[i - 2])
            query_grad(i - 2, invs[i - 2])
    last = heads - 2
    differ(last, *reads[last])
    query_grad(last, invs[last])
    for i in parts:
        dot = reads[i][2]
        total = total + dot[:rows] + dot[rows:]
    tok_ref[...] += total

    @pl.when(
        (pl.program_id(0) == pl.num_programs(0) - 1) & (pl.program_id(1) == pl.num_programs(1) - 1)
    )
    def _():
        def done(k, carry):
            copy(k).wait()
            return carry

        own_copy.wait()
        lax.fori_loop(1, n, done, 0)


WINDOW = 256


def attend(q, t, prompt_keys, prompt_values, resp, lengths, hidden, n, scale, grouped, chunk):
    rows = q.shape[0]
    tokens, kv_width = prompt_keys.shape
    kv_heads = kv_width // 128
    pad = rows + -rows % 128
    steps = grouped // chunk
    m = chunk * rows
    total = grouped * rows
    row_block = pl.BlockSpec((rows, chunk * 128), lambda h, c: (0, h * steps + c))
    head_block = pl.BlockSpec((tokens, 128), lambda h, c: (0, h))

    def score_block(width):
        return pl.BlockSpec((1, m, width), lambda h, c: (h, c, 0))

    return pl.pallas_call(
        functools.partial(attend_kernel, scale),
        grid=(kv_heads, steps),
        in_specs=[
            row_block,
            row_block,
            head_block,
            head_block,
            pl.BlockSpec((2, rows, 128), lambda h, c: (0, 0, h)),
            pl.BlockSpec(memory_space=pltpu.SMEM),
            pl.BlockSpec(memory_space=pl.ANY),
        ],
        out_specs=[
            score_block(tokens + pad),
            score_block(tokens + pad),
            score_block(1),
            row_block,
            pl.BlockSpec((rows, 1), lambda h, c: (0, 0)),
            pl.BlockSpec(memory_space=pl.ANY),
        ],
        out_shape=[
            jax.ShapeDtypeStruct((kv_heads, total, tokens + pad), BF16),
            jax.ShapeDtypeStruct((kv_heads, total, tokens + pad), BF16),
            jax.ShapeDtypeStruct((kv_heads, total, 1), F32),
            jax.ShapeDtypeStruct(q.shape, BF16),
            jax.ShapeDtypeStruct((rows, 1), F32),
            jax.ShapeDtypeStruct((n, hidden.shape[0], WINDOW), BF16),
        ],
        scratch_shapes=[
            pltpu.SemaphoreType.DMA,
            pltpu.SemaphoreType.DMA((n - 1,)),
            pltpu.SemaphoreType.DMA((n - 1,)),
        ],
        compiler_params=params(56, collective_id=3, has_side_effects=True),
        name="attend",
    )(q, t, prompt_keys, prompt_values, resp, lengths, hidden)


def norm_backward(raw, gain, grad):
    parts = []
    for h in range(raw.shape[1] // 128):
        keys = raw[:, h * 128 : (h + 1) * 128]
        kg = gain * grad[:, h * 128 : (h + 1) * 128]
        inv = lax.rsqrt(jnp.mean(keys * keys, axis=1, keepdims=True) + NORM_EPS)
        mix = jnp.mean(keys * kg, axis=1, keepdims=True)
        parts.append(inv * kg - keys * (inv * inv * inv) * mix)
    return jnp.concatenate(parts, axis=1)


def total_of(*refs):
    value = refs[0][...].astype(F32)
    for ref in refs[1:]:
        value = value + ref[...].astype(F32)
    return value


REDUCE_COPIES = 68


class Reduce:
    def __init__(self, d_ref, c_ref, a_ref, b_ref, r_ref, s_ref, copies):
        self.d, self.c, self.a, self.b, self.r, self.s = d_ref, c_ref, a_ref, b_ref, r_ref, s_ref
        self.copies = copies
        x, z, self.core = place()
        self.partner = ctx_id(x, z, 1 - self.core)
        rows = a_ref.shape[3]
        self.low, self.high = pl.ds(0, rows // 2), pl.ds(rows // 2, rows // 2)
        self.rings = {}
        for kv in range(2):
            for inner in range(2):
                p, at = ring(1 - kv if inner else kv)
                right, left, opposite = around(p)
                self.rings[kv, inner] = ((opposite, right, left, p), at(right), at(left))

    def place_of(self, kv, i):
        return self.rings[kv, 0][0][i]

    def to_core(self, kv, i):
        self.copies.send(
            self.d.at[kv, i, :, 1 - self.core], self.c.at[kv, i], self.partner, kv * 4 + i
        )

    def landing(self, kv, i, k):
        return self.s.at[kv, k] if i is None else self.b.at[kv, i, k]

    def slot(self, kv, i, k):
        return 56 + kv * 6 + k if i is None else 8 + (kv * 4 + i) * 6 + k

    def unit(self, kv, i, j, part):
        if i is None:
            return self.r.at[kv, j, part]
        return self.a.at[kv, i, self.rings[kv, 1][0][j], part]

    def message(self, kv, i, k, ref):
        _, right, left = self.rings[kv, 0 if i is None else 1]
        peer = right if k in (0, 2, 4) else left
        self.copies.send(ref, self.landing(kv, i, k), peer, self.slot(kv, i, k))

    def landed(self, kv, i, k):
        ref = self.landing(kv, i, k)
        self.copies.arrived(ref, self.slot(kv, i, k))
        return ref

    def opening(self, kv, i, j):
        if j == 0:
            self.message(kv, i, 0, self.unit(kv, i, 0, self.low))
            self.message(kv, i, 1, self.unit(kv, i, 0, self.high))
        if j == 1:
            self.message(kv, i, 2, self.unit(kv, i, 1, self.high))
        if j == 2:
            self.message(kv, i, 3, self.unit(kv, i, 2, self.low))

    def passing(self, kv, i):
        for k, j, part in ((0, 1, self.low), (1, 2, self.high)):
            came = self.landed(kv, i, k)
            mine = self.unit(kv, i, j, part)
            mine[...] = total_of(mine, came).astype(BF16)
            self.message(kv, i, 4 + k, mine)

    def result(self, kv, i):
        lows = total_of(
            self.unit(kv, i, 3, self.low), self.landed(kv, i, 3), self.landed(kv, i, 4)
        )
        highs = total_of(
            self.unit(kv, i, 3, self.high), self.landed(kv, i, 2), self.landed(kv, i, 5)
        )
        return jnp.concatenate([lows, highs], axis=0)

    def start_inner(self, kv, i):
        self.copies.arrived(self.c.at[kv, i], kv * 4 + i)
        self.a[kv, i] = total_of(self.d.at[kv, i, :, self.core], self.c.at[kv, i]).astype(BF16)
        for j in range(3):
            self.opening(kv, i, j)

    def end_inner(self, kv, i):
        self.r[kv, i] = self.result(kv, i).astype(BF16)
        self.opening(kv, None, i)


def share_scores(buf, me, peer, copies, base):
    sent = []
    for k in range(1, 8):
        copies.send(buf.at[me], buf.at[me], peer(k), base + k - 1)
    for k in range(1, 8):
        copies.arrived(buf.at[(me - k + 8) % 8], base + k - 1)
    value = buf[0]
    for i in range(1, 8):
        value = value + buf[i]
    return value


def backward_kernel(
    scale,
    token_ref,
    lengths_ref,
    map_ref,
    ref_ref,
    q_ref,
    t_ref,
    inv_ref,
    dq_ref,
    raw_ref,
    gain_ref,
    e_ref,
    g_ref,
    kw_ref,
    vw_ref,
    hw_ref,
    loss_ref,
    qgrad_ref,
    resp_ref,
    pgrad_ref,
    wgrad_ref,
    one_ref,
    two_ref,
    qs_ref,
    ts_ref,
    gbuf_ref,
    ebuf_ref,
    rbuf_ref,
    d_ref,
    c_ref,
    a_ref,
    b_ref,
    r_ref,
    s_ref,
    gk_ref,
    gv_ref,
    w_ref,
    h_ref,
    paway_ref,
    pcame_ref,
    pown_ref,
    wpart_ref,
    waway_ref,
    wcame_ref,
    load_sem,
    score_send,
    score_recv,
    reduce_send,
    reduce_recv,
    gather_send,
    gather_recv,
    last_send,
    last_recv,
):
    x, z, core = place()
    ctx, tp, dp = lax.axis_index("ctx"), lax.axis_index("tp"), lax.axis_index("dp")
    kv_heads, total, _ = qs_ref.shape
    rows = q_ref.shape[0]
    grouped = total // rows
    tokens = e_ref.shape[2] - rbuf_ref.shape[3]
    chunk = gbuf_ref.shape[3]
    unit = chunk // SIDE

    reduce_copies = Copies(reduce_send, reduce_recv)
    reduce = Reduce(d_ref, c_ref, a_ref, b_ref, r_ref, s_ref, reduce_copies)

    def loads(i):
        buf = i % 2
        start = pl.multiple_of(reduce.place_of(0, i) * chunk, chunk)
        parts = [
            pltpu.make_async_copy(
                g_ref.at[:, :, pl.ds(start, chunk)], gbuf_ref.at[buf], load_sem.at[buf, 0]
            )
        ]
        for j in range(SIDE):
            start = pl.multiple_of(j * chunk + reduce.place_of(1, i) * unit, unit)
            parts.append(
                pltpu.make_async_copy(
                    e_ref.at[:, :, pl.ds(start, unit)],
                    ebuf_ref.at[buf, :, :, pl.ds(j * unit, unit)],
                    load_sem.at[buf, 1 + j],
                )
            )
        return parts

    def start(parts):
        for one in parts:
            one.start()

    def wait(parts):
        for one in parts:
            one.wait()

    tail = pl.ds(tokens, rbuf_ref.shape[3])
    more = [
        pltpu.make_async_copy(g_ref.at[:, :, tail], rbuf_ref.at[0], load_sem.at[2, 0]),
        pltpu.make_async_copy(e_ref.at[:, :, tail], rbuf_ref.at[1], load_sem.at[2, 1]),
    ]
    late = [
        pltpu.make_async_copy(kw_ref, w_ref.at[0], load_sem.at[2, 2]),
        pltpu.make_async_copy(vw_ref, w_ref.at[1], load_sem.at[2, 3]),
        pltpu.make_async_copy(hw_ref, h_ref, load_sem.at[2, 4]),
    ]
    for i in range(2):
        start(loads(i))

    def first(k):
        q = (x * 2 + tp + k) % 8
        return {"ctx": ((q // 2) * SIDE + z) * 2 + core, "tp": q % 2}

    def second(k):
        q = (z * 2 + core + k) % 8
        return {"ctx": x * SIDE * 2 + q}

    other_dp = {"dp": 1 - dp}
    greet([first(k) for k in range(1, 8)] + [second(k) for k in range(1, 8)] + [other_dp])
    score_copies = Copies(score_send, score_recv)
    pick = response_pick(lengths_ref, map_ref, rows, ref_ref.shape[1])
    part = jnp.sum(pick * token_ref[...], axis=0, keepdims=True)
    one_ref[x * 2 + tp] = jnp.broadcast_to(part, one_ref.shape[1:])
    half_sum = share_scores(one_ref, x * 2 + tp, first, score_copies, 0)
    two_ref[z * 2 + core] = half_sum
    scores = share_scores(two_ref, z * 2 + core, second, score_copies, 7)[:1]
    pairs = scores.shape[1] // 2
    shifted = scores - ref_ref[...]
    margin = DPO_BETA * (shifted[:, :pairs] - shifted[:, pairs:])
    small = jnp.exp(-jnp.abs(margin))
    pair_grad = -DPO_BETA * jnp.where(margin >= 0.0, small, 1.0) / (1.0 + small)
    score_grad = jnp.concatenate([pair_grad, -pair_grad], axis=1)
    row_grad = jnp.sum(pick * score_grad, axis=1, keepdims=True)
    row_factor = jnp.concatenate([row_grad] * grouped, axis=0)
    start(more)
    for h in range(kv_heads):
        factor = inv_ref[h] * row_factor
        base = h * grouped * 128
        pieces = [q_ref[:, base + i * 128 : base + (i + 1) * 128] for i in range(grouped)]
        q = jnp.concatenate(pieces, axis=0).astype(F32)
        qs_ref[h] = (q * (factor * scale)).astype(BF16)
        pieces = [t_ref[:, base + i * 128 : base + (i + 1) * 128] for i in range(grouped)]
        t = jnp.concatenate(pieces, axis=0).astype(F32)
        ts_ref[h] = (t * factor).astype(BF16)

    def chunk_grads(i):
        buf = i % 2
        for kv, (kept, scaled) in enumerate(((gbuf_ref, qs_ref), (ebuf_ref, ts_ref))):
            for h in range(kv_heads):
                grads = lax.dot_general(kept[buf, h], scaled[h], TN, preferred_element_type=F32)
                grads = grads.astype(BF16).reshape(SIDE, 2, unit // 2, 128)
                d_ref[kv, i, :, :, :, h * 128 : (h + 1) * 128] = grads
            reduce.to_core(kv, i)

    for i in range(SIDE):
        wait(loads(i))
        chunk_grads(i)
        if i + 2 < SIDE:
            start(loads(i + 2))
        if i == SIDE - 2:
            start(late)
        if i >= 1:
            for kv in range(2):
                reduce.start_inner(kv, i - 1)
        if i >= 2:
            for kv in range(2):
                reduce.passing(kv, i - 2)
        if i >= 3:
            for kv in range(2):
                reduce.end_inner(kv, i - 3)
    for kv in range(2):
        reduce.start_inner(kv, 3)
    for kv in range(2):
        reduce.passing(kv, 2)
    for kv in range(2):
        reduce.end_inner(kv, 1)
    for kv in range(2):
        reduce.passing(kv, 3)
    wait(more)
    for kv, scaled in enumerate((qs_ref, ts_ref)):
        for h in range(kv_heads):
            grads = lax.dot_general(rbuf_ref[kv, h], scaled[h], TN, preferred_element_type=F32)
            resp_ref[kv, :, h * 128 : (h + 1) * 128] = grads[:rows].astype(BF16)
    qgrad_ref[...] = (dq_ref[...].astype(F32) * row_grad).astype(BF16)
    loss = jnp.maximum(-margin, 0.0) + jnp.log1p(small)
    loss_ref[...] = jnp.sum(loss, axis=1, keepdims=True)
    for kv in range(2):
        reduce.end_inner(kv, 2)
    for kv in range(2):
        reduce.passing(kv, None)
    for kv in range(2):
        reduce.end_inner(kv, 3)
    key_sum = reduce.result(0, None)
    gk_ref[x, z, core] = norm_backward(raw_ref[...], gain_ref[...], key_sum).astype(BF16)
    gv_ref[x, z, core] = reduce.result(1, None).astype(BF16)

    gather_copies = Copies(gather_send, gather_recv)
    stages = gather_stages((gk_ref, gv_ref), gather_copies)
    last_copies = Copies(last_send, last_recv)
    stages[0]()
    wait(late)
    tile = 512
    half = paway_ref.shape[1]

    def input_grad(side, store):
        key_grad, value_grad = gk_ref[x, z, core], gv_ref[x, z, core]

        def step(i, carry):
            here = pl.ds(pl.multiple_of(side * half + i * tile, tile), tile)
            value = lax.dot_general(key_grad, w_ref[0, here], NT, preferred_element_type=F32)
            value += lax.dot_general(value_grad, w_ref[1, here], NT, preferred_element_type=F32)
            store(pl.ds(pl.multiple_of(i * tile, tile), tile), value)
            return carry

        lax.fori_loop(0, half // tile, step, 0)

    def store_away(here, value):
        paway_ref[:, here] = value.astype(BF16)

    def store_own(here, value):
        pown_ref[:, here] = value

    input_grad(1 - tp, store_away)
    last_copies.send(paway_ref, pcame_ref, {"tp": 1 - tp}, 0)
    for stage in stages[1:5]:
        stage()
    input_grad(tp, store_own)
    for stage in stages[5:-2]:
        stage()
    last_copies.arrived(pcame_ref, 0)
    pgrad_ref[...] = (pown_ref[...] + pcame_ref[...].astype(F32)).astype(BF16)

    out_rows = wgrad_ref.shape[0]
    shift = (ctx % 4) * 32
    hidden = h_ref[...].reshape(-1, h_ref.shape[2])
    for kv, ref in enumerate((gk_ref, gv_ref)):
        stages[-2 + kv]()
        grads = ref[...].reshape(-1, ref.shape[4])
        wpart_ref[kv] = lax.dot_general(hidden, grads, TN, preferred_element_type=F32)
        away = pl.ds(pl.multiple_of(shift + (1 - dp) * out_rows, 16), out_rows)
        waway_ref[kv] = wpart_ref[kv, away].astype(BF16)
        last_copies.send(waway_ref.at[kv], wcame_ref.at[kv], other_dp, 1 + kv)
    for copies in (score_copies, reduce_copies, gather_copies):
        copies.finish()
    own = pl.ds(pl.multiple_of(shift + dp * out_rows, 16), out_rows)
    for kv in range(2):
        last_copies.arrived(wcame_ref.at[kv], 1 + kv)
        wgrad_ref[:, kv] = wpart_ref[kv, own] + wcame_ref[kv].astype(F32)
    last_copies.finish()


def backward(
    token_part,
    lengths,
    places,
    ref_scores,
    q,
    t,
    inv,
    dq,
    raw_keys,
    gain,
    e,
    g,
    kw,
    vw,
    windows,
    scale,
    out_rows,
):
    rows, responses = q.shape[0], ref_scores.shape[1]
    kv_heads, total, width = e.shape
    prompt_rows, kv_width = raw_keys.shape
    depth = kw.shape[0]
    n = windows.shape[0]
    tokens = n * prompt_rows
    pad = width - tokens
    chunk = tokens // SIDE
    half = depth // 2
    vmem, anywhere = pl.BlockSpec(memory_space=pltpu.VMEM), pl.BlockSpec(memory_space=pl.ANY)
    smem = pl.BlockSpec(memory_space=pltpu.SMEM)
    dma = pltpu.SemaphoreType.DMA
    small = (prompt_rows // 2, kv_width)
    return pl.pallas_call(
        functools.partial(backward_kernel, scale),
        out_shape=[
            jax.ShapeDtypeStruct((1, 1), F32),
            jax.ShapeDtypeStruct(q.shape, BF16),
            jax.ShapeDtypeStruct((2, rows, kv_width), BF16),
            jax.ShapeDtypeStruct((prompt_rows, half), BF16),
            jax.ShapeDtypeStruct((out_rows, 2, kv_width), F32),
        ],
        in_specs=[vmem, smem, smem] + [vmem] * 7 + [anywhere] * 5,
        out_specs=[vmem] * 5,
        scratch_shapes=[
            pltpu.VMEM((8, 8, responses), F32),
            pltpu.VMEM((8, 8, responses), F32),
            pltpu.VMEM((kv_heads, total, 128), BF16),
            pltpu.VMEM((kv_heads, total, 128), BF16),
            pltpu.VMEM((2, kv_heads, total, chunk), BF16),
            pltpu.VMEM((2, kv_heads, total, chunk), BF16),
            pltpu.VMEM((2, kv_heads, total, pad), BF16),
            pltpu.VMEM((2, SIDE, SIDE, 2, prompt_rows, kv_width), BF16),
            pltpu.VMEM((2, SIDE, SIDE, prompt_rows, kv_width), BF16),
            pltpu.VMEM((2, SIDE, SIDE, prompt_rows, kv_width), BF16),
            pltpu.VMEM((2, SIDE, 6) + small, BF16),
            pltpu.VMEM((2, SIDE, prompt_rows, kv_width), BF16),
            pltpu.VMEM((2, 6) + small, BF16),
            pltpu.VMEM((SIDE, SIDE, 2, prompt_rows, kv_width), BF16),
            pltpu.VMEM((SIDE, SIDE, 2, prompt_rows, kv_width), BF16),
            pltpu.VMEM((2, depth, kv_width), BF16),
            pltpu.VMEM(windows.shape, BF16),
            pltpu.VMEM((prompt_rows, half), BF16),
            pltpu.VMEM((prompt_rows, half), BF16),
            pltpu.VMEM((prompt_rows, half), F32),
            pltpu.VMEM((2, WINDOW, kv_width), F32),
            pltpu.VMEM((2, out_rows, kv_width), BF16),
            pltpu.VMEM((2, out_rows, kv_width), BF16),
            dma((3, 5)),
            dma((14,)),
            dma((14,)),
            dma((REDUCE_COPIES,)),
            dma((REDUCE_COPIES,)),
            dma((GATHER_COPIES,)),
            dma((GATHER_COPIES,)),
            dma((3,)),
            dma((3,)),
        ],
        compiler_params=params(60, collective_id=1, has_side_effects=True),
        name="backward",
    )(
        token_part,
        lengths,
        places,
        ref_scores,
        q,
        t,
        inv,
        dq,
        raw_keys,
        gain,
        e,
        g,
        kw,
        vw,
        windows,
    )


def finish_kernel(*refs):
    count = len(refs) // 2
    for i in range(count):
        refs[count + i][...] = refs[i][...]


def finish(*arrays):
    vmem = pl.BlockSpec(memory_space=pltpu.VMEM)
    return pl.pallas_call(
        finish_kernel,
        out_shape=[jax.ShapeDtypeStruct(a.shape, a.dtype) for a in arrays],
        in_specs=[vmem] * len(arrays),
        out_specs=[vmem] * len(arrays),
        compiler_params=params(60),
        name="finish",
    )(*arrays)


def shards(
    prompt_hidden,
    key_weight,
    value_weight,
    key_gain,
    queries,
    response_kv,
    targets,
    ref_scores,
    lengths,
    placement_map,
):
    hidden = prompt_hidden[0]
    prompt_rows, model_width = hidden.shape
    head_width = key_gain.shape[0]
    kv_width = key_weight.shape[1]
    kv_heads = kv_width // head_width
    query_heads = queries.shape[2] // head_width
    grouped = query_heads // kv_heads
    n_ctx = lax.axis_size("ctx")
    qk_scale = 1.0 / math.sqrt(head_width)
    gain = key_gain[None]

    raw_keys, prompt_keys, prompt_values = project_and_gather(
        hidden, key_weight, value_weight, gain
    )

    resp = response_kv[0].transpose(1, 0, 2)
    q, t = queries[0], targets[0]
    e, g, inv, dq, token_part, windows = attend(
        q,
        t,
        prompt_keys,
        prompt_values,
        resp,
        lengths[0, 0],
        hidden,
        n_ctx,
        qk_scale,
        grouped,
        4,
    )
    dpo_loss, query_grad, resp_grad, prompt_grad, weight_grad = backward(
        token_part,
        lengths[0, 0],
        placement_map[0],
        ref_scores,
        q,
        t,
        inv,
        dq,
        raw_keys,
        gain,
        e,
        g,
        key_weight,
        value_weight,
        windows,
        qk_scale,
        model_width // n_ctx // 2,
    )
    query_grad, prompt_grad, weight_grad = finish(query_grad, prompt_grad, weight_grad)
    return (
        dpo_loss.reshape(1),
        query_grad[None],
        resp_grad.transpose(1, 0, 2)[None],
        prompt_grad[None],
        weight_grad,
    )


def solution(mesh):
    in_specs = (
        P("dp", "ctx", None),
        P(None, "tp"),
        P(None, "tp"),
        P(),
        P("dp", "ctx", "tp"),
        P("dp", "ctx", None, "tp"),
        P("dp", "ctx", "tp"),
        P("dp", None),
        P("dp", "ctx", None),
        P("dp", "ctx"),
    )
    out_specs = (
        P("dp"),
        P("dp", "ctx", "tp"),
        P("dp", "ctx", None, "tp"),
        P("dp", "ctx", "tp"),
        P(("ctx", "dp"), None, "tp"),
    )
    return jax.shard_map(shards, mesh=mesh, in_specs=in_specs, out_specs=out_specs, check_vma=False)
```
